256 devices in a mesh: stream: 32 (over x, z), vert: 8 (over y, core).
Axes of the slice: x: 4, y: 4, z: 8, core: 2. Of those that a mesh axis runs over, the one named last changes fastest.
Arguments:
- base_flow: float32 [3, 512, 128, 256], P(None, 'stream', 'vert'), may hold values from -6 to 6
- adjoint_velocity: float32 [3, 512, 128, 256], P(None, 'stream', 'vert'), may hold values from -6 to 6
- reaction: float32 [512, 128, 256], P('stream', 'vert'), may hold values from 0.2 to 20
Outputs:
- advanced_velocity: float32 [3, 512, 128, 256], P(None, 'stream', 'vert')
- pressure: float32 [512, 128, 256], P('stream', 'vert')
The draws below stay inside these ranges and needn't reach their ends.
All inputs are finite; a program needn't handle non-finite values.
Results may differ from the reference program's by a relative error of at most 0.00014.
Values sent between devices are 32-bit elements; how exact they have to be, the bound alone decides.
A program may use at most 64 MiB of HBM per device.

```python
import math
import jax
import jax.numpy as jnp
import numpy as np
from jax import lax

ITERS = 3
NX = 512
NY = 128
NZ = 256


def shard_levels(rng, shape, pieces, smallest, top_value):
    factor_of = 1.0
    for dim, shards_of in pieces:
        draws = jax.random.uniform(jax.random.fold_in(jax.random.fold_in(rng, 6), dim), (shards_of,), jnp.float32, smallest / len(pieces), top_value / len(pieces))
        factor_of = factor_of * jnp.repeat(jnp.exp(draws), shape[dim] // shards_of).reshape((-1,) + (1,) * (len(shape) - 1 - dim))
    return factor_of


def gaussian(rng, shape, scale, reach, cuts=(), held_as=jnp.bfloat16):
    drawn = jax.random.normal(rng, shape, jnp.float32) * scale
    if len(cuts) > 0:
        drawn = shard_levels(rng, shape, cuts, -0.22, 0.18) * drawn
    return jnp.clip(drawn, min=-reach, max=reach).astype(held_as)


def setup_inputs(seed: int = 0) -> dict:
    seeds = jax.random.split(jax.random.key(seed), 4)
    base_flow = gaussian(seeds[0], (3, NX, NY, NZ), 1.0, 6.0, ((1, 32), (2, 8)), jnp.float32)
    adjoint_velocity = gaussian(seeds[1], (3, NX, NY, NZ), 1.0, 6.0, ((1, 32), (2, 8)), jnp.float32)
    reaction = jnp.clip(jnp.exp(math.log(20.0) - 4.6051702 * jax.random.uniform(seeds[2], (NX, NY, NZ), jnp.float32) ** shard_levels(seeds[2], (NX, NY, NZ), ((0, 32), (1, 8)), -0.2, 0.2)), 0.2, 20.0)
    return dict(base_flow=base_flow, adjoint_velocity=adjoint_velocity, reaction=reaction)


time_step = 0.05


def gll_tables():
    degree = 7
    inner_nodes = np.array([0.8717401485096066, 0.5917001814331423, 0.2092992179024789])
    points_ref = np.concatenate([[-1.0], -inner_nodes, inner_nodes[::-1], [1.0]])
    previous = np.ones(8)
    current = points_ref.copy()
    for order_now in range(1, degree):
        following = ((2 * order_now + 1) * points_ref * current - order_now * previous) / (order_now + 1)
        previous = current
        current = following
    legendre_at = current
    quadrature = 2.0 / (degree * (degree + 1) * legendre_at ** 2)
    derivative_table = np.zeros((8, 8))
    for i in range(8):
        for j in range(8):
            if i != j:
                derivative_table[i, j] = legendre_at[i] / (legendre_at[j] * (points_ref[i] - points_ref[j]))
    derivative_table[0, 0] = -degree * (degree + 1) / 4.0
    derivative_table[7, 7] = degree * (degree + 1) / 4.0
    return derivative_table, quadrature


def derive(volume, operator_table, which_axis):
    components, rows_x, rows_y, rows_z = volume.shape
    if which_axis == 1:
        blocks = volume.reshape(components, rows_x // 8, 8, rows_y * rows_z)
        result = jnp.einsum("ab,cebr->cear", operator_table, blocks, precision=lax.Precision.HIGHEST)
    elif which_axis == 2:
        blocks = volume.reshape(components * rows_x, rows_y // 8, 8, rows_z)
        result = jnp.einsum("ab,mebz->meaz", operator_table, blocks, precision=lax.Precision.HIGHEST)
    else:
        band_matrix = jnp.kron(jnp.eye(16, dtype=operator_table.dtype), operator_table.T)
        result = jnp.dot(volume.reshape(-1, 128), band_matrix, precision=lax.Precision.HIGHEST)
    return result.reshape(volume.shape)


def fold_rim(padded, which_axis):
    length = padded.shape[which_axis] - 2
    centre = lax.slice_in_dim(padded, 1, length + 1, axis=which_axis)
    upper_side = lax.slice_in_dim(padded, 2, length + 2, axis=which_axis)
    lower_side = lax.slice_in_dim(padded, 0, length, axis=which_axis)
    position = lax.broadcasted_iota(jnp.int32, centre.shape, which_axis) % 8
    return centre + jnp.where(position == 7, upper_side, 0.0) + jnp.where(position == 0, lower_side, 0.0)


def fold_span(volume):
    position = lax.broadcasted_iota(jnp.int32, volume.shape, 3) % 8
    upper_side = jnp.roll(volume, -1, axis=3)
    lower_side = jnp.roll(volume, 1, axis=3)
    return volume + jnp.where(position == 7, upper_side, 0.0) + jnp.where(position == 0, lower_side, 0.0)


def assemble(volume):
    padded = jnp.pad(volume, ((0, 0), (1, 1), (1, 1), (0, 0)))
    return fold_span(fold_rim(fold_rim(padded, 1), 2))


def multiplicity(rows, offset, summed_rows):
    position = jnp.arange(rows, dtype=jnp.int32)
    global_row = offset + position
    shared = ((position % 8 == 7) & (global_row < summed_rows - 1)) | ((position % 8 == 0) & (global_row > 0))
    return 1.0 + shared.astype(jnp.float32)


def local_operator(volume, derivative_table, weights, reaction):
    summed = derive(weights * derive(volume, derivative_table, 1), derivative_table.T, 1)
    summed = summed + derive(weights * derive(volume, derivative_table, 2), derivative_table.T, 2)
    summed = summed + derive(weights * derive(volume, derivative_table, 3), derivative_table.T, 3)
    return summed + reaction * weights * volume


def convection(base_flow, adjoint_velocity, derivative_table):
    grad_adjoint = [derive(adjoint_velocity, derivative_table, which_axis) for which_axis in (1, 2, 3)]
    grad_base = [derive(base_flow, derivative_table, which_axis) for which_axis in (1, 2, 3)]
    carried = base_flow[0] * grad_adjoint[0] + base_flow[1] * grad_adjoint[1] + base_flow[2] * grad_adjoint[2]
    turned = jnp.stack([jnp.sum(adjoint_velocity * grad_base[c], axis=0) for c in range(3)])
    return carried - turned


def reference(base_flow, adjoint_velocity, reaction):
    table_host, quad_host = gll_tables()
    derivative_table = jnp.asarray(table_host, jnp.float32)
    quadrature = jnp.asarray(quad_host, jnp.float32)
    components, rows_x, rows_y, rows_z = adjoint_velocity.shape
    weight_x = jnp.tile(quadrature, rows_x // 8)
    weight_y = jnp.tile(quadrature, rows_y // 8)
    weight_z = jnp.tile(quadrature, rows_z // 8)
    weights = weight_x[:, None, None] * weight_y[None, :, None] * weight_z[None, None, :]
    mult_x = multiplicity(rows_x, 0, rows_x)
    mult_y = multiplicity(rows_y, 0, rows_y)
    span_pos = jnp.arange(rows_z, dtype=jnp.int32) % 8
    mult_z = 1.0 + ((span_pos == 7) | (span_pos == 0)).astype(jnp.float32)
    mult_all = mult_x[:, None, None] * mult_y[None, :, None] * mult_z[None, None, :]
    inverse_mult = 1.0 / mult_all
    mass_sum = weights * mult_all

    conv = convection(base_flow, adjoint_velocity, derivative_table)
    advanced = adjoint_velocity + time_step * assemble(weights * conv) / mass_sum
    rhs = derive(weights * advanced[0:1], derivative_table.T, 1)
    rhs = rhs + derive(weights * advanced[1:2], derivative_table.T, 2)
    rhs = rhs + derive(weights * advanced[2:3], derivative_table.T, 3)
    rhs = assemble(rhs)

    pressure = jnp.zeros_like(rhs)
    residual = rhs
    direction = rhs
    norm_now = jnp.sum(residual * residual * inverse_mult)
    for iteration in range(ITERS):
        applied = assemble(local_operator(direction, derivative_table, weights, reaction))
        step_size = norm_now / jnp.sum(direction * applied * inverse_mult)
        pressure = pressure + step_size * direction
        residual = residual - step_size * applied
        if iteration + 1 < ITERS:
            norm_next = jnp.sum(residual * residual * inverse_mult)
            direction = residual + (norm_next / norm_now) * direction
            norm_now = norm_next
    grad_pressure = jnp.concatenate([derive(pressure, derivative_table, which_axis) for which_axis in (1, 2, 3)], axis=0)
    result = advanced - assemble(weights * grad_pressure) / mass_sum
    return result, pressure[0]
```

```python
import functools

import jax
import jax.numpy as jnp
import ml_dtypes
import numpy as np
from jax import lax
from jax.experimental import pallas as pl
from jax.experimental.pallas import tpu as pltpu
from jax.sharding import PartitionSpec as P

time_step = 0.05
MESH = pl.DeviceIdType.MESH
F32 = jnp.float32
BF16 = jnp.bfloat16
SIDES = ((1, 0), (-1, 0), (0, 1), (0, -1), (1, 1), (1, -1), (-1, 1), (-1, -1))
FIELDS = (3, 1, 1, 4, 6)


def gll_tables():
    degree = 7
    inner_nodes = np.array([0.8717401485096066, 0.5917001814331423, 0.2092992179024789])
    points_ref = np.concatenate([[-1.0], -inner_nodes, inner_nodes[::-1], [1.0]])
    previous = np.ones(8)
    current = points_ref.copy()
    for order_now in range(1, degree):
        following = ((2 * order_now + 1) * points_ref * current - order_now * previous) / (
            order_now + 1
        )
        previous = current
        current = following
    quadrature = 2.0 / (degree * (degree + 1) * current**2)
    derivative_table = np.zeros((8, 8))
    for i in range(8):
        for j in range(8):
            if i != j:
                derivative_table[i, j] = current[i] / (current[j] * (points_ref[i] - points_ref[j]))
    derivative_table[0, 0] = -degree * (degree + 1) / 4.0
    derivative_table[7, 7] = degree * (degree + 1) / 4.0
    return (derivative_table, quadrature)


def halves(matrix):
    high = matrix.astype(np.float32).astype(ml_dtypes.bfloat16)
    low = (matrix - high.astype(np.float64)).astype(ml_dtypes.bfloat16)
    return np.stack([high, low])


def constants(nx, ny, nz):
    table, quad = gll_tables()
    table = table.astype(np.float32).astype(np.float64)
    quad = quad.astype(np.float32).astype(np.float64)
    turned = table.T * quad[None, :] / quad[:, None]
    stiff = turned @ table
    eye = np.eye

    def along_x(m):
        return np.kron(np.kron(eye(nx // 8), m), eye(ny))

    def along_y(m):
        return np.kron(eye(nx * ny // 8), m)

    def along_z(m):
        return np.kron(eye(nz // 8), m.T)

    weights = (
        np.tile(quad, nx // 8)[:, None, None]
        * np.tile(quad, ny // 8)[None, :, None]
        * np.tile(quad, nz // 8)[None, None, :]
    ).astype(np.float32)
    twice = np.array([2.0, 1, 1, 1, 1, 1, 1, 2.0])
    mult = (
        np.tile(twice, nx // 8)[:, None, None]
        * np.tile(twice, ny // 8)[None, :, None]
        * np.tile(twice, nz // 8)[None, None, :]
    )
    return [
        halves(np.concatenate([along_x(table), along_y(table)], axis=0)),
        halves(along_z(table)),
        halves(np.concatenate([along_x(turned), along_y(turned)], axis=1)),
        halves(along_z(turned)),
        halves(along_x(stiff) + along_y(stiff)),
        halves(along_z(stiff)),
        weights,
        (1.0 / mult).astype(np.float32),
    ]


def split(value):
    high = value.astype(BF16)
    low = (value - high.astype(F32)).astype(BF16)
    return high, low


def dot(a, b):
    return jnp.dot(a, b, preferred_element_type=F32)


def left(matrix, parts):
    high, low = parts
    return dot(matrix[0], high) + dot(matrix[0], low) + dot(matrix[1], high)


def right(parts, matrix):
    high, low = parts
    return dot(high, matrix[0]) + dot(low, matrix[0]) + dot(high, matrix[1])


def kernel(
    n_stream,
    n_vert,
    base_h, adj_h, reac_h, kxy_h, kz_h, cxy_h, cz_h, bxy_h, bz_h, w_h, im_h,
    out_h, pres_h,
    base, adj, reac, kxy, kz, cxy, cz, bxy, bz, wts, imult,
    imass, conv, moved, loc, vec, grads, part3, outbuf, pbuf,
    tiles, red_a, red_b,
    in_sem, out_sem, send_sem, recv_sem, red_send, red_recv,
    *halo,
):
    me_s = lax.axis_index("stream")
    me_v = lax.axis_index("vert")
    nx, ny, nz = reac.shape
    rows = nx * ny

    inputs = [
        (kxy_h, kxy), (kz_h, kz), (adj_h, adj), (base_h, base), (w_h, wts), (im_h, imult),
        (cxy_h, cxy), (cz_h, cz), (bxy_h, bxy), (bz_h, bz), (reac_h, reac),
    ]
    loads = [pltpu.make_async_copy(a, b, in_sem.at[i]) for i, (a, b) in enumerate(inputs)]
    for load in loads:
        load.start()

    def near(ds, dv):
        return (lax.rem(me_s + ds + n_stream, n_stream), lax.rem(me_v + dv + n_vert, n_vert))

    barrier = pltpu.get_barrier_semaphore()
    partners = [near(ds, dv) for ds, dv in SIDES]
    partners += [near(0, k) for k in range(1, n_vert)]
    partners += [near(k, 0) for k in range(1, n_stream)]
    for partner in partners:
        pl.semaphore_signal(barrier, inc=1, device_id=partner, device_id_type=MESH)

    def flat(ref):
        return ref[...].reshape(rows, nz)

    lane = lax.broadcasted_iota(jnp.int32, (ny, nz), 1) % 8
    sub = lax.broadcasted_iota(jnp.int32, (8, nz), 0)
    row = lax.broadcasted_iota(jnp.int32, (ny, nz), 0)

    def fold_store(value, ref):
        for i in range(nx):
            v = value[i * ny:(i + 1) * ny]
            up = pltpu.roll(v, nz - 1, 1)
            down = pltpu.roll(v, 1, 1)
            ref[i] = v + jnp.where(lane == 7, up, 0.0) + jnp.where(lane == 0, down, 0.0)
        both = ref[7] + ref[8]
        ref[7] = both
        ref[8] = both
        both = ref[:, 7:8, :] + ref[:, 8:9, :]
        ref[:, 7:8, :] = both
        ref[:, 8:9, :] = both

    def copies(e, src):
        xs, ys, cs = halo[3 * e:3 * e + 3]
        made = []
        for n, (ds, dv) in enumerate(SIDES):
            if dv == 0:
                a = src.at[:, nx - 1 if ds > 0 else 0]
                b = xs.at[0 if ds > 0 else 1]
            else:
                at = pl.ds(ny - 1 if dv > 0 else 0, 1)
                if ds == 0:
                    a = src.at[:, :, at, :]
                    b = ys.at[0 if dv > 0 else 1].at[:, :, pl.ds(0 if dv > 0 else 7, 1), :]
                else:
                    a = src.at[:, nx - 1 if ds > 0 else 0, at, :]
                    b = cs.at[0 if ds > 0 else 1].at[:, pl.ds(0 if dv > 0 else ny - 1, 1), :]
            made.append(
                pltpu.make_async_remote_copy(
                    src_ref=a, dst_ref=b,
                    send_sem=send_sem.at[e, n], recv_sem=recv_sem.at[e, n],
                    device_id=near(ds, dv), device_id_type=MESH,
                )
            )
        for copy in made:
            copy.start()
        return made

    has_xl = me_s > 0
    has_xh = me_s < n_stream - 1
    has_yl = me_v > 0
    has_yh = me_v < n_vert - 1

    def with_halo(e, f, src, i):
        xs, ys, cs = halo[3 * e:3 * e + 3]
        low = src[f, i, 0:8, :] + jnp.where((sub == 0) & has_yl, ys[0, f, i], 0.0)
        high = src[f, i, ny - 8:ny, :] + jnp.where((sub == 7) & has_yh, ys[1, f, i], 0.0)
        value = jnp.concatenate([low, high], axis=0)
        if i in (0, nx - 1):
            side = 0 if i == 0 else 1
            there = has_xl if i == 0 else has_xh
            known = ((row == 0) & has_yl) | ((row == ny - 1) & has_yh)
            value = value + jnp.where(there, xs[side, f] + jnp.where(known, cs[side, f], 0.0), 0.0)
        return value

    def operate(value, parts):
        return wts[...].reshape(rows, nz) * (
            left(bxy, parts) + right(parts, bz) + flat(reac) * value
        )

    def gradient(parts, k, dst, at):
        w = wts[...].reshape(rows, nz)
        both = left(kxy, parts)
        fold_store(w * both[:rows], dst.at[at])
        fold_store(w * both[rows:], dst.at[at + 1])
        fold_store(w * right(parts, kz), dst.at[at + 2])

    def to_row(value, slot):
        s = value.reshape(rows // 8, 8, nz).sum(axis=0)
        s = s[:, :128] + s[:, 128:]
        tiles[0, slot:slot + 1, :] = jnp.sum(s, axis=0, keepdims=True)

    for i in range(4):
        loads[i].wait()
    for c in range(3):
        parts = split(flat(adj.at[c]))
        both = left(kxy, parts)
        conv[c] = (
            flat(base.at[0]) * both[:rows] + flat(base.at[1]) * both[rows:]
            + flat(base.at[2]) * right(parts, kz)
        ).reshape(nx, ny, nz)
    for j in range(3):
        parts = split(flat(base.at[j]))
        a = flat(adj.at[j])
        both = left(kxy, parts)
        conv[0] -= (a * both[:rows]).reshape(nx, ny, nz)
        conv[1] -= (a * both[rows:]).reshape(nx, ny, nz)
        conv[2] -= (a * right(parts, kz)).reshape(nx, ny, nz)
    loads[4].wait()
    for c in range(3):
        fold_store(flat(conv.at[c]) * flat(wts), part3.at[c])
    pl.semaphore_wait(barrier, len(partners))
    sends = [copies(0, part3)]

    loads[5].wait()
    for i in range(nx):
        value = imult[i]
        edge = ((row == 0) & (me_v == 0)) | ((row == ny - 1) & (me_v == n_vert - 1))
        value = value * jnp.where(edge, 2.0, 1.0)
        if i in (0, nx - 1):
            value = value * jnp.where((me_s == 0) if i == 0 else (me_s == n_stream - 1), 2.0, 1.0)
        imult[i] = value
        imass[i] = value / wts[i]
    for i in range(6, 11):
        loads[i].wait()

    for copy in sends[0]:
        copy.wait_recv()
    for c in range(3):
        for i in range(nx):
            moved[c, i] = adj[c, i] + time_step * with_halo(0, c, part3, i) * imass[i]

    pair = jnp.concatenate([flat(moved.at[0]), flat(moved.at[1])], axis=0)
    rhs = left(cxy, split(pair)) + right(split(flat(moved.at[2])), cz)
    fold_store(rhs * flat(wts), loc.at[0].at[0])
    sends.append(copies(1, loc.at[0]))
    for copy in sends[1]:
        copy.wait_recv()
    for i in range(nx):
        vec[0, i] = with_halo(1, 0, loc.at[0], i)

    v = flat(vec.at[0])
    parts = split(v)
    image = operate(v, parts)
    fold_store(image, loc.at[1].at[0])
    sends.append(copies(2, loc.at[1]))
    to_row(v * v * flat(imult), 0)
    to_row(v * image, 1)
    gradient(parts, 0, grads, 1)
    for copy in sends[2]:
        copy.wait_recv()
    for i in range(nx):
        vec[1, i] = with_halo(2, 0, loc.at[1], i)

    v = flat(vec.at[1])
    parts = split(v)
    image = operate(v, parts)
    fold_store(image, grads.at[0])
    sends.append(copies(3, grads))
    to_row(v * v * flat(imult), 2)
    to_row(v * image, 3)
    gradient(parts, 1, outbuf, 0)
    for copy in sends[3]:
        copy.wait_recv()
    for i in range(nx):
        vec[2, i] = with_halo(3, 0, grads, i)

    v = flat(vec.at[2])
    parts = split(v)
    image = operate(v, parts)
    to_row(v * v * flat(imult), 4)
    to_row(v * image, 5)
    tiles[0, 6:8, :] = jnp.zeros((2, 128), F32)

    def spread(src, slots, n, which):
        made = [
            pltpu.make_async_remote_copy(
                src_ref=src, dst_ref=slots.at[k - 1],
                send_sem=red_send.at[which], recv_sem=red_recv.at[which],
                device_id=near(0, k) if which == 0 else near(k, 0), device_id_type=MESH,
            )
            for k in range(1, n)
        ]
        for copy in made:
            copy.start()

    def whole(slots, which):
        return pltpu.make_async_remote_copy(
            src_ref=slots, dst_ref=slots,
            send_sem=red_send.at[which], recv_sem=red_recv.at[which],
            device_id=near(0, 1), device_id_type=MESH,
        )

    spread(tiles.at[0], red_a, n_vert, 0)
    gradient(parts, 2, outbuf, 3)
    sends.append(copies(4, outbuf))
    whole(red_a, 0).wait_recv()
    total = tiles[0]
    for k in range(n_vert - 1):
        total = total + red_a[k]
    tiles[1] = total
    spread(tiles.at[1], red_b, n_stream, 1)

    for d in range(3):
        for i in range(nx):
            conv[d, i] = with_halo(3, 1 + d, grads, i) * imass[i]
    for copy in sends[4]:
        copy.wait_recv()
    for d in range(3):
        for i in range(nx):
            base[d, i] = with_halo(4, d, outbuf, i) * imass[i]
            adj[d, i] = with_halo(4, 3 + d, outbuf, i) * imass[i]

    whole(red_b, 1).wait_recv()
    total = tiles[1]
    for k in range(n_stream - 1):
        total = total + red_b[k]
    m = [jnp.sum(total[k:k + 1], axis=1, keepdims=True) for k in range(6)]
    a0 = m[0] / m[1]
    r1 = a0 * a0 * m[2] - m[0]
    k1 = 1.0 + r1 / m[0]
    p1 = k1 * k1 * m[1] - 2.0 * k1 * a0 * m[2] + a0 * a0 * m[3]
    a1 = r1 / p1
    e1 = -(a0 + a1 * k1)
    e2 = a1 * a0
    r2 = m[0] + 2.0 * e1 * m[1] + (e1 * e1 + 2.0 * e2) * m[2] + 2.0 * e1 * e2 * m[3] + e2 * e2 * m[4]
    b2 = r2 / r1
    f0 = 1.0 + b2 * k1
    f1 = e1 - b2 * a0
    f2 = e2
    p2 = (
        f0 * f0 * m[1] + 2.0 * f0 * f1 * m[2] + (f1 * f1 + 2.0 * f0 * f2) * m[3]
        + 2.0 * f1 * f2 * m[4] + f2 * f2 * m[5]
    )
    a2 = r2 / p2
    c0 = a0 + a1 * k1 + a2 * f0
    c1 = a2 * f1 - a1 * a0
    c2 = a2 * f2

    outs = []
    for i in range(nx):
        pbuf[i] = c0 * vec[0, i] + c1 * vec[1, i] + c2 * vec[2, i]
    outs.append(pltpu.make_async_copy(pbuf, pres_h, out_sem.at[3]))
    outs[-1].start()
    for d in range(3):
        for i in range(nx):
            moved[d, i] = moved[d, i] - (c0 * conv[d, i] + c1 * base[d, i] + c2 * adj[d, i])
        outs.append(pltpu.make_async_copy(moved.at[d], out_h.at[d], out_sem.at[d]))
        outs[-1].start()
    for group in sends:
        for copy in group:
            copy.wait_send()
    whole(red_a, 0).wait_send()
    whole(red_b, 1).wait_send()
    for copy in outs:
        copy.wait()


def on_device(n_stream, n_vert, base_flow, adjoint_velocity, reaction):
    nx, ny, nz = reaction.shape
    consts = constants(nx, ny, nz)
    field = (nx, ny, nz)
    scratch = [
        pltpu.VMEM(base_flow.shape, F32),
        pltpu.VMEM(base_flow.shape, F32),
        pltpu.VMEM(field, F32),
        *[pltpu.VMEM(c.shape, c.dtype) for c in consts],
        pltpu.VMEM(field, F32),
        pltpu.VMEM((3, *field), F32),
        pltpu.VMEM((3, *field), F32),
        pltpu.VMEM((2, 1, *field), F32),
        pltpu.VMEM((3, *field), F32),
        pltpu.VMEM((4, *field), F32),
        pltpu.VMEM((3, *field), F32),
        pltpu.VMEM((6, *field), F32),
        pltpu.VMEM(field, F32),
        pltpu.VMEM((2, 8, 128), F32),
        pltpu.VMEM((n_vert - 1, 8, 128), F32),
        pltpu.VMEM((n_stream - 1, 8, 128), F32),
        pltpu.SemaphoreType.DMA((11,)),
        pltpu.SemaphoreType.DMA((4,)),
        pltpu.SemaphoreType.DMA((5, 8)),
        pltpu.SemaphoreType.DMA((5, 8)),
        pltpu.SemaphoreType.DMA((2,)),
        pltpu.SemaphoreType.DMA((2,)),
    ]
    for count in FIELDS:
        scratch += [
            pltpu.VMEM((2, count, ny, nz), F32),
            pltpu.VMEM((2, count, nx, 8, nz), F32),
            pltpu.VMEM((2, count, ny, nz), F32),
        ]
    return pl.pallas_call(
        functools.partial(kernel, n_stream, n_vert),
        out_shape=(
            jax.ShapeDtypeStruct(base_flow.shape, F32),
            jax.ShapeDtypeStruct(field, F32),
        ),
        in_specs=[pl.BlockSpec(memory_space=pl.ANY)] * 11,
        out_specs=(pl.BlockSpec(memory_space=pl.ANY), pl.BlockSpec(memory_space=pl.ANY)),
        scratch_shapes=scratch,
        compiler_params=pltpu.CompilerParams(
            collective_id=0, has_side_effects=True, vmem_limit_bytes=48 * 1024 * 1024
        ),
    )(base_flow, adjoint_velocity, reaction, *[jnp.asarray(c) for c in consts])


def solution(mesh):
    placed = (
        P(None, "stream", "vert", None),
        P(None, "stream", "vert", None),
        P("stream", "vert", None),
    )
    return jax.shard_map(
        functools.partial(on_device, mesh.shape["stream"], mesh.shape["vert"]),
        mesh=mesh,
        in_specs=placed,
        out_specs=(P(None, "stream", "vert", None), P("stream", "vert", None)),
        check_vma=False,
    )
```

```python
import functools

import jax
import jax.numpy as jnp
import ml_dtypes
import numpy as np
from jax import lax
from jax.experimental import pallas as pl
from jax.experimental.pallas import tpu as pltpu
from jax.sharding import PartitionSpec as P

time_step = 0.05
MESH = pl.DeviceIdType.MESH
F32 = jnp.float32
BF16 = jnp.bfloat16
SIDES = ((1, 0), (-1, 0), (0, 1), (0, -1), (1, 1), (1, -1), (-1, 1), (-1, -1))
FIELDS = (3, 1, 1, 4, 6)


def gll_tables():
    degree = 7
    inner_nodes = np.array([0.8717401485096066, 0.5917001814331423, 0.2092992179024789])
    points_ref = np.concatenate([[-1.0], -inner_nodes, inner_nodes[::-1], [1.0]])
    previous = np.ones(8)
    current = points_ref.copy()
    for order_now in range(1, degree):
        following = ((2 * order_now + 1) * points_ref * current - order_now * previous) / (
            order_now + 1
        )
        previous = current
        current = following
    quadrature = 2.0 / (degree * (degree + 1) * current**2)
    derivative_table = np.zeros((8, 8))
    for i in range(8):
        for j in range(8):
            if i != j:
                derivative_table[i, j] = current[i] / (current[j] * (points_ref[i] - points_ref[j]))
    derivative_table[0, 0] = -degree * (degree + 1) / 4.0
    derivative_table[7, 7] = degree * (degree + 1) / 4.0
    return (derivative_table, quadrature)


def halves(matrix):
    high = matrix.astype(np.float32).astype(ml_dtypes.bfloat16)
    low = (matrix - high.astype(np.float64)).astype(ml_dtypes.bfloat16)
    return np.stack([high, low])


def constants(nx, ny, nz):
    table, quad = gll_tables()
    table = table.astype(np.float32).astype(np.float64)
    quad = quad.astype(np.float32).astype(np.float64)
    turned = table.T * quad[None, :] / quad[:, None]
    stiff = turned @ table
    eye = np.eye

    def along_x(m):
        return np.kron(np.kron(eye(nx // 8), m), eye(ny))

    def along_y(m):
        return np.kron(eye(nx * ny // 8), m)

    def along_z(m):
        return np.kron(eye(nz // 8), m.T)

    weights = (
        np.tile(quad, nx // 8)[:, None, None]
        * np.tile(quad, ny // 8)[None, :, None]
        * np.tile(quad, nz // 8)[None, None, :]
    ).astype(np.float32)
    twice = np.array([2.0, 1, 1, 1, 1, 1, 1, 2.0])
    mult = (
        np.tile(twice, nx // 8)[:, None, None]
        * np.tile(twice, ny // 8)[None, :, None]
        * np.tile(twice, nz // 8)[None, None, :]
    )
    return [
        halves(np.concatenate([along_x(table), along_y(table)], axis=0)),
        halves(along_z(table)),
        halves(np.concatenate([along_x(turned), along_y(turned)], axis=1)),
        halves(along_z(turned)),
        halves(along_x(stiff) + along_y(stiff)),
        halves(along_z(stiff)),
        weights,
        (1.0 / mult).astype(np.float32),
    ]


def split(value):
    high = value.astype(BF16)
    low = (value - high.astype(F32)).astype(BF16)
    return high, low


def dot(a, b):
    return jnp.dot(a, b, preferred_element_type=F32)


def left(matrix, parts):
    high, low = parts
    return dot(matrix[0], high) + dot(matrix[0], low) + dot(matrix[1], high)


def right(parts, matrix):
    high, low = parts
    return dot(high, matrix[0]) + dot(low, matrix[0]) + dot(high, matrix[1])


def kernel(
    n_stream,
    n_vert,
    base_h, adj_h, reac_h, kxy_h, kz_h, cxy_h, cz_h, bxy_h, bz_h, w_h, im_h,
    out_h, pres_h,
    base, adj, reac, kxy, kz, cxy, cz, bxy, bz, wts, imult,
    imass, conv, moved, loc, vec, grads, part3, outbuf, pbuf,
    tiles, red_a, red_b,
    in_sem, out_sem, send_sem, recv_sem, red_send, red_recv,
    *halo,
):
    me_s = lax.axis_index("stream")
    me_v = lax.axis_index("vert")
    nx, ny, nz = reac.shape
    rows = nx * ny

    inputs = [
        (kxy_h, kxy), (kz_h, kz), (adj_h, adj), (base_h, base), (w_h, wts), (im_h, imult),
        (cxy_h, cxy), (cz_h, cz), (bxy_h, bxy), (bz_h, bz), (reac_h, reac),
    ]
    loads = [pltpu.make_async_copy(a, b, in_sem.at[i]) for i, (a, b) in enumerate(inputs)]
    for load in loads:
        load.start()

    def near(ds, dv):
        return (lax.rem(me_s + ds + n_stream, n_stream), lax.rem(me_v + dv + n_vert, n_vert))

    barrier = pltpu.get_barrier_semaphore()
    partners = [near(ds, dv) for ds, dv in SIDES]
    partners += [near(0, k) for k in range(1, n_vert)]
    partners += [near(k, 0) for k in range(1, n_stream)]
    for partner in partners:
        pl.semaphore_signal(barrier, inc=1, device_id=partner, device_id_type=MESH)

    has_xl = me_s > 0
    has_xh = me_s < n_stream - 1
    has_yl = me_v > 0
    has_yh = me_v < n_vert - 1

    def exists(ds, dv):
        conditions = []
        if ds:
            conditions.append(has_xh if ds > 0 else has_xl)
        if dv:
            conditions.append(has_yh if dv > 0 else has_yl)
        return functools.reduce(jnp.logical_and, conditions)

    def flat(ref):
        return ref[...].reshape(rows, nz)

    lane = lax.broadcasted_iota(jnp.int32, (ny, nz), 1) % 8
    sub = lax.broadcasted_iota(jnp.int32, (8, nz), 0)
    row = lax.broadcasted_iota(jnp.int32, (ny, nz), 0)

    def fold_store(value, ref):
        for i in range(nx):
            v = value[i * ny:(i + 1) * ny]
            up = pltpu.roll(v, nz - 1, 1)
            down = pltpu.roll(v, 1, 1)
            ref[i] = v + jnp.where(lane == 7, up, 0.0) + jnp.where(lane == 0, down, 0.0)
        both = ref[7] + ref[8]
        ref[7] = both
        ref[8] = both
        both = ref[:, 7:8, :] + ref[:, 8:9, :]
        ref[:, 7:8, :] = both
        ref[:, 8:9, :] = both

    def copies(e, src):
        xs, ys, cs = halo[3 * e:3 * e + 3]
        made = []
        for n, (ds, dv) in enumerate(SIDES):
            if dv == 0:
                a = src.at[:, nx - 1 if ds > 0 else 0]
                b = xs.at[0 if ds > 0 else 1]
            else:
                at = pl.ds(ny - 1 if dv > 0 else 0, 1)
                if ds == 0:
                    a = src.at[:, :, at, :]
                    b = ys.at[0 if dv > 0 else 1].at[:, :, pl.ds(0 if dv > 0 else 7, 1), :]
                else:
                    a = src.at[:, nx - 1 if ds > 0 else 0, at, :]
                    b = cs.at[0 if ds > 0 else 1].at[:, pl.ds(0 if dv > 0 else ny - 1, 1), :]
            made.append(
                pltpu.make_async_remote_copy(
                    src_ref=a, dst_ref=b,
                    send_sem=send_sem.at[e, n], recv_sem=recv_sem.at[e, n],
                    device_id=near(ds, dv), device_id_type=MESH,
                )
            )
        for copy, (ds, dv) in zip(made, SIDES):
            pl.when(exists(ds, dv))(copy.start)
        return made

    def arrive(made):
        for copy, (ds, dv) in zip(made, SIDES):
            pl.when(exists(-ds, -dv))(copy.wait_recv)

    def leave(made):
        for copy, (ds, dv) in zip(made, SIDES):
            pl.when(exists(ds, dv))(copy.wait_send)

    def with_halo(e, f, src, i):
        xs, ys, cs = halo[3 * e:3 * e + 3]
        low = src[f, i, 0:8, :] + jnp.where((sub == 0) & has_yl, ys[0, f, i], 0.0)
        high = src[f, i, ny - 8:ny, :] + jnp.where((sub == 7) & has_yh, ys[1, f, i], 0.0)
        value = jnp.concatenate([low, high], axis=0)
        if i in (0, nx - 1):
            side = 0 if i == 0 else 1
            there = has_xl if i == 0 else has_xh
            known = ((row == 0) & has_yl) | ((row == ny - 1) & has_yh)
            value = value + jnp.where(there, xs[side, f] + jnp.where(known, cs[side, f], 0.0), 0.0)
        return value

    def operate(value, parts):
        return wts[...].reshape(rows, nz) * (
            left(bxy, parts) + right(parts, bz) + flat(reac) * value
        )

    def gradient(parts, k, dst, at):
        w = wts[...].reshape(rows, nz)
        both = left(kxy, parts)
        fold_store(w * both[:rows], dst.at[at])
        fold_store(w * both[rows:], dst.at[at + 1])
        fold_store(w * right(parts, kz), dst.at[at + 2])

    def to_row(value, slot):
        s = value.reshape(rows // 8, 8, nz).sum(axis=0)
        s = s[:, :128] + s[:, 128:]
        tiles[slot:slot + 1, :] = jnp.sum(s, axis=0, keepdims=True)

    for i in range(4):
        loads[i].wait()
    for c in range(3):
        parts = split(flat(adj.at[c]))
        both = left(kxy, parts)
        conv[c] = (
            flat(base.at[0]) * both[:rows] + flat(base.at[1]) * both[rows:]
            + flat(base.at[2]) * right(parts, kz)
        ).reshape(nx, ny, nz)
    for j in range(3):
        parts = split(flat(base.at[j]))
        a = flat(adj.at[j])
        both = left(kxy, parts)
        conv[0] -= (a * both[:rows]).reshape(nx, ny, nz)
        conv[1] -= (a * both[rows:]).reshape(nx, ny, nz)
        conv[2] -= (a * right(parts, kz)).reshape(nx, ny, nz)
    loads[4].wait()
    for c in range(3):
        fold_store(flat(conv.at[c]) * flat(wts), part3.at[c])
    pl.semaphore_wait(barrier, len(partners))
    sends = [copies(0, part3)]

    loads[5].wait()
    for i in range(nx):
        value = imult[i]
        edge = ((row == 0) & (me_v == 0)) | ((row == ny - 1) & (me_v == n_vert - 1))
        value = value * jnp.where(edge, 2.0, 1.0)
        if i in (0, nx - 1):
            value = value * jnp.where((me_s == 0) if i == 0 else (me_s == n_stream - 1), 2.0, 1.0)
        imult[i] = value
        imass[i] = value / wts[i]
    for i in range(6, 11):
        loads[i].wait()

    arrive(sends[0])
    for c in range(3):
        for i in range(nx):
            moved[c, i] = adj[c, i] + time_step * with_halo(0, c, part3, i) * imass[i]

    pair = jnp.concatenate([flat(moved.at[0]), flat(moved.at[1])], axis=0)
    rhs = left(cxy, split(pair)) + right(split(flat(moved.at[2])), cz)
    fold_store(rhs * flat(wts), loc.at[0].at[0])
    sends.append(copies(1, loc.at[0]))
    arrive(sends[1])
    for i in range(nx):
        vec[0, i] = with_halo(1, 0, loc.at[0], i)

    v = flat(vec.at[0])
    parts = split(v)
    image = operate(v, parts)
    fold_store(image, loc.at[1].at[0])
    sends.append(copies(2, loc.at[1]))
    to_row(v * v * flat(imult), 0)
    to_row(v * image, 1)
    gradient(parts, 0, grads, 1)
    arrive(sends[2])
    for i in range(nx):
        vec[1, i] = with_halo(2, 0, loc.at[1], i)

    v = flat(vec.at[1])
    parts = split(v)
    image = operate(v, parts)
    fold_store(image, grads.at[0])
    sends.append(copies(3, grads))
    to_row(v * v * flat(imult), 2)
    to_row(v * image, 3)
    gradient(parts, 1, outbuf, 0)
    arrive(sends[3])
    for i in range(nx):
        vec[2, i] = with_halo(3, 0, grads, i)

    v = flat(vec.at[2])
    parts = split(v)
    image = operate(v, parts)
    to_row(v * v * flat(imult), 4)
    to_row(v * image, 5)

    tiles[6:8, :] = jnp.zeros((2, 128), F32)
    group = lax.broadcasted_iota(jnp.int32, (8, 128), 1) // 16
    packed = tiles[...]
    for shift in (64, 32, 16):
        packed = packed + pltpu.roll(packed, shift, 1)
    packed = jnp.where(group == lax.broadcasted_iota(jnp.int32, (8, 128), 0), packed, 0.0)
    red_a[n_vert - 1:n_vert, :] = jnp.sum(packed, axis=0, keepdims=True)

    def spread(slots, n, which):
        for k in range(1, n):
            pltpu.make_async_remote_copy(
                src_ref=slots.at[pl.ds(n - 1, 1)], dst_ref=slots.at[pl.ds(k - 1, 1)],
                send_sem=red_send.at[which], recv_sem=red_recv.at[which],
                device_id=near(0, k) if which == 0 else near(k, 0), device_id_type=MESH,
            ).start()

    def whole(slots, n, which):
        return pltpu.make_async_remote_copy(
            src_ref=slots.at[pl.ds(0, n - 1)], dst_ref=slots.at[pl.ds(0, n - 1)],
            send_sem=red_send.at[which], recv_sem=red_recv.at[which],
            device_id=near(0, 1), device_id_type=MESH,
        )

    spread(red_a, n_vert, 0)
    gradient(parts, 2, outbuf, 3)
    sends.append(copies(4, outbuf))
    whole(red_a, n_vert, 0).wait_recv()
    red_b[n_stream - 1:n_stream, :] = jnp.sum(red_a[...], axis=0, keepdims=True)
    spread(red_b, n_stream, 1)

    for d in range(3):
        for i in range(nx):
            conv[d, i] = with_halo(3, 1 + d, grads, i) * imass[i]
    arrive(sends[4])
    for d in range(3):
        for i in range(nx):
            base[d, i] = with_halo(4, d, outbuf, i) * imass[i]
            adj[d, i] = with_halo(4, 3 + d, outbuf, i) * imass[i]

    whole(red_b, n_stream, 1).wait_recv()
    total = jnp.sum(red_b[...], axis=0, keepdims=True)
    m = [jnp.sum(jnp.where(group[0:1] == k, total, 0.0), axis=1, keepdims=True) for k in range(6)]
    a0 = m[0] / m[1]
    r1 = a0 * a0 * m[2] - m[0]
    k1 = 1.0 + r1 / m[0]
    p1 = k1 * k1 * m[1] - 2.0 * k1 * a0 * m[2] + a0 * a0 * m[3]
    a1 = r1 / p1
    e1 = -(a0 + a1 * k1)
    e2 = a1 * a0
    r2 = m[0] + 2.0 * e1 * m[1] + (e1 * e1 + 2.0 * e2) * m[2] + 2.0 * e1 * e2 * m[3] + e2 * e2 * m[4]
    b2 = r2 / r1
    f0 = 1.0 + b2 * k1
    f1 = e1 - b2 * a0
    f2 = e2
    p2 = (
        f0 * f0 * m[1] + 2.0 * f0 * f1 * m[2] + (f1 * f1 + 2.0 * f0 * f2) * m[3]
        + 2.0 * f1 * f2 * m[4] + f2 * f2 * m[5]
    )
    a2 = r2 / p2
    c0 = a0 + a1 * k1 + a2 * f0
    c1 = a2 * f1 - a1 * a0
    c2 = a2 * f2

    outs = []
    for i in range(nx):
        pbuf[i] = c0 * vec[0, i] + c1 * vec[1, i] + c2 * vec[2, i]
    outs.append(pltpu.make_async_copy(pbuf, pres_h, out_sem.at[3]))
    outs[-1].start()
    for d in range(3):
        for i in range(nx):
            moved[d, i] = moved[d, i] - (c0 * conv[d, i] + c1 * base[d, i] + c2 * adj[d, i])
        outs.append(pltpu.make_async_copy(moved.at[d], out_h.at[d], out_sem.at[d]))
        outs[-1].start()
    for made in sends:
        leave(made)
    whole(red_a, n_vert, 0).wait_send()
    whole(red_b, n_stream, 1).wait_send()
    for copy in outs:
        copy.wait()


def on_device(n_stream, n_vert, base_flow, adjoint_velocity, reaction):
    nx, ny, nz = reaction.shape
    consts = constants(nx, ny, nz)
    field = (nx, ny, nz)
    scratch = [
        pltpu.VMEM(base_flow.shape, F32),
        pltpu.VMEM(base_flow.shape, F32),
        pltpu.VMEM(field, F32),
        *[pltpu.VMEM(c.shape, c.dtype) for c in consts],
        pltpu.VMEM(field, F32),
        pltpu.VMEM((3, *field), F32),
        pltpu.VMEM((3, *field), F32),
        pltpu.VMEM((2, 1, *field), F32),
        pltpu.VMEM((3, *field), F32),
        pltpu.VMEM((4, *field), F32),
        pltpu.VMEM((3, *field), F32),
        pltpu.VMEM((6, *field), F32),
        pltpu.VMEM(field, F32),
        pltpu.VMEM((8, 128), F32),
        pltpu.VMEM((n_vert, 128), F32),
        pltpu.VMEM((n_stream, 128), F32),
        pltpu.SemaphoreType.DMA((11,)),
        pltpu.SemaphoreType.DMA((4,)),
        pltpu.SemaphoreType.DMA((5, 8)),
        pltpu.SemaphoreType.DMA((5, 8)),
        pltpu.SemaphoreType.DMA((2,)),
        pltpu.SemaphoreType.DMA((2,)),
    ]
    for count in FIELDS:
        scratch += [
            pltpu.VMEM((2, count, ny, nz), F32),
            pltpu.VMEM((2, count, nx, 8, nz), F32),
            pltpu.VMEM((2, count, ny, nz), F32),
        ]
    return pl.pallas_call(
        functools.partial(kernel, n_stream, n_vert),
        out_shape=(
            jax.ShapeDtypeStruct(base_flow.shape, F32),
            jax.ShapeDtypeStruct(field, F32),
        ),
        in_specs=[pl.BlockSpec(memory_space=pl.ANY)] * 11,
        out_specs=(pl.BlockSpec(memory_space=pl.ANY), pl.BlockSpec(memory_space=pl.ANY)),
        scratch_shapes=scratch,
        compiler_params=pltpu.CompilerParams(
            collective_id=0, has_side_effects=True, vmem_limit_bytes=60 * 1024 * 1024
        ),
    )(base_flow, adjoint_velocity, reaction, *[jnp.asarray(c) for c in consts])


def solution(mesh):
    placed = (
        P(None, "stream", "vert", None),
        P(None, "stream", "vert", None),
        P("stream", "vert", None),
    )
    return jax.shard_map(
        functools.partial(on_device, mesh.shape["stream"], mesh.shape["vert"]),
        mesh=mesh,
        in_specs=placed,
        out_specs=(P(None, "stream", "vert", None), P("stream", "vert", None)),
        check_vma=False,
    )
```

```python
import functools

import jax
import jax.numpy as jnp
import ml_dtypes
import numpy as np
from jax import lax
from jax.experimental import pallas as pl
from jax.experimental.pallas import tpu as pltpu
from jax.sharding import PartitionSpec as P

time_step = 0.05
MESH = pl.DeviceIdType.MESH
F32 = jnp.float32
BF16 = jnp.bfloat16
SIDES = ((1, 0), (-1, 0), (0, 1), (0, -1), (1, 1), (1, -1), (-1, 1), (-1, -1))
FIELDS = (3, 1, 1, 4, 6)


def gll_tables():
    degree = 7
    inner_nodes = np.array([0.8717401485096066, 0.5917001814331423, 0.2092992179024789])
    points_ref = np.concatenate([[-1.0], -inner_nodes, inner_nodes[::-1], [1.0]])
    previous = np.ones(8)
    current = points_ref.copy()
    for order_now in range(1, degree):
        following = ((2 * order_now + 1) * points_ref * current - order_now * previous) / (
            order_now + 1
        )
        previous = current
        current = following
    quadrature = 2.0 / (degree * (degree + 1) * current**2)
    derivative_table = np.zeros((8, 8))
    for i in range(8):
        for j in range(8):
            if i != j:
                derivative_table[i, j] = current[i] / (current[j] * (points_ref[i] - points_ref[j]))
    derivative_table[0, 0] = -degree * (degree + 1) / 4.0
    derivative_table[7, 7] = degree * (degree + 1) / 4.0
    return (derivative_table, quadrature)


def halves(matrix):
    high = matrix.astype(np.float32).astype(ml_dtypes.bfloat16)
    low = (matrix - high.astype(np.float64)).astype(ml_dtypes.bfloat16)
    return np.stack([high, low])


def constants(nx, ny, nz):
    table, quad = gll_tables()
    table = table.astype(np.float32).astype(np.float64)
    quad = quad.astype(np.float32).astype(np.float64)
    turned = table.T * quad[None, :] / quad[:, None]
    stiff = turned @ table
    eye = np.eye

    def along_x(m):
        return np.kron(np.kron(eye(nx // 8), m), eye(ny))

    def along_y(m):
        return np.kron(eye(nx * ny // 8), m)

    def along_z(m):
        return np.kron(eye(nz // 8), m.T)

    weights = (
        np.tile(quad, nx // 8)[:, None, None]
        * np.tile(quad, ny // 8)[None, :, None]
        * np.tile(quad, nz // 8)[None, None, :]
    ).astype(np.float32)
    twice = np.array([2.0, 1, 1, 1, 1, 1, 1, 2.0])
    mult = (
        np.tile(twice, nx // 8)[:, None, None]
        * np.tile(twice, ny // 8)[None, :, None]
        * np.tile(twice, nz // 8)[None, None, :]
    )
    return [
        halves(np.concatenate([along_x(table), along_y(table)], axis=0)),
        halves(along_z(table)),
        halves(np.concatenate([along_x(turned), along_y(turned)], axis=1)),
        halves(along_z(turned)),
        halves(along_x(stiff) + along_y(stiff)),
        halves(along_z(stiff)),
        weights,
        (1.0 / mult).astype(np.float32),
    ]


def split(value):
    high = value.astype(BF16)
    low = (value - high.astype(F32)).astype(BF16)
    return high, low


def dot(a, b):
    return jnp.dot(a, b, preferred_element_type=F32)


def left(matrix, parts):
    high, low = parts
    return dot(matrix[0], high) + dot(matrix[0], low) + dot(matrix[1], high)


def right(parts, matrix):
    high, low = parts
    return dot(high, matrix[0]) + dot(low, matrix[0]) + dot(high, matrix[1])


def kernel(
    n_stream,
    n_vert,
    base_h, adj_h, reac_h, kxy_h, kz_h, cxy_h, cz_h, bxy_h, bz_h, w_h, im_h,
    out_h, pres_h,
    base, adj, reac, kxy, kz, cxy, cz, bxy, bz, wts, imult,
    imass, conv, moved, loc, vec, grads, part3, outbuf, pbuf,
    tiles, red_a, red_b,
    in_sem, out_sem, send_sem, recv_sem, red_send, red_recv,
    *halo,
):
    me_s = lax.axis_index("stream")
    me_v = lax.axis_index("vert")
    nx, ny, nz = reac.shape
    rows = nx * ny

    inputs = [
        (kxy_h, kxy), (kz_h, kz), (adj_h, adj), (base_h, base), (w_h, wts), (im_h, imult),
        (cxy_h, cxy), (cz_h, cz), (bxy_h, bxy), (bz_h, bz), (reac_h, reac),
    ]
    loads = [pltpu.make_async_copy(a, b, in_sem.at[i]) for i, (a, b) in enumerate(inputs)]
    for load in loads:
        load.start()

    def near(ds, dv):
        return (lax.rem(me_s + ds + n_stream, n_stream), lax.rem(me_v + dv + n_vert, n_vert))

    barrier = pltpu.get_barrier_semaphore()
    partners = [near(ds, dv) for ds, dv in SIDES]
    partners += [near(0, k) for k in range(1, n_vert)]
    partners += [near(k, 0) for k in range(1, n_stream)]
    for partner in partners:
        pl.semaphore_signal(barrier, inc=1, device_id=partner, device_id_type=MESH)

    has_xl = me_s > 0
    has_xh = me_s < n_stream - 1
    has_yl = me_v > 0
    has_yh = me_v < n_vert - 1

    def exists(ds, dv):
        conditions = []
        if ds:
            conditions.append(has_xh if ds > 0 else has_xl)
        if dv:
            conditions.append(has_yh if dv > 0 else has_yl)
        return functools.reduce(jnp.logical_and, conditions)

    def flat(ref):
        return ref[...].reshape(rows, nz)

    lane = lax.broadcasted_iota(jnp.int32, (ny, nz), 1) % 8
    sub = lax.broadcasted_iota(jnp.int32, (8, nz), 0)
    row = lax.broadcasted_iota(jnp.int32, (ny, nz), 0)

    def fold_store(value, ref):
        for i in range(nx):
            v = value[i * ny:(i + 1) * ny]
            up = pltpu.roll(v, nz - 1, 1)
            down = pltpu.roll(v, 1, 1)
            ref[i] = v + jnp.where(lane == 7, up, 0.0) + jnp.where(lane == 0, down, 0.0)
        both = ref[7] + ref[8]
        ref[7] = both
        ref[8] = both
        both = ref[:, 7:8, :] + ref[:, 8:9, :]
        ref[:, 7:8, :] = both
        ref[:, 8:9, :] = both

    def copies(e, src):
        xs, ys, cs = halo[3 * e:3 * e + 3]
        made = []
        for n, (ds, dv) in enumerate(SIDES):
            if dv == 0:
                a = src.at[:, nx - 1 if ds > 0 else 0]
                b = xs.at[0 if ds > 0 else 1]
            else:
                at = pl.ds(ny - 1 if dv > 0 else 0, 1)
                if ds == 0:
                    a = src.at[:, :, at, :]
                    b = ys.at[0 if dv > 0 else 1].at[:, :, pl.ds(0 if dv > 0 else 7, 1), :]
                else:
                    a = src.at[:, nx - 1 if ds > 0 else 0, at, :]
                    b = cs.at[0 if ds > 0 else 1].at[:, pl.ds(0 if dv > 0 else ny - 1, 1), :]
            made.append(
                pltpu.make_async_remote_copy(
                    src_ref=a, dst_ref=b,
                    send_sem=send_sem.at[e, n], recv_sem=recv_sem.at[e, n],
                    device_id=near(ds, dv), device_id_type=MESH,
                )
            )
        for copy, (ds, dv) in zip(made, SIDES):
            pl.when(exists(ds, dv))(copy.start)
        return made

    def arrive(made):
        for copy, (ds, dv) in zip(made, SIDES):
            pl.when(exists(-ds, -dv))(copy.wait_recv)

    def leave(made):
        for copy, (ds, dv) in zip(made, SIDES):
            pl.when(exists(ds, dv))(copy.wait_send)

    def with_halo(e, f, src, i):
        xs, ys, cs = halo[3 * e:3 * e + 3]
        low = src[f, i, 0:8, :] + jnp.where((sub == 0) & has_yl, ys[0, f, i], 0.0)
        high = src[f, i, ny - 8:ny, :] + jnp.where((sub == 7) & has_yh, ys[1, f, i], 0.0)
        value = jnp.concatenate([low, high], axis=0)
        if i in (0, nx - 1):
            side = 0 if i == 0 else 1
            there = has_xl if i == 0 else has_xh
            known = ((row == 0) & has_yl) | ((row == ny - 1) & has_yh)
            value = value + jnp.where(there, xs[side, f] + jnp.where(known, cs[side, f], 0.0), 0.0)
        return value

    def operate(value, parts):
        return wts[...].reshape(rows, nz) * (
            left(bxy, parts) + right(parts, bz) + flat(reac) * value
        )

    def gradient(parts, k, dst, at):
        w = wts[...].reshape(rows, nz)
        both = left(kxy, parts)
        fold_store(w * both[:rows], dst.at[at])
        fold_store(w * both[rows:], dst.at[at + 1])
        fold_store(w * right(parts, kz), dst.at[at + 2])

    def to_row(value, slot):
        s = value.reshape(rows // 8, 8, nz).sum(axis=0)
        s = s[:, :128] + s[:, 128:]
        tiles[slot:slot + 1, :] = jnp.sum(s, axis=0, keepdims=True)

    for i in range(4):
        loads[i].wait()
    for c in range(3):
        parts = split(flat(adj.at[c]))
        both = left(kxy, parts)
        conv[c] = (
            flat(base.at[0]) * both[:rows] + flat(base.at[1]) * both[rows:]
            + flat(base.at[2]) * right(parts, kz)
        ).reshape(nx, ny, nz)
    for j in range(3):
        parts = split(flat(base.at[j]))
        a = flat(adj.at[j])
        both = left(kxy, parts)
        conv[0] -= (a * both[:rows]).reshape(nx, ny, nz)
        conv[1] -= (a * both[rows:]).reshape(nx, ny, nz)
        conv[2] -= (a * right(parts, kz)).reshape(nx, ny, nz)
    loads[4].wait()
    for c in range(3):
        fold_store(flat(conv.at[c]) * flat(wts), part3.at[c])
    pl.semaphore_wait(barrier, len(partners))
    sends = [copies(0, part3)]

    loads[5].wait()
    for i in range(nx):
        value = imult[i]
        edge = ((row == 0) & (me_v == 0)) | ((row == ny - 1) & (me_v == n_vert - 1))
        value = value * jnp.where(edge, 2.0, 1.0)
        if i in (0, nx - 1):
            value = value * jnp.where((me_s == 0) if i == 0 else (me_s == n_stream - 1), 2.0, 1.0)
        imult[i] = value
        imass[i] = value / wts[i]
    for i in range(6, 11):
        loads[i].wait()

    arrive(sends[0])
    for c in range(3):
        for i in range(nx):
            moved[c, i] = adj[c, i] + time_step * with_halo(0, c, part3, i) * imass[i]

    pair = jnp.concatenate([flat(moved.at[0]), flat(moved.at[1])], axis=0)
    rhs = left(cxy, split(pair)) + right(split(flat(moved.at[2])), cz)
    fold_store(rhs * flat(wts), loc.at[0].at[0])
    sends.append(copies(1, loc.at[0]))
    arrive(sends[1])
    for i in range(nx):
        vec[0, i] = with_halo(1, 0, loc.at[0], i)

    v = flat(vec.at[0])
    parts = split(v)
    image = operate(v, parts)
    fold_store(image, loc.at[1].at[0])
    sends.append(copies(2, loc.at[1]))
    to_row(v * v * flat(imult), 0)
    to_row(v * image, 1)
    gradient(parts, 0, grads, 1)
    arrive(sends[2])
    for i in range(nx):
        vec[1, i] = with_halo(2, 0, loc.at[1], i)

    v = flat(vec.at[1])
    parts = split(v)
    image = operate(v, parts)
    fold_store(image, grads.at[0])
    sends.append(copies(3, grads))
    to_row(v * v * flat(imult), 2)
    to_row(v * image, 3)
    gradient(parts, 1, outbuf, 0)
    arrive(sends[3])
    for i in range(nx):
        vec[2, i] = with_halo(3, 0, grads, i)

    v = flat(vec.at[2])
    parts = split(v)
    image = operate(v, parts)
    to_row(v * v * flat(imult), 4)
    to_row(v * image, 5)

    tiles[6:8, :] = jnp.zeros((2, 128), F32)
    group = lax.broadcasted_iota(jnp.int32, (8, 128), 1) // 16
    packed = tiles[...]
    for shift in (64, 32, 16):
        packed = packed + pltpu.roll(packed, shift, 1)
    packed = jnp.where(group == lax.broadcasted_iota(jnp.int32, (8, 128), 0), packed, 0.0)
    red_a[n_vert - 1:n_vert, :] = jnp.sum(packed, axis=0, keepdims=True)

    def spread(slots, n, which):
        for k in range(1, n):
            pltpu.make_async_remote_copy(
                src_ref=slots.at[pl.ds(n - 1, 1)], dst_ref=slots.at[pl.ds(k - 1, 1)],
                send_sem=red_send.at[which], recv_sem=red_recv.at[which],
                device_id=near(0, k) if which == 0 else near(k, 0), device_id_type=MESH,
            ).start()

    def whole(slots, n, which):
        return pltpu.make_async_remote_copy(
            src_ref=slots.at[pl.ds(0, n - 1)], dst_ref=slots.at[pl.ds(0, n - 1)],
            send_sem=red_send.at[which], recv_sem=red_recv.at[which],
            device_id=near(0, 1), device_id_type=MESH,
        )

    spread(red_a, n_vert, 0)
    gradient(parts, 2, outbuf, 3)
    sends.append(copies(4, outbuf))
    whole(red_a, n_vert, 0).wait_recv()
    red_b[n_stream - 1:n_stream, :] = jnp.sum(red_a[...], axis=0, keepdims=True)
    spread(red_b, n_stream, 1)

    for d in range(3):
        for i in range(nx):
            conv[d, i] = with_halo(3, 1 + d, grads, i) * imass[i]
    arrive(sends[4])
    for d in range(3):
        for i in range(nx):
            base[d, i] = with_halo(4, d, outbuf, i) * imass[i]
            adj[d, i] = with_halo(4, 3 + d, outbuf, i) * imass[i]

    whole(red_b, n_stream, 1).wait_recv()
    total = jnp.sum(red_b[...], axis=0, keepdims=True)
    m = [jnp.sum(jnp.where(group[0:1] == k, total, 0.0), axis=1, keepdims=True) for k in range(6)]
    a0 = m[0] / m[1]
    r1 = a0 * a0 * m[2] - m[0]
    k1 = 1.0 + r1 / m[0]
    p1 = k1 * k1 * m[1] - 2.0 * k1 * a0 * m[2] + a0 * a0 * m[3]
    a1 = r1 / p1
    e1 = -(a0 + a1 * k1)
    e2 = a1 * a0
    r2 = m[0] + 2.0 * e1 * m[1] + (e1 * e1 + 2.0 * e2) * m[2] + 2.0 * e1 * e2 * m[3] + e2 * e2 * m[4]
    b2 = r2 / r1
    f0 = 1.0 + b2 * k1
    f1 = e1 - b2 * a0
    f2 = e2
    p2 = (
        f0 * f0 * m[1] + 2.0 * f0 * f1 * m[2] + (f1 * f1 + 2.0 * f0 * f2) * m[3]
        + 2.0 * f1 * f2 * m[4] + f2 * f2 * m[5]
    )
    a2 = r2 / p2
    c0 = a0 + a1 * k1 + a2 * f0
    c1 = a2 * f1 - a1 * a0
    c2 = a2 * f2

    outs = []
    for i in range(nx):
        pbuf[i] = c0 * vec[0, i] + c1 * vec[1, i] + c2 * vec[2, i]
    outs.append(pltpu.make_async_copy(pbuf, pres_h, out_sem.at[3]))
    outs[-1].start()
    for d in range(3):
        for i in range(nx):
            moved[d, i] = moved[d, i] - (c0 * conv[d, i] + c1 * base[d, i] + c2 * adj[d, i])
        outs.append(pltpu.make_async_copy(moved.at[d], out_h.at[d], out_sem.at[d]))
        outs[-1].start()
    for made in sends:
        leave(made)
    whole(red_a, n_vert, 0).wait_send()
    whole(red_b, n_stream, 1).wait_send()
    for copy in outs:
        copy.wait()


def write_out(result, pressure, out_h, pres_h, sems):
    copies = [pltpu.make_async_copy(result.at[d], out_h.at[d], sems.at[d]) for d in range(3)]
    copies.append(pltpu.make_async_copy(pressure, pres_h, sems.at[3]))
    for copy in copies:
        copy.start()
    for copy in copies:
        copy.wait()


def on_device(n_stream, n_vert, base_flow, adjoint_velocity, reaction):
    nx, ny, nz = reaction.shape
    consts = constants(nx, ny, nz)
    field = (nx, ny, nz)
    operands = [base_flow, adjoint_velocity, reaction, *[jnp.asarray(c) for c in consts]]
    scratch = [
        pltpu.VMEM(base_flow.shape, F32),
        pltpu.VMEM(base_flow.shape, F32),
        pltpu.VMEM(field, F32),
        *[pltpu.VMEM(c.shape, c.dtype) for c in consts],
        pltpu.VMEM(field, F32),
        pltpu.VMEM((3, *field), F32),
        pltpu.VMEM((3, *field), F32),
        pltpu.VMEM((2, 1, *field), F32),
        pltpu.VMEM((3, *field), F32),
        pltpu.VMEM((4, *field), F32),
        pltpu.VMEM((3, *field), F32),
        pltpu.VMEM((6, *field), F32),
        pltpu.VMEM(field, F32),
        pltpu.VMEM((8, 128), F32),
        pltpu.VMEM((n_vert, 128), F32),
        pltpu.VMEM((n_stream, 128), F32),
        pltpu.SemaphoreType.DMA((11,)),
        pltpu.SemaphoreType.DMA((4,)),
        pltpu.SemaphoreType.DMA((5, 8)),
        pltpu.SemaphoreType.DMA((5, 8)),
        pltpu.SemaphoreType.DMA((2,)),
        pltpu.SemaphoreType.DMA((2,)),
    ]
    for count in FIELDS:
        scratch += [
            pltpu.VMEM((2, count, ny, nz), F32),
            pltpu.VMEM((2, count, nx, 8, nz), F32),
            pltpu.VMEM((2, count, ny, nz), F32),
        ]
    result, pressure = pl.pallas_call(
        functools.partial(kernel, n_stream, n_vert),
        out_shape=(
            pltpu.VMEM(base_flow.shape, F32),
            pltpu.VMEM(field, F32),
        ),
        in_specs=[pl.BlockSpec(memory_space=pl.ANY)] * 11,
        out_specs=(pl.BlockSpec(memory_space=pl.ANY), pl.BlockSpec(memory_space=pl.ANY)),
        scratch_shapes=scratch,
        compiler_params=pltpu.CompilerParams(
            collective_id=0, has_side_effects=True, vmem_limit_bytes=48 * 1024 * 1024
        ),
    )(*[pltpu.with_memory_space_constraint(a, pltpu.HBM) for a in operands])
    return pl.pallas_call(
        write_out,
        out_shape=(
            pltpu.HBM(base_flow.shape, F32),
            pltpu.HBM(field, F32),
        ),
        in_specs=[pl.BlockSpec(memory_space=pl.ANY)] * 2,
        out_specs=tuple([pl.BlockSpec(memory_space=pl.ANY)] * 2),
        scratch_shapes=[pltpu.SemaphoreType.DMA((4,))],
        compiler_params=pltpu.CompilerParams(vmem_limit_bytes=8 * 1024 * 1024),
    )(*[pltpu.with_memory_space_constraint(a, pltpu.VMEM) for a in (result, pressure)])


def solution(mesh):
    placed = (
        P(None, "stream", "vert", None),
        P(None, "stream", "vert", None),
        P("stream", "vert", None),
    )
    return jax.shard_map(
        functools.partial(on_device, mesh.shape["stream"], mesh.shape["vert"]),
        mesh=mesh,
        in_specs=placed,
        out_specs=(P(None, "stream", "vert", None), P("stream", "vert", None)),
        check_vma=False,
    )
```

```python
import functools

import jax
import jax.numpy as jnp
import ml_dtypes
import numpy as np
from jax import lax
from jax.experimental import pallas as pl
from jax.experimental.pallas import tpu as pltpu
from jax.sharding import PartitionSpec as P

time_step = 0.05
MESH = pl.DeviceIdType.MESH
F32 = jnp.float32
BF16 = jnp.bfloat16
SIDES = ((1, 0), (-1, 0), (0, 1), (0, -1), (1, 1), (1, -1), (-1, 1), (-1, -1))
FIELDS = (3, 1, 1, 1, 6, 3)
X_UP, X_DOWN, Y_UP, Y_DOWN, CORNERS, POINTS, STRIPS = 0, 16, 32, 48, 64, 80, 256


def gll_tables():
    degree = 7
    inner_nodes = np.array([0.8717401485096066, 0.5917001814331423, 0.2092992179024789])
    points_ref = np.concatenate([[-1.0], -inner_nodes, inner_nodes[::-1], [1.0]])
    previous = np.ones(8)
    current = points_ref.copy()
    for order_now in range(1, degree):
        following = ((2 * order_now + 1) * points_ref * current - order_now * previous) / (
            order_now + 1
        )
        previous = current
        current = following
    quadrature = 2.0 / (degree * (degree + 1) * current**2)
    derivative_table = np.zeros((8, 8))
    for i in range(8):
        for j in range(8):
            if i != j:
                derivative_table[i, j] = current[i] / (current[j] * (points_ref[i] - points_ref[j]))
    derivative_table[0, 0] = -degree * (degree + 1) / 4.0
    derivative_table[7, 7] = degree * (degree + 1) / 4.0
    return (derivative_table, quadrature)


def halves(matrix):
    high = matrix.astype(np.float32).astype(ml_dtypes.bfloat16)
    low = (matrix - high.astype(np.float64)).astype(ml_dtypes.bfloat16)
    return np.stack([high, low])


def constants(nx, ny, nz):
    table, quad = gll_tables()
    table = table.astype(np.float32).astype(np.float64)
    quad = quad.astype(np.float32).astype(np.float64)
    turned = table.T * quad[None, :] / quad[:, None]
    stiff = turned @ table
    eye = np.eye

    def along_x(m):
        return np.kron(np.kron(eye(nx // 8), m), eye(ny))

    def along_y(m):
        return np.kron(eye(nx * ny // 8), m)

    def along_z(m):
        return np.kron(eye(nz // 8), m.T)

    weights = (
        np.tile(quad, nx // 8)[:, None, None]
        * np.tile(quad, ny // 8)[None, :, None]
        * np.tile(quad, nz // 8)[None, None, :]
    ).astype(np.float32)
    twice = np.array([2.0, 1, 1, 1, 1, 1, 1, 2.0])
    mult = (
        np.tile(twice, nx // 8)[:, None, None]
        * np.tile(twice, ny // 8)[None, :, None]
        * np.tile(twice, nz // 8)[None, None, :]
    )
    ghost_rhs = ghost_matrices(turned)
    ghost_weights = np.zeros((POINTS, nz), np.float32)
    for top, face in ((X_UP, weights[0]), (X_DOWN, weights[-1]), (Y_UP, weights[:, 0]), (Y_DOWN, weights[:, -1])):
        ghost_weights[top:top + 16] = face
    ghost_weights[CORNERS:CORNERS + 4] = weights[0, 0]
    return [
        halves(np.concatenate([along_x(table), along_y(table)], axis=0)),
        halves(along_z(table)),
        halves(np.concatenate([along_x(turned), along_y(turned)], axis=1)),
        halves(along_z(turned)),
        halves(along_x(stiff) + along_y(stiff)),
        halves(along_z(stiff)),
        weights,
        (1.0 / mult).astype(np.float32),
        halves(np.concatenate([ghost_rhs[0], ghost_rhs[1]], axis=1)),
        halves(ghost_matrices(stiff).sum(axis=0)),
        ghost_weights,
        (time_step / (mult * weights)[:8, 0]).astype(np.float32),
    ]


def corner_row(sx, sy):
    return CORNERS + (0 if sx > 0 else 2) + (0 if sy > 0 else 1)


def strip_row(kind, sx, sy):
    if kind == "x":
        return POINTS + (0 if sx > 0 else 16) + (8 if sy > 0 else 0)
    if kind == "y":
        return POINTS + 32 + (0 if sy > 0 else 16) + (8 if sx > 0 else 0)
    return POINTS + 64 + 16 * (corner_row(sx, sy) - CORNERS) + (0 if kind == "cx" else 8)


def ghost_matrices(m):
    along = np.zeros((2, POINTS, STRIPS))
    blocks = np.kron(np.eye(2), m)
    for sign in (1, -1):
        node = 0 if sign > 0 else 7
        others = [j for j in range(8) if j != node]
        top_x, top_y = (X_UP, Y_UP) if sign > 0 else (X_DOWN, Y_DOWN)
        for r in range(16):
            along[0, top_x + r, top_x + r] += m[node, node]
            along[1, top_x + r, top_x:top_x + 16] += blocks[r]
            along[1, top_y + r, top_y + r] += m[node, node]
            along[0, top_y + r, top_y:top_y + 16] += blocks[r]
        for side in (1, -1):
            r = 15 if side > 0 else 0
            for j in others:
                along[0, top_x + r, strip_row("x", sign, side) + j] += m[node, j]
                along[1, top_y + r, strip_row("y", side, sign) + j] += m[node, j]
                along[0, corner_row(sign, side), strip_row("cx", sign, side) + j] += m[node, j]
                along[1, corner_row(side, sign), strip_row("cy", side, sign) + j] += m[node, j]
            along[0, corner_row(sign, side), corner_row(sign, side)] += m[node, node]
            along[1, corner_row(side, sign), corner_row(side, sign)] += m[node, node]
    return along


def split(value):
    high = value.astype(BF16)
    low = (value - high.astype(F32)).astype(BF16)
    return high, low


def dot(a, b):
    return jnp.dot(a, b, preferred_element_type=F32)


def left(matrix, parts):
    high, low = parts
    return dot(matrix[0], high) + dot(matrix[0], low) + dot(matrix[1], high)


def right(parts, matrix):
    high, low = parts
    return dot(high, matrix[0]) + dot(low, matrix[0]) + dot(high, matrix[1])


def kernel(
    n_stream,
    n_vert,
    base_h, adj_h, reac_h, kxy_h, kz_h, cxy_h, cz_h, bxy_h, bz_h, w_h, im_h,
    gc_h, gb_h, gw_h, sc_h,
    out_h, pres_h,
    base, adj, reac, kxy, kz, cxy, cz, bxy, bz, wts, imult, gc, gb, gw, sc,
    imass, conv, moved, loc, vec, grads, part3, outbuf, pbuf,
    own, strips, ghost_reac, extra, tiles, red_a, red_b,
    in_sem, out_sem, send_sem, recv_sem, strip_send, strip_recv, red_send, red_recv,
    *halo,
):
    me_s = lax.axis_index("stream")
    me_v = lax.axis_index("vert")
    nx, ny, nz = reac.shape
    rows = nx * ny

    inputs = [
        (kxy_h, kxy), (kz_h, kz), (adj_h, adj), (base_h, base), (w_h, wts), (im_h, imult),
        (cxy_h, cxy), (cz_h, cz), (reac_h, reac), (gc_h, gc), (sc_h, sc), (gw_h, gw),
        (bxy_h, bxy), (bz_h, bz), (gb_h, gb),
    ]
    loads = [pltpu.make_async_copy(a, b, in_sem.at[i]) for i, (a, b) in enumerate(inputs)]
    for load in loads:
        load.start()

    def near(ds, dv):
        return (lax.rem(me_s + ds + n_stream, n_stream), lax.rem(me_v + dv + n_vert, n_vert))

    strips[...] = jnp.zeros_like(strips)
    ghost_reac[...] = jnp.zeros_like(ghost_reac)

    barrier = pltpu.get_barrier_semaphore()
    partners = [near(ds, dv) for ds, dv in SIDES]
    partners += [near(0, k) for k in range(1, n_vert)]
    partners += [near(k, 0) for k in range(1, n_stream)]
    for partner in partners:
        pl.semaphore_signal(barrier, inc=1, device_id=partner, device_id_type=MESH)

    has_xl = me_s > 0
    has_xh = me_s < n_stream - 1
    has_yl = me_v > 0
    has_yh = me_v < n_vert - 1

    def exists(ds, dv):
        conditions = []
        if ds:
            conditions.append(has_xh if ds > 0 else has_xl)
        if dv:
            conditions.append(has_yh if dv > 0 else has_yl)
        return functools.reduce(jnp.logical_and, conditions)

    def flat(ref):
        return ref[...].reshape(rows, nz)

    lane = lax.broadcasted_iota(jnp.int32, (ny, nz), 1) % 8
    sub = lax.broadcasted_iota(jnp.int32, (8, nz), 0)
    row = lax.broadcasted_iota(jnp.int32, (ny, nz), 0)

    def fold_store(value, ref):
        for i in range(nx):
            v = value[i * ny:(i + 1) * ny]
            up = pltpu.roll(v, nz - 1, 1)
            down = pltpu.roll(v, 1, 1)
            ref[i] = v + jnp.where(lane == 7, up, 0.0) + jnp.where(lane == 0, down, 0.0)
        both = ref[7] + ref[8]
        ref[7] = both
        ref[8] = both
        both = ref[:, 7:8, :] + ref[:, 8:9, :]
        ref[:, 7:8, :] = both
        ref[:, 8:9, :] = both

    def copies(e, src):
        xs, ys, cs = halo[3 * e:3 * e + 3]
        made = []
        for n, (ds, dv) in enumerate(SIDES):
            if dv == 0:
                a = src.at[:, nx - 1 if ds > 0 else 0]
                b = xs.at[0 if ds > 0 else 1]
            else:
                at = pl.ds(ny - 1 if dv > 0 else 0, 1)
                if ds == 0:
                    a = src.at[:, :, at, :]
                    b = ys.at[0 if dv > 0 else 1].at[:, :, pl.ds(0 if dv > 0 else 7, 1), :]
                else:
                    a = src.at[:, nx - 1 if ds > 0 else 0, at, :]
                    b = cs.at[0 if ds > 0 else 1].at[:, pl.ds(0 if dv > 0 else ny - 1, 1), :]
            made.append(
                pltpu.make_async_remote_copy(
                    src_ref=a, dst_ref=b,
                    send_sem=send_sem.at[e, n], recv_sem=recv_sem.at[e, n],
                    device_id=near(ds, dv), device_id_type=MESH,
                )
            )
        for copy, (ds, dv) in zip(made, SIDES):
            pl.when(exists(ds, dv))(copy.start)
        return [[copy] for copy in made]

    def strip_copies(pair, field_x, field_y, along_x, along_y):
        made = []
        count = 0
        for ds, dv in SIDES:
            mine = []
            here_x, here_y = (nx - 1 if ds > 0 else 0), (ny - 1 if dv > 0 else 0)
            part_x, part_y = pl.ds(nx - 8 if ds > 0 else 0, 8), pl.ds(ny - 8 if dv > 0 else 0, 8)
            if dv == 0:
                for sy in (1, -1):
                    mine.append((field_x.at[part_x, ny - 1 if sy > 0 else 0, :], along_x, strip_row("cx", -ds, sy)))
            elif ds == 0:
                for sx in (1, -1):
                    mine.append((field_y.at[nx - 1 if sx > 0 else 0, part_y, :], along_y, strip_row("cy", sx, -dv)))
            else:
                mine.append((field_x.at[part_x, here_y, :], along_x, strip_row("x", -ds, -dv)))
                mine.append((field_y.at[here_x, part_y, :], along_y, strip_row("y", -ds, -dv)))
            group = []
            for src, which, at in mine:
                group.append(
                    pltpu.make_async_remote_copy(
                        src_ref=src, dst_ref=strips.at[which, pl.ds(at, 8), :],
                        send_sem=strip_send.at[pair, count], recv_sem=strip_recv.at[pair, count],
                        device_id=near(ds, dv), device_id_type=MESH,
                    )
                )
                count += 1
            made.append(group)
        return launch(made)

    def reaction_copies():
        made = []
        for n, (ds, dv) in enumerate(SIDES):
            here_x, here_y = (nx - 1 if ds > 0 else 0), (ny - 1 if dv > 0 else 0)
            if dv == 0:
                src, at, size = reac.at[here_x], (X_UP if ds < 0 else X_DOWN), 16
            elif ds == 0:
                src, at, size = reac.at[:, here_y, :], (Y_UP if dv < 0 else Y_DOWN), 16
            else:
                src, at, size = reac.at[here_x, pl.ds(here_y, 1), :], corner_row(-ds, -dv), 1
            made.append([
                pltpu.make_async_remote_copy(
                    src_ref=src, dst_ref=ghost_reac.at[pl.ds(at, size), :],
                    send_sem=send_sem.at[6, n], recv_sem=recv_sem.at[6, n],
                    device_id=near(ds, dv), device_id_type=MESH,
                )
            ])
        return launch(made)

    def launch(made):
        for group, (ds, dv) in zip(made, SIDES):
            @pl.when(exists(ds, dv))
            def _(group=group):
                for copy in group:
                    copy.start()
        return made

    def arrive(made):
        for group, (ds, dv) in zip(made, SIDES):
            @pl.when(exists(-ds, -dv))
            def _(group=group):
                for copy in group:
                    copy.wait_recv()

    def leave(made):
        for group, (ds, dv) in zip(made, SIDES):
            @pl.when(exists(ds, dv))
            def _(group=group):
                for copy in group:
                    copy.wait_send()

    def with_halo(e, f, src, i, more=False):
        xs, ys, cs = halo[3 * e:3 * e + 3]
        low, high = ys[0, f, i], ys[1, f, i]
        if more:
            low = low + extra[Y_DOWN + i:Y_DOWN + i + 1]
            high = high + extra[Y_UP + i:Y_UP + i + 1]
        low = src[f, i, 0:8, :] + jnp.where((sub == 0) & has_yl, low, 0.0)
        high = src[f, i, ny - 8:ny, :] + jnp.where((sub == 7) & has_yh, high, 0.0)
        value = jnp.concatenate([low, high], axis=0)
        if i in (0, nx - 1):
            side = 0 if i == 0 else 1
            sx = -1 if i == 0 else 1
            there = has_xl if i == 0 else has_xh
            known = ((row == 0) & has_yl) | ((row == ny - 1) & has_yh)
            face, corner = xs[side, f], cs[side, f]
            if more:
                top = X_UP if sx > 0 else X_DOWN
                face = face + extra[top:top + 16]
                below, above = corner_row(sx, -1), corner_row(sx, 1)
                corner = corner + jnp.where(row == 0, extra[below:below + 1], extra[above:above + 1])
            value = value + jnp.where(there, face + jnp.where(known, corner, 0.0), 0.0)
        return value

    def ghost_points(e, f, value, i, which, scale=None):
        xs, ys, cs = halo[3 * e:3 * e + 3]

        def put(at, size, mine, theirs, weight, there):
            rest = mine - theirs
            if scale is not None:
                rest = rest * weight
            strips[which, at:at + size, :] = jnp.where(there, rest, 0.0)

        by = [None] * 3 if scale is None else [scale, scale[0:1], scale[ny - 1:ny]]
        put(Y_DOWN + i, 1, value[0:1], ys[0, f, i, 0:1, :], by[1], has_yl)
        put(Y_UP + i, 1, value[ny - 1:ny], ys[1, f, i, 7:8, :], by[2], has_yh)
        if i in (0, nx - 1):
            side = 0 if i == 0 else 1
            sx = -1 if i == 0 else 1
            there = has_xl if i == 0 else has_xh
            put(X_UP if sx > 0 else X_DOWN, 16, value, xs[side, f], by[0], there)
            put(corner_row(sx, -1), 1, value[0:1], cs[side, f, 0:1, :], by[1], there & has_yl)
            put(corner_row(sx, 1), 1, value[ny - 1:ny], cs[side, f, ny - 1:ny, :], by[2], there & has_yh)

    lane_p = lax.broadcasted_iota(jnp.int32, (POINTS, nz), 1) % 8
    row_p = lax.broadcasted_iota(jnp.int32, (POINTS, nz), 0)

    def fold_points(value):
        up = pltpu.roll(value, nz - 1, 1)
        down = pltpu.roll(value, 1, 1)
        value = value + jnp.where(lane_p == 7, up, 0.0) + jnp.where(lane_p == 0, down, 0.0)
        up = pltpu.roll(value, POINTS - 1, 0)
        down = pltpu.roll(value, 1, 0)
        on_face = row_p < CORNERS
        extra[...] = (
            value
            + jnp.where(on_face & (row_p % 16 == 7), up, 0.0)
            + jnp.where(on_face & (row_p % 16 == 8), down, 0.0)
        )

    def operate(value, parts):
        return wts[...].reshape(rows, nz) * (
            left(bxy, parts) + right(parts, bz) + flat(reac) * value
        )

    def gradient(parts, k, dst, at):
        w = wts[...].reshape(rows, nz)
        both = left(kxy, parts)
        fold_store(w * both[:rows], dst.at[at])
        fold_store(w * both[rows:], dst.at[at + 1])
        fold_store(w * right(parts, kz), dst.at[at + 2])

    def to_row(value, slot):
        s = value.reshape(rows // 8, 8, nz).sum(axis=0)
        s = s[:, :128] + s[:, 128:]
        tiles[slot:slot + 1, :] = jnp.sum(s, axis=0, keepdims=True)

    for i in range(4):
        loads[i].wait()
    for c in range(3):
        parts = split(flat(adj.at[c]))
        both = left(kxy, parts)
        conv[c] = (
            flat(base.at[0]) * both[:rows] + flat(base.at[1]) * both[rows:]
            + flat(base.at[2]) * right(parts, kz)
        ).reshape(nx, ny, nz)
    for j in range(3):
        parts = split(flat(base.at[j]))
        a = flat(adj.at[j])
        both = left(kxy, parts)
        conv[0] -= (a * both[:rows]).reshape(nx, ny, nz)
        conv[1] -= (a * both[rows:]).reshape(nx, ny, nz)
        conv[2] -= (a * right(parts, kz)).reshape(nx, ny, nz)
    loads[4].wait()
    loads[5].wait()
    for i in range(nx):
        value = imult[i]
        edge = ((row == 0) & (me_v == 0)) | ((row == ny - 1) & (me_v == n_vert - 1))
        value = value * jnp.where(edge, 2.0, 1.0)
        if i in (0, nx - 1):
            value = value * jnp.where((me_s == 0) if i == 0 else (me_s == n_stream - 1), 2.0, 1.0)
        imult[i] = value
        imass[i] = time_step * value / wts[i]
    for c in range(3):
        fold_store(flat(conv.at[c]) * flat(wts), part3.at[c])
    pl.semaphore_wait(barrier, len(partners))
    sends = [copies(0, part3), strip_copies(0, part3.at[0], part3.at[1], 0, 1)]

    def right_side(fields):
        pair = jnp.concatenate([fields[0], fields[1]], axis=0)
        return flat(wts) * (left(cxy, split(pair)) + right(split(fields[2]), cz))

    for i in range(6, len(loads)):
        loads[i].wait()
    fold_store(
        right_side([flat(adj.at[c]) + flat(imass) * flat(part3.at[c]) for c in range(3)]),
        loc.at[0].at[0],
    )
    sends += [copies(1, loc.at[0]), reaction_copies()]

    arrive(sends[0])
    for c in range(3):
        for i in range(nx):
            value = with_halo(0, c, part3, i)
            moved[c, i] = adj[c, i] + value * imass[i]
            ghost_points(0, c, value, i, c, imass[i])
    fold_store(right_side([flat(moved.at[c]) for c in range(3)]), own.at[0])
    arrive(sends[1])
    for c in (0, 1):
        for at in range(POINTS, 208, 8):
            strips[c, at:at + 8, :] = strips[c, at:at + 8, :] * sc[...]
    ghosts = jnp.concatenate([strips[0], strips[1]], axis=0)
    fold_points(gw[...] * (left(gc, split(ghosts)) + right(split(strips[2, 0:POINTS, :]), cz)))
    arrive(sends[2])
    for i in range(nx):
        vec[0, i] = with_halo(1, 0, own, i, True)

    v = flat(vec.at[0])
    parts = split(v)
    image = operate(v, parts)
    fold_store(image, loc.at[1].at[0])
    sends += [copies(2, loc.at[1]), strip_copies(1, loc.at[1].at[0], loc.at[1].at[0], 3, 3)]
    first = flat(loc.at[1].at[0])
    fold_store(operate(first, split(first)), loc.at[2].at[0])
    sends.append(copies(3, loc.at[2]))
    to_row(v * v * flat(imult), 0)
    to_row(v * image, 1)
    gradient(parts, 0, grads, 0)
    sends.append(copies(5, grads))
    arrive(sends[3])
    arrive(sends[4])
    for i in range(nx):
        value = with_halo(2, 0, loc.at[1], i)
        vec[1, i] = value
        ghost_points(2, 0, value, i, 3)

    v = flat(vec.at[1])
    parts = split(v)
    image = operate(v, parts)
    fold_store(image, own.at[0])
    arrive(sends[5])
    points = strips[3, 0:POINTS, :]
    fold_points(
        gw[...] * (left(gb, split(strips[3])) + right(split(points), bz) + ghost_reac[...] * points)
    )
    to_row(v * v * flat(imult), 2)
    to_row(v * image, 3)
    arrive(sends[6])
    for i in range(nx):
        vec[2, i] = with_halo(3, 0, own, i, True)
    gradient(parts, 1, outbuf, 0)

    v = flat(vec.at[2])
    parts = split(v)
    image = operate(v, parts)
    to_row(v * v * flat(imult), 4)
    to_row(v * image, 5)

    tiles[6:8, :] = jnp.zeros((2, 128), F32)
    group = lax.broadcasted_iota(jnp.int32, (8, 128), 1) // 16
    packed = tiles[...]
    for shift in (64, 32, 16):
        packed = packed + pltpu.roll(packed, shift, 1)
    packed = jnp.where(group == lax.broadcasted_iota(jnp.int32, (8, 128), 0), packed, 0.0)
    red_a[n_vert - 1:n_vert, :] = jnp.sum(packed, axis=0, keepdims=True)

    def spread(slots, n, which):
        for k in range(1, n):
            pltpu.make_async_remote_copy(
                src_ref=slots.at[pl.ds(n - 1, 1)], dst_ref=slots.at[pl.ds(k - 1, 1)],
                send_sem=red_send.at[which], recv_sem=red_recv.at[which],
                device_id=near(0, k) if which == 0 else near(k, 0), device_id_type=MESH,
            ).start()

    def whole(slots, n, which):
        return pltpu.make_async_remote_copy(
            src_ref=slots.at[pl.ds(0, n - 1)], dst_ref=slots.at[pl.ds(0, n - 1)],
            send_sem=red_send.at[which], recv_sem=red_recv.at[which],
            device_id=near(0, 1), device_id_type=MESH,
        )

    spread(red_a, n_vert, 0)
    gradient(parts, 2, outbuf, 3)
    sends.append(copies(4, outbuf))
    whole(red_a, n_vert, 0).wait_recv()
    red_b[n_stream - 1:n_stream, :] = jnp.sum(red_a[...], axis=0, keepdims=True)
    spread(red_b, n_stream, 1)

    arrive(sends[7])
    for d in range(3):
        for i in range(nx):
            conv[d, i] = with_halo(5, d, grads, i) * imass[i]
    arrive(sends[8])
    for d in range(3):
        for i in range(nx):
            base[d, i] = with_halo(4, d, outbuf, i) * imass[i]
            adj[d, i] = with_halo(4, 3 + d, outbuf, i) * imass[i]

    whole(red_b, n_stream, 1).wait_recv()
    total = jnp.sum(red_b[...], axis=0, keepdims=True)
    m = [jnp.sum(jnp.where(group[0:1] == k, total, 0.0), axis=1, keepdims=True) for k in range(6)]
    a0 = m[0] / m[1]
    r1 = a0 * a0 * m[2] - m[0]
    k1 = 1.0 + r1 / m[0]
    p1 = k1 * k1 * m[1] - 2.0 * k1 * a0 * m[2] + a0 * a0 * m[3]
    a1 = r1 / p1
    e1 = -(a0 + a1 * k1)
    e2 = a1 * a0
    r2 = m[0] + 2.0 * e1 * m[1] + (e1 * e1 + 2.0 * e2) * m[2] + 2.0 * e1 * e2 * m[3] + e2 * e2 * m[4]
    b2 = r2 / r1
    f0 = 1.0 + b2 * k1
    f1 = e1 - b2 * a0
    f2 = e2
    p2 = (
        f0 * f0 * m[1] + 2.0 * f0 * f1 * m[2] + (f1 * f1 + 2.0 * f0 * f2) * m[3]
        + 2.0 * f1 * f2 * m[4] + f2 * f2 * m[5]
    )
    a2 = r2 / p2
    c0 = a0 + a1 * k1 + a2 * f0
    c1 = a2 * f1 - a1 * a0
    c2 = a2 * f2
    d0, d1, d2 = [c * (1.0 / time_step) for c in (c0, c1, c2)]

    outs = []
    for i in range(nx):
        pbuf[i] = c0 * vec[0, i] + c1 * vec[1, i] + c2 * vec[2, i]
    outs.append(pltpu.make_async_copy(pbuf, pres_h, out_sem.at[3]))
    outs[-1].start()
    for d in range(3):
        for i in range(nx):
            moved[d, i] = moved[d, i] - (d0 * conv[d, i] + d1 * base[d, i] + d2 * adj[d, i])
        outs.append(pltpu.make_async_copy(moved.at[d], out_h.at[d], out_sem.at[d]))
        outs[-1].start()
    for made in sends:
        leave(made)
    whole(red_a, n_vert, 0).wait_send()
    whole(red_b, n_stream, 1).wait_send()
    for copy in outs:
        copy.wait()


def write_out(result, pressure, out_h, pres_h, sems):
    copies = [pltpu.make_async_copy(result.at[d], out_h.at[d], sems.at[d]) for d in range(3)]
    copies.append(pltpu.make_async_copy(pressure, pres_h, sems.at[3]))
    for copy in copies:
        copy.start()
    for copy in copies:
        copy.wait()


def on_device(n_stream, n_vert, base_flow, adjoint_velocity, reaction):
    nx, ny, nz = reaction.shape
    consts = constants(nx, ny, nz)
    field = (nx, ny, nz)
    operands = [base_flow, adjoint_velocity, reaction, *[jnp.asarray(c) for c in consts]]
    scratch = [
        pltpu.VMEM(base_flow.shape, F32),
        pltpu.VMEM(base_flow.shape, F32),
        pltpu.VMEM(field, F32),
        *[pltpu.VMEM(c.shape, c.dtype) for c in consts],
        pltpu.VMEM(field, F32),
        pltpu.VMEM((3, *field), F32),
        pltpu.VMEM((3, *field), F32),
        pltpu.VMEM((3, 1, *field), F32),
        pltpu.VMEM((3, *field), F32),
        pltpu.VMEM((3, *field), F32),
        pltpu.VMEM((3, *field), F32),
        pltpu.VMEM((6, *field), F32),
        pltpu.VMEM(field, F32),
        pltpu.VMEM((1, *field), F32),
        pltpu.VMEM((4, STRIPS, nz), F32),
        pltpu.VMEM((POINTS, nz), F32),
        pltpu.VMEM((POINTS, nz), F32),
        pltpu.VMEM((8, 128), F32),
        pltpu.VMEM((n_vert, 128), F32),
        pltpu.VMEM((n_stream, 128), F32),
        pltpu.SemaphoreType.DMA((3 + len(consts),)),
        pltpu.SemaphoreType.DMA((4,)),
        pltpu.SemaphoreType.DMA((7, 8)),
        pltpu.SemaphoreType.DMA((7, 8)),
        pltpu.SemaphoreType.DMA((2, 16)),
        pltpu.SemaphoreType.DMA((2, 16)),
        pltpu.SemaphoreType.DMA((2,)),
        pltpu.SemaphoreType.DMA((2,)),
    ]
    for count in FIELDS:
        scratch += [
            pltpu.VMEM((2, count, ny, nz), F32),
            pltpu.VMEM((2, count, nx, 8, nz), F32),
            pltpu.VMEM((2, count, ny, nz), F32),
        ]
    result, pressure = pl.pallas_call(
        functools.partial(kernel, n_stream, n_vert),
        out_shape=(
            pltpu.VMEM(base_flow.shape, F32),
            pltpu.VMEM(field, F32),
        ),
        in_specs=[pl.BlockSpec(memory_space=pl.ANY)] * len(operands),
        out_specs=(pl.BlockSpec(memory_space=pl.ANY), pl.BlockSpec(memory_space=pl.ANY)),
        scratch_shapes=scratch,
        compiler_params=pltpu.CompilerParams(
            collective_id=0, has_side_effects=True, vmem_limit_bytes=48 * 1024 * 1024
        ),
    )(*[pltpu.with_memory_space_constraint(a, pltpu.HBM) for a in operands])
    return pl.pallas_call(
        write_out,
        out_shape=(
            pltpu.HBM(base_flow.shape, F32),
            pltpu.HBM(field, F32),
        ),
        in_specs=[pl.BlockSpec(memory_space=pl.ANY)] * 2,
        out_specs=tuple([pl.BlockSpec(memory_space=pl.ANY)] * 2),
        scratch_shapes=[pltpu.SemaphoreType.DMA((4,))],
        compiler_params=pltpu.CompilerParams(vmem_limit_bytes=8 * 1024 * 1024),
    )(*[pltpu.with_memory_space_constraint(a, pltpu.VMEM) for a in (result, pressure)])


def solution(mesh):
    placed = (
        P(None, "stream", "vert", None),
        P(None, "stream", "vert", None),
        P("stream", "vert", None),
    )
    return jax.shard_map(
        functools.partial(on_device, mesh.shape["stream"], mesh.shape["vert"]),
        mesh=mesh,
        in_specs=placed,
        out_specs=(P(None, "stream", "vert", None), P("stream", "vert", None)),
        check_vma=False,
    )
```

```python
import functools

import jax
import jax.numpy as jnp
import ml_dtypes
import numpy as np
from jax import lax
from jax.experimental import pallas as pl
from jax.experimental.pallas import tpu as pltpu
from jax.sharding import PartitionSpec as P

time_step = 0.05
MESH = pl.DeviceIdType.MESH
F32 = jnp.float32
BF16 = jnp.bfloat16
SIDES = ((1, 0), (-1, 0), (0, 1), (0, -1), (1, 1), (1, -1), (-1, 1), (-1, -1))
FIELDS = (3, 1, 1, 1, 2, 1)
X_UP, X_DOWN, Y_UP, Y_DOWN, CORNERS, POINTS, STRIPS = 0, 16, 32, 48, 64, 80, 256


def gll_tables():
    degree = 7
    inner_nodes = np.array([0.8717401485096066, 0.5917001814331423, 0.2092992179024789])
    points_ref = np.concatenate([[-1.0], -inner_nodes, inner_nodes[::-1], [1.0]])
    previous = np.ones(8)
    current = points_ref.copy()
    for order_now in range(1, degree):
        following = ((2 * order_now + 1) * points_ref * current - order_now * previous) / (
            order_now + 1
        )
        previous = current
        current = following
    quadrature = 2.0 / (degree * (degree + 1) * current**2)
    derivative_table = np.zeros((8, 8))
    for i in range(8):
        for j in range(8):
            if i != j:
                derivative_table[i, j] = current[i] / (current[j] * (points_ref[i] - points_ref[j]))
    derivative_table[0, 0] = -degree * (degree + 1) / 4.0
    derivative_table[7, 7] = degree * (degree + 1) / 4.0
    return (derivative_table, quadrature)


def halves(matrix):
    high = matrix.astype(np.float32).astype(ml_dtypes.bfloat16)
    low = (matrix - high.astype(np.float64)).astype(ml_dtypes.bfloat16)
    return np.stack([high, low])


def constants(nx, ny, nz):
    table, quad = gll_tables()
    table = table.astype(np.float32).astype(np.float64)
    quad = quad.astype(np.float32).astype(np.float64)
    turned = table.T * quad[None, :] / quad[:, None]
    stiff = turned @ table
    eye = np.eye

    def along_x(m):
        return np.kron(np.kron(eye(nx // 8), m), eye(ny))

    def along_y(m):
        return np.kron(eye(nx * ny // 8), m)

    def along_z(m):
        return np.kron(eye(nz // 8), m.T)

    weights = (
        np.tile(quad, nx // 8)[:, None, None]
        * np.tile(quad, ny // 8)[None, :, None]
        * np.tile(quad, nz // 8)[None, None, :]
    ).astype(np.float32)
    twice = np.array([2.0, 1, 1, 1, 1, 1, 1, 2.0])
    mult = (
        np.tile(twice, nx // 8)[:, None, None]
        * np.tile(twice, ny // 8)[None, :, None]
        * np.tile(twice, nz // 8)[None, None, :]
    )
    ghost_rhs = ghost_matrices(turned)
    ghost_weights = np.zeros((POINTS, nz), np.float32)
    for top, face in ((X_UP, weights[0]), (X_DOWN, weights[-1]), (Y_UP, weights[:, 0]), (Y_DOWN, weights[:, -1])):
        ghost_weights[top:top + 16] = face
    ghost_weights[CORNERS:CORNERS + 4] = weights[0, 0]
    first = np.zeros((nx, nz))
    for r in range(nx):
        first[r] = np.tile(np.repeat(table[r % 8], ny), nx // 8) * (np.arange(nz) // 128 == r // 8)
    across = np.tile(quad[:, None] * quad[None, :], (1, nz // 8))
    return [
        np.concatenate(
            [np.tile(table.T, (1, nz // 8)), np.tile(table, (1, nz // 8)), first, across, 1.0 / mult[1, :8]]
        ).astype(np.float32),
        halves(np.concatenate([along_x(turned), along_y(turned)], axis=1)),
        halves(along_z(turned)),
        halves(along_x(stiff) + along_y(stiff)),
        halves(along_z(stiff)),
        halves(np.concatenate([ghost_rhs[0], ghost_rhs[1]], axis=1)),
        halves(ghost_matrices(stiff).sum(axis=0)),
        ghost_weights,
        (time_step / (mult * weights)[:8, 0]).astype(np.float32),
    ]


def corner_row(sx, sy):
    return CORNERS + (0 if sx > 0 else 2) + (0 if sy > 0 else 1)


def strip_row(kind, sx, sy):
    if kind == "x":
        return POINTS + (0 if sx > 0 else 16) + (8 if sy > 0 else 0)
    if kind == "y":
        return POINTS + 32 + (0 if sy > 0 else 16) + (8 if sx > 0 else 0)
    return POINTS + 64 + 16 * (corner_row(sx, sy) - CORNERS) + (0 if kind == "cx" else 8)


def ghost_matrices(m):
    along = np.zeros((2, POINTS, STRIPS))
    blocks = np.kron(np.eye(2), m)
    for sign in (1, -1):
        node = 0 if sign > 0 else 7
        others = [j for j in range(8) if j != node]
        top_x, top_y = (X_UP, Y_UP) if sign > 0 else (X_DOWN, Y_DOWN)
        for r in range(16):
            along[0, top_x + r, top_x + r] += m[node, node]
            along[1, top_x + r, top_x:top_x + 16] += blocks[r]
            along[1, top_y + r, top_y + r] += m[node, node]
            along[0, top_y + r, top_y:top_y + 16] += blocks[r]
        for side in (1, -1):
            r = 15 if side > 0 else 0
            for j in others:
                along[0, top_x + r, strip_row("x", sign, side) + j] += m[node, j]
                along[1, top_y + r, strip_row("y", side, sign) + j] += m[node, j]
                along[0, corner_row(sign, side), strip_row("cx", sign, side) + j] += m[node, j]
                along[1, corner_row(side, sign), strip_row("cy", side, sign) + j] += m[node, j]
            along[0, corner_row(sign, side), corner_row(sign, side)] += m[node, node]
            along[1, corner_row(side, sign), corner_row(side, sign)] += m[node, node]
    return along


def split(value):
    high = value.astype(BF16)
    low = (value - high.astype(F32)).astype(BF16)
    return high, low


def dot(a, b):
    return jnp.dot(a, b, preferred_element_type=F32)


def left(matrix, parts):
    high, low = parts
    return dot(matrix[0], high) + dot(matrix[0], low) + dot(matrix[1], high)


def right(parts, matrix):
    high, low = parts
    return dot(high, matrix[0]) + dot(low, matrix[0]) + dot(high, matrix[1])


def kernel(
    n_stream,
    n_vert,
    base_h, adj_h, reac_h, tab_h, cxy_h, cz_h, bxy_h, bz_h,
    gc_h, gb_h, gw_h, sc_h,
    moved, asm, vec, coef,
    base, adj, reac, tab, cxy, cz, bxy, bz, gc, gb, gw, sc, kxy, kz, wts, imult,
    imass, conv, loc, raw, part3,
    own, strips, ghost_reac, extra, tiles, red_a, red_b,
    in_sem, send_sem, recv_sem, strip_send, strip_recv, red_send, red_recv,
    *halo,
):
    me_s = lax.axis_index("stream")
    me_v = lax.axis_index("vert")
    nx, ny, nz = reac.shape
    rows = nx * ny

    inputs = [
        (tab_h, tab), (adj_h, adj), (base_h, base),
        (cxy_h, cxy), (cz_h, cz), (reac_h, reac), (gc_h, gc), (sc_h, sc), (gw_h, gw),
        (bxy_h, bxy), (bz_h, bz), (gb_h, gb),
    ]
    loads = [pltpu.make_async_copy(a, b, in_sem.at[i]) for i, (a, b) in enumerate(inputs)]
    for load in loads[:3]:
        load.start()

    def near(ds, dv):
        return (lax.rem(me_s + ds + n_stream, n_stream), lax.rem(me_v + dv + n_vert, n_vert))

    strips[...] = jnp.zeros_like(strips)
    ghost_reac[...] = jnp.zeros_like(ghost_reac)

    barrier = pltpu.get_barrier_semaphore()
    partners = [near(ds, dv) for ds, dv in SIDES]
    partners += [near(0, k) for k in range(1, n_vert)]
    partners += [near(k, 0) for k in range(1, n_stream)]
    for partner in partners:
        pl.semaphore_signal(barrier, inc=1, device_id=partner, device_id_type=MESH)

    has_xl = me_s > 0
    has_xh = me_s < n_stream - 1
    has_yl = me_v > 0
    has_yh = me_v < n_vert - 1

    def exists(ds, dv):
        conditions = []
        if ds:
            conditions.append(has_xh if ds > 0 else has_xl)
        if dv:
            conditions.append(has_yh if dv > 0 else has_yl)
        return functools.reduce(jnp.logical_and, conditions)

    def flat(ref):
        return ref[...].reshape(rows, nz)

    lane = lax.broadcasted_iota(jnp.int32, (ny, nz), 1) % 8
    sub = lax.broadcasted_iota(jnp.int32, (8, nz), 0)
    row = lax.broadcasted_iota(jnp.int32, (ny, nz), 0)

    def fold_store(value, ref):
        for i in range(nx):
            v = value[i * ny:(i + 1) * ny]
            up = pltpu.roll(v, nz - 1, 1)
            down = pltpu.roll(v, 1, 1)
            ref[i] = v + jnp.where(lane == 7, up, 0.0) + jnp.where(lane == 0, down, 0.0)
        both = ref[7] + ref[8]
        ref[7] = both
        ref[8] = both
        both = ref[:, 7:8, :] + ref[:, 8:9, :]
        ref[:, 7:8, :] = both
        ref[:, 8:9, :] = both

    def copies(e, src):
        xs, ys, cs = halo[3 * e:3 * e + 3]
        made = []
        for n, (ds, dv) in enumerate(SIDES):
            if dv == 0:
                a = src.at[:, nx - 1 if ds > 0 else 0]
                b = xs.at[0 if ds > 0 else 1]
            else:
                at = pl.ds(ny - 1 if dv > 0 else 0, 1)
                if ds == 0:
                    a = src.at[:, :, at, :]
                    b = ys.at[0 if dv > 0 else 1].at[:, :, pl.ds(0 if dv > 0 else 7, 1), :]
                else:
                    a = src.at[:, nx - 1 if ds > 0 else 0, at, :]
                    b = cs.at[0 if ds > 0 else 1].at[:, pl.ds(0 if dv > 0 else ny - 1, 1), :]
            made.append(
                pltpu.make_async_remote_copy(
                    src_ref=a, dst_ref=b,
                    send_sem=send_sem.at[e, n], recv_sem=recv_sem.at[e, n],
                    device_id=near(ds, dv), device_id_type=MESH,
                )
            )
        for copy, (ds, dv) in zip(made, SIDES):
            pl.when(exists(ds, dv))(copy.start)
        return [[copy] for copy in made]

    def strip_copies(pair, field_x, field_y, along_x, along_y):
        made = []
        count = 0
        for ds, dv in SIDES:
            mine = []
            here_x, here_y = (nx - 1 if ds > 0 else 0), (ny - 1 if dv > 0 else 0)
            part_x, part_y = pl.ds(nx - 8 if ds > 0 else 0, 8), pl.ds(ny - 8 if dv > 0 else 0, 8)
            if dv == 0:
                for sy in (1, -1):
                    mine.append((field_x.at[part_x, ny - 1 if sy > 0 else 0, :], along_x, strip_row("cx", -ds, sy)))
            elif ds == 0:
                for sx in (1, -1):
                    mine.append((field_y.at[nx - 1 if sx > 0 else 0, part_y, :], along_y, strip_row("cy", sx, -dv)))
            else:
                mine.append((field_x.at[part_x, here_y, :], along_x, strip_row("x", -ds, -dv)))
                mine.append((field_y.at[here_x, part_y, :], along_y, strip_row("y", -ds, -dv)))
            group = []
            for src, which, at in mine:
                group.append(
                    pltpu.make_async_remote_copy(
                        src_ref=src, dst_ref=strips.at[which, pl.ds(at, 8), :],
                        send_sem=strip_send.at[pair, count], recv_sem=strip_recv.at[pair, count],
                        device_id=near(ds, dv), device_id_type=MESH,
                    )
                )
                count += 1
            made.append(group)
        return launch(made)

    def reaction_copies():
        made = []
        for n, (ds, dv) in enumerate(SIDES):
            here_x, here_y = (nx - 1 if ds > 0 else 0), (ny - 1 if dv > 0 else 0)
            if dv == 0:
                src, at, size = reac.at[here_x], (X_UP if ds < 0 else X_DOWN), 16
            elif ds == 0:
                src, at, size = reac.at[:, here_y, :], (Y_UP if dv < 0 else Y_DOWN), 16
            else:
                src, at, size = reac.at[here_x, pl.ds(here_y, 1), :], corner_row(-ds, -dv), 1
            made.append([
                pltpu.make_async_remote_copy(
                    src_ref=src, dst_ref=ghost_reac.at[pl.ds(at, size), :],
                    send_sem=send_sem.at[6, n], recv_sem=recv_sem.at[6, n],
                    device_id=near(ds, dv), device_id_type=MESH,
                )
            ])
        return launch(made)

    def launch(made):
        for group, (ds, dv) in zip(made, SIDES):
            @pl.when(bool(group) and exists(ds, dv))
            def _(group=group):
                for copy in group:
                    copy.start()
        return made

    def arrive(made):
        for group, (ds, dv) in zip(made, SIDES):
            @pl.when(bool(group) and exists(-ds, -dv))
            def _(group=group):
                for copy in group:
                    copy.wait_recv()

    def leave(made):
        for group, (ds, dv) in zip(made, SIDES):
            @pl.when(bool(group) and exists(ds, dv))
            def _(group=group):
                for copy in group:
                    copy.wait_send()

    def with_halo(e, f, src, i, more=False):
        xs, ys, cs = halo[3 * e:3 * e + 3]
        low, high = ys[0, f, i], ys[1, f, i]
        if more:
            low = low + extra[Y_DOWN + i:Y_DOWN + i + 1]
            high = high + extra[Y_UP + i:Y_UP + i + 1]
        low = src[f, i, 0:8, :] + jnp.where((sub == 0) & has_yl, low, 0.0)
        high = src[f, i, ny - 8:ny, :] + jnp.where((sub == 7) & has_yh, high, 0.0)
        value = jnp.concatenate([low, high], axis=0)
        if i in (0, nx - 1):
            side = 0 if i == 0 else 1
            sx = -1 if i == 0 else 1
            there = has_xl if i == 0 else has_xh
            known = ((row == 0) & has_yl) | ((row == ny - 1) & has_yh)
            face, corner = xs[side, f], cs[side, f]
            if more:
                top = X_UP if sx > 0 else X_DOWN
                face = face + extra[top:top + 16]
                below, above = corner_row(sx, -1), corner_row(sx, 1)
                corner = corner + jnp.where(row == 0, extra[below:below + 1], extra[above:above + 1])
            value = value + jnp.where(there, face + jnp.where(known, corner, 0.0), 0.0)
        return value

    def ghost_points(e, f, value, i, which, scale=None):
        xs, ys, cs = halo[3 * e:3 * e + 3]

        def put(at, size, mine, theirs, weight, there):
            rest = mine - theirs
            if scale is not None:
                rest = rest * weight
            strips[which, at:at + size, :] = jnp.where(there, rest, 0.0)

        by = [None] * 3 if scale is None else [scale, scale[0:1], scale[ny - 1:ny]]
        put(Y_DOWN + i, 1, value[0:1], ys[0, f, i, 0:1, :], by[1], has_yl)
        put(Y_UP + i, 1, value[ny - 1:ny], ys[1, f, i, 7:8, :], by[2], has_yh)
        if i in (0, nx - 1):
            side = 0 if i == 0 else 1
            sx = -1 if i == 0 else 1
            there = has_xl if i == 0 else has_xh
            put(X_UP if sx > 0 else X_DOWN, 16, value, xs[side, f], by[0], there)
            put(corner_row(sx, -1), 1, value[0:1], cs[side, f, 0:1, :], by[1], there & has_yl)
            put(corner_row(sx, 1), 1, value[ny - 1:ny], cs[side, f, ny - 1:ny, :], by[2], there & has_yh)

    lane_p = lax.broadcasted_iota(jnp.int32, (POINTS, nz), 1) % 8
    row_p = lax.broadcasted_iota(jnp.int32, (POINTS, nz), 0)

    def fold_points(value):
        up = pltpu.roll(value, nz - 1, 1)
        down = pltpu.roll(value, 1, 1)
        value = value + jnp.where(lane_p == 7, up, 0.0) + jnp.where(lane_p == 0, down, 0.0)
        up = pltpu.roll(value, POINTS - 1, 0)
        down = pltpu.roll(value, 1, 0)
        on_face = row_p < CORNERS
        extra[...] = (
            value
            + jnp.where(on_face & (row_p % 16 == 7), up, 0.0)
            + jnp.where(on_face & (row_p % 16 == 8), down, 0.0)
        )

    def operate(value, parts):
        return wts[...].reshape(rows, nz) * (
            left(bxy, parts) + right(parts, bz) + flat(reac) * value
        )

    def slopes(parts, k):
        both = left(kxy, parts)
        raw[k, 0] = both[:rows].reshape(nx, ny, nz)
        raw[k, 1] = both[rows:].reshape(nx, ny, nz)
        third = right(parts, kz)
        for i in range(nx):
            v = third[i * ny:(i + 1) * ny]
            other = jnp.where(lane == 7, pltpu.roll(v, nz - 1, 1), pltpu.roll(v, 1, 1))
            asm[k, 2, i] = jnp.where((lane == 7) | (lane == 0), 0.5 * (v + other), v)

    def slope_copies(e, first, count):
        xs, ys = halo[3 * e:3 * e + 2]
        made = []
        for n, (ds, dv) in enumerate(SIDES):
            group = []
            if ds * dv == 0:
                some = pl.ds(first, count)
                if dv == 0:
                    a = raw.at[some, 0, nx - 1 if ds > 0 else 0]
                    b = xs.at[0 if ds > 0 else 1]
                else:
                    a = raw.at[some, 1, :, pl.ds(ny - 1 if dv > 0 else 0, 1), :]
                    b = ys.at[0 if dv > 0 else 1].at[:, :, pl.ds(0 if dv > 0 else 7, 1), :]
                group.append(
                    pltpu.make_async_remote_copy(
                        src_ref=a, dst_ref=b,
                        send_sem=send_sem.at[e, n], recv_sem=recv_sem.at[e, n],
                        device_id=near(ds, dv), device_id_type=MESH,
                    )
                )
            made.append(group)
        return launch(made)

    def average(e, f, k):
        xs, ys = halo[3 * e:3 * e + 2]
        middle = 0.5 * (raw[k, 0, 7] + raw[k, 0, 8])
        for i in range(nx):
            v = raw[k, 0, i]
            if i in (7, 8):
                v = middle
            elif i == 0:
                v = jnp.where(has_xl, 0.5 * (v + xs[0, f]), v)
            elif i == nx - 1:
                v = jnp.where(has_xh, 0.5 * (v + xs[1, f]), v)
            asm[k, 0, i] = v
            v = raw[k, 1, i]
            other = jnp.concatenate([ys[0, f, i], ys[1, f, i]], axis=0)
            other = jnp.where(row == 7, pltpu.roll(v, ny - 1, 0), other)
            other = jnp.where(row == 8, pltpu.roll(v, 1, 0), other)
            shared = (row == 7) | (row == 8) | ((row == 0) & has_yl) | ((row == ny - 1) & has_yh)
            asm[k, 1, i] = jnp.where(shared, 0.5 * (v + other), v)

    def to_row(value, slot):
        s = value.reshape(rows // 8, 8, nz).sum(axis=0)
        s = s[:, :128] + s[:, 128:]
        tiles[slot:slot + 1, :] = jnp.sum(s, axis=0, keepdims=True)

    _, quad = gll_tables()
    loads[0].wait()
    column = lax.broadcasted_iota(jnp.int32, (ny, nz), 1)

    def put_block(dst, at, mask, tile):
        high = tile.astype(BF16).astype(F32)
        dst[0, at:at + ny, :] = jnp.where(mask, high, 0.0).astype(BF16)
        dst[1, at:at + ny, :] = jnp.where(mask, tile - high, 0.0).astype(BF16)

    tile_z = jnp.concatenate([tab[0:8], tab[0:8]], axis=0)
    tile_y = jnp.concatenate([tab[8:16], tab[8:16]], axis=0)
    tile_w = jnp.concatenate([tab[32:40], tab[32:40]], axis=0)
    tile_m = jnp.concatenate([tab[40:48], tab[40:48]], axis=0)
    edge = ((row == 0) & (me_v == 0)) | ((row == ny - 1) & (me_v == n_vert - 1))
    tile_m = tile_m * jnp.where(edge, 2.0, 1.0)
    for i in range(nx):
        here = column // 8 == 2 * i + row // 8
        put_block(kz, i * ny, here, tile_z)
        put_block(kxy, rows + i * ny, here, tile_y)
        put_block(kxy, i * ny, column % ny == row, jnp.broadcast_to(tab[16 + i:17 + i], (ny, nz)))
        wts[i] = tile_w * float(quad[i % 8])
        value = tile_m
        if i in (0, nx - 1):
            value = value * jnp.where((me_s == 0) if i == 0 else (me_s == n_stream - 1), 1.0, 0.5)
        elif i % 8 in (0, 7):
            value = value * 0.5
        imult[i] = value
        imass[i] = time_step * value / wts[i]

    loads[1].wait()
    for c in range(3):
        parts = split(flat(adj.at[c]))
        both = left(kxy, parts)
        third = right(parts, kz)
        if c == 0:
            loads[2].wait()
            for load in loads[3:]:
                load.start()
        conv[c] = (
            flat(base.at[0]) * both[:rows] + flat(base.at[1]) * both[rows:] + flat(base.at[2]) * third
        ).reshape(nx, ny, nz)
    for j in range(3):
        parts = split(flat(base.at[j]))
        a = flat(adj.at[j])
        both = left(kxy, parts)
        conv[0] -= (a * both[:rows]).reshape(nx, ny, nz)
        conv[1] -= (a * both[rows:]).reshape(nx, ny, nz)
        conv[2] -= (a * right(parts, kz)).reshape(nx, ny, nz)
    for c in range(3):
        fold_store(flat(conv.at[c]) * flat(wts), part3.at[c])
    pl.semaphore_wait(barrier, len(partners))
    sends = [copies(0, part3), strip_copies(0, part3.at[0], part3.at[1], 0, 1)]

    def right_side(fields):
        pair = jnp.concatenate([fields[0], fields[1]], axis=0)
        return flat(wts) * (left(cxy, split(pair)) + right(split(fields[2]), cz))

    for load in loads[3:]:
        load.wait()
    fold_store(
        right_side([flat(adj.at[c]) + flat(imass) * flat(part3.at[c]) for c in range(3)]),
        loc.at[0].at[0],
    )
    sends += [copies(1, loc.at[0]), reaction_copies()]

    arrive(sends[0])
    for c in range(3):
        for i in range(nx):
            value = with_halo(0, c, part3, i)
            moved[c, i] = adj[c, i] + value * imass[i]
            ghost_points(0, c, value, i, c, imass[i])
    fold_store(right_side([flat(moved.at[c]) for c in range(3)]), own.at[0])
    arrive(sends[1])
    for c in (0, 1):
        for at in range(POINTS, 208, 8):
            strips[c, at:at + 8, :] = strips[c, at:at + 8, :] * sc[...]
    ghosts = jnp.concatenate([strips[0], strips[1]], axis=0)
    fold_points(gw[...] * (left(gc, split(ghosts)) + right(split(strips[2, 0:POINTS, :]), cz)))
    arrive(sends[2])
    for i in range(nx):
        vec[0, i] = with_halo(1, 0, own, i, True)

    v = flat(vec.at[0])
    parts = split(v)
    image = operate(v, parts)
    fold_store(image, loc.at[1].at[0])
    sends += [copies(2, loc.at[1]), strip_copies(1, loc.at[1].at[0], loc.at[1].at[0], 3, 3)]
    first = flat(loc.at[1].at[0])
    fold_store(operate(first, split(first)), loc.at[2].at[0])
    sends.append(copies(3, loc.at[2]))
    to_row(v * v * flat(imult), 0)
    to_row(v * image, 1)
    slopes(parts, 0)
    sends.append(slope_copies(5, 0, 1))
    arrive(sends[3])
    arrive(sends[4])
    for i in range(nx):
        value = with_halo(2, 0, loc.at[1], i)
        vec[1, i] = value
        ghost_points(2, 0, value, i, 3)

    v = flat(vec.at[1])
    parts = split(v)
    image = operate(v, parts)
    fold_store(image, own.at[0])
    arrive(sends[5])
    points = strips[3, 0:POINTS, :]
    fold_points(
        gw[...] * (left(gb, split(strips[3])) + right(split(points), bz) + ghost_reac[...] * points)
    )
    to_row(v * v * flat(imult), 2)
    to_row(v * image, 3)
    arrive(sends[6])
    for i in range(nx):
        vec[2, i] = with_halo(3, 0, own, i, True)

    v = flat(vec.at[2])
    parts = split(v)
    image = operate(v, parts)
    to_row(v * v * flat(imult), 4)
    to_row(v * image, 5)

    tiles[6:8, :] = jnp.zeros((2, 128), F32)
    group = lax.broadcasted_iota(jnp.int32, (8, 128), 1) // 16
    packed = tiles[...]
    for shift in (64, 32, 16):
        packed = packed + pltpu.roll(packed, shift, 1)
    packed = jnp.where(group == lax.broadcasted_iota(jnp.int32, (8, 128), 0), packed, 0.0)
    red_a[n_vert - 1:n_vert, :] = jnp.sum(packed, axis=0, keepdims=True)

    def spread(slots, n, which):
        for k in range(1, n):
            pltpu.make_async_remote_copy(
                src_ref=slots.at[pl.ds(n - 1, 1)], dst_ref=slots.at[pl.ds(k - 1, 1)],
                send_sem=red_send.at[which], recv_sem=red_recv.at[which],
                device_id=near(0, k) if which == 0 else near(k, 0), device_id_type=MESH,
            ).start()

    def whole(slots, n, which):
        return pltpu.make_async_remote_copy(
            src_ref=slots.at[pl.ds(0, n - 1)], dst_ref=slots.at[pl.ds(0, n - 1)],
            send_sem=red_send.at[which], recv_sem=red_recv.at[which],
            device_id=near(0, 1), device_id_type=MESH,
        )

    spread(red_a, n_vert, 0)
    slopes(split(flat(vec.at[1])), 1)
    slopes(parts, 2)
    sends.append(slope_copies(4, 1, 2))
    whole(red_a, n_vert, 0).wait_recv()
    red_b[n_stream - 1:n_stream, :] = jnp.sum(red_a[...], axis=0, keepdims=True)
    spread(red_b, n_stream, 1)

    arrive(sends[7])
    average(5, 0, 0)
    arrive(sends[8])
    average(4, 0, 1)
    average(4, 1, 2)

    whole(red_b, n_stream, 1).wait_recv()
    total = jnp.sum(red_b[...], axis=0, keepdims=True)
    m = [jnp.sum(jnp.where(group[0:1] == k, total, 0.0), axis=1, keepdims=True) for k in range(6)]
    a0 = m[0] / m[1]
    r1 = a0 * a0 * m[2] - m[0]
    k1 = 1.0 + r1 / m[0]
    p1 = k1 * k1 * m[1] - 2.0 * k1 * a0 * m[2] + a0 * a0 * m[3]
    a1 = r1 / p1
    e1 = -(a0 + a1 * k1)
    e2 = a1 * a0
    r2 = m[0] + 2.0 * e1 * m[1] + (e1 * e1 + 2.0 * e2) * m[2] + 2.0 * e1 * e2 * m[3] + e2 * e2 * m[4]
    b2 = r2 / r1
    f0 = 1.0 + b2 * k1
    f1 = e1 - b2 * a0
    f2 = e2
    p2 = (
        f0 * f0 * m[1] + 2.0 * f0 * f1 * m[2] + (f1 * f1 + 2.0 * f0 * f2) * m[3]
        + 2.0 * f1 * f2 * m[4] + f2 * f2 * m[5]
    )
    a2 = r2 / p2
    c0 = a0 + a1 * k1 + a2 * f0
    c1 = a2 * f1 - a1 * a0
    c2 = a2 * f2
    for k, c in enumerate((c0, c1, c2)):
        coef[k:k + 1, :] = jnp.broadcast_to(c, (1, nz))
    for made in sends:
        leave(made)
    whole(red_a, n_vert, 0).wait_send()
    whole(red_b, n_stream, 1).wait_send()


def combine(moved, asm, vec, coef, out_h, pres_h, out, pres, sems):
    copies = []
    for i in range(pres.shape[0]):
        pres[i] = coef[0:1] * vec[0, i] + coef[1:2] * vec[1, i] + coef[2:3] * vec[2, i]
    copies.append(pltpu.make_async_copy(pres, pres_h, sems.at[3]))
    copies[-1].start()
    for d in range(3):
        for i in range(pres.shape[0]):
            out[d, i] = moved[d, i] - (
                coef[0:1] * asm[0, d, i] + coef[1:2] * asm[1, d, i] + coef[2:3] * asm[2, d, i]
            )
        copies.append(pltpu.make_async_copy(out.at[d], out_h.at[d], sems.at[d]))
        copies[-1].start()
    for copy in copies:
        copy.wait()


def on_device(n_stream, n_vert, base_flow, adjoint_velocity, reaction):
    nx, ny, nz = reaction.shape
    consts = constants(nx, ny, nz)
    field = (nx, ny, nz)
    operands = [base_flow, adjoint_velocity, reaction, *[jnp.asarray(c) for c in consts]]
    scratch = [
        pltpu.VMEM(base_flow.shape, F32),
        pltpu.VMEM(base_flow.shape, F32),
        pltpu.VMEM(field, F32),
        *[pltpu.VMEM(c.shape, c.dtype) for c in consts],
        pltpu.VMEM((2, 2 * nx * ny, nx * ny), BF16),
        pltpu.VMEM((2, nz, nz), BF16),
        pltpu.VMEM(field, F32),
        pltpu.VMEM(field, F32),
        pltpu.VMEM(field, F32),
        pltpu.VMEM((3, *field), F32),
        pltpu.VMEM((3, 1, *field), F32),
        pltpu.VMEM((3, 2, *field), F32),
        pltpu.VMEM((3, *field), F32),
        pltpu.VMEM((1, *field), F32),
        pltpu.VMEM((4, STRIPS, nz), F32),
        pltpu.VMEM((POINTS, nz), F32),
        pltpu.VMEM((POINTS, nz), F32),
        pltpu.VMEM((8, 128), F32),
        pltpu.VMEM((n_vert, 128), F32),
        pltpu.VMEM((n_stream, 128), F32),
        pltpu.SemaphoreType.DMA((3 + len(consts),)),
        pltpu.SemaphoreType.DMA((7, 8)),
        pltpu.SemaphoreType.DMA((7, 8)),
        pltpu.SemaphoreType.DMA((2, 16)),
        pltpu.SemaphoreType.DMA((2, 16)),
        pltpu.SemaphoreType.DMA((2,)),
        pltpu.SemaphoreType.DMA((2,)),
    ]
    for count in FIELDS:
        scratch += [
            pltpu.VMEM((2, count, ny, nz), F32),
            pltpu.VMEM((2, count, nx, 8, nz), F32),
            pltpu.VMEM((2, count, ny, nz), F32),
        ]
    pieces = pl.pallas_call(
        functools.partial(kernel, n_stream, n_vert),
        out_shape=(
            pltpu.VMEM((3, *field), F32),
            pltpu.VMEM((3, 3, *field), F32),
            pltpu.VMEM((3, *field), F32),
            pltpu.VMEM((8, nz), F32),
        ),
        in_specs=[pl.BlockSpec(memory_space=pl.ANY)] * len(operands),
        out_specs=tuple([pl.BlockSpec(memory_space=pltpu.VMEM)] * 4),
        scratch_shapes=scratch,
        compiler_params=pltpu.CompilerParams(
            collective_id=0, has_side_effects=True, vmem_limit_bytes=48 * 1024 * 1024
        ),
    )(*[pltpu.with_memory_space_constraint(a, pltpu.HBM) for a in operands])
    return pl.pallas_call(
        combine,
        out_shape=(
            pltpu.HBM(base_flow.shape, F32),
            pltpu.HBM(field, F32),
        ),
        in_specs=[pl.BlockSpec(memory_space=pltpu.VMEM)] * 4,
        out_specs=tuple([pl.BlockSpec(memory_space=pl.ANY)] * 2),
        scratch_shapes=[
            pltpu.VMEM(base_flow.shape, F32),
            pltpu.VMEM(field, F32),
            pltpu.SemaphoreType.DMA((4,)),
        ],
        compiler_params=pltpu.CompilerParams(vmem_limit_bytes=16 * 1024 * 1024),
    )(*[pltpu.with_memory_space_constraint(a, pltpu.VMEM) for a in pieces])


def solution(mesh):
    placed = (
        P(None, "stream", "vert", None),
        P(None, "stream", "vert", None),
        P("stream", "vert", None),
    )
    return jax.shard_map(
        functools.partial(on_device, mesh.shape["stream"], mesh.shape["vert"]),
        mesh=mesh,
        in_specs=placed,
        out_specs=(P(None, "stream", "vert", None), P("stream", "vert", None)),
        check_vma=False,
    )
```

```python
import functools

import jax
import jax.numpy as jnp
import ml_dtypes
import numpy as np
from jax import lax
from jax.experimental import pallas as pl
from jax.experimental.pallas import tpu as pltpu
from jax.sharding import PartitionSpec as P

time_step = 0.05
MESH = pl.DeviceIdType.MESH
F32 = jnp.float32
BF16 = jnp.bfloat16
SIDES = ((1, 0), (-1, 0), (0, 1), (0, -1), (1, 1), (1, -1), (-1, 1), (-1, -1))
FIELDS = (3, 1, 1, 1, 2, 1)
X_UP, X_DOWN, Y_UP, Y_DOWN, CORNERS, POINTS, STRIPS = 0, 16, 32, 48, 64, 80, 128


def gll_tables():
    degree = 7
    inner_nodes = np.array([0.8717401485096066, 0.5917001814331423, 0.2092992179024789])
    points_ref = np.concatenate([[-1.0], -inner_nodes, inner_nodes[::-1], [1.0]])
    previous = np.ones(8)
    current = points_ref.copy()
    for order_now in range(1, degree):
        following = ((2 * order_now + 1) * points_ref * current - order_now * previous) / (
            order_now + 1
        )
        previous = current
        current = following
    quadrature = 2.0 / (degree * (degree + 1) * current**2)
    derivative_table = np.zeros((8, 8))
    for i in range(8):
        for j in range(8):
            if i != j:
                derivative_table[i, j] = current[i] / (current[j] * (points_ref[i] - points_ref[j]))
    derivative_table[0, 0] = -degree * (degree + 1) / 4.0
    derivative_table[7, 7] = degree * (degree + 1) / 4.0
    return (derivative_table, quadrature)


def halves(matrix):
    high = matrix.astype(np.float32).astype(ml_dtypes.bfloat16)
    low = (matrix - high.astype(np.float64)).astype(ml_dtypes.bfloat16)
    return np.stack([high, low])


def constants(nx, ny, nz):
    table, quad = gll_tables()
    table = table.astype(np.float32).astype(np.float64)
    quad = quad.astype(np.float32).astype(np.float64)
    turned = table.T * quad[None, :] / quad[:, None]
    stiff = turned @ table
    eye = np.eye

    def along_x(m):
        return np.kron(np.kron(eye(nx // 8), m), eye(ny))

    def along_y(m):
        return np.kron(eye(nx * ny // 8), m)

    def along_z(m):
        return np.kron(eye(nz // 8), m.T)

    weights = (
        np.tile(quad, nx // 8)[:, None, None]
        * np.tile(quad, ny // 8)[None, :, None]
        * np.tile(quad, nz // 8)[None, None, :]
    ).astype(np.float32)
    twice = np.array([2.0, 1, 1, 1, 1, 1, 1, 2.0])
    mult = (
        np.tile(twice, nx // 8)[:, None, None]
        * np.tile(twice, ny // 8)[None, :, None]
        * np.tile(twice, nz // 8)[None, None, :]
    )
    ghost_rhs = ghost_matrices(turned)
    points = np.zeros(POINTS, np.int64)
    points[X_UP:X_UP + 16] = (nx - 1) * ny + np.arange(ny)
    points[X_DOWN:X_DOWN + 16] = np.arange(ny)
    points[Y_UP:Y_UP + 16] = np.arange(nx) * ny + ny - 1
    points[Y_DOWN:Y_DOWN + 16] = np.arange(nx) * ny
    for sx in (1, -1):
        for sy in (1, -1):
            points[corner_row(sx, sy)] = ((nx - 1) * ny if sx > 0 else 0) + (ny - 1 if sy > 0 else 0)
    ghost_weights = np.zeros((POINTS, nz), np.float32)
    for top, face in ((X_UP, weights[0]), (X_DOWN, weights[-1]), (Y_UP, weights[:, 0]), (Y_DOWN, weights[:, -1])):
        ghost_weights[top:top + 16] = face
    ghost_weights[CORNERS:CORNERS + 4] = weights[0, 0]
    first = np.zeros((nx, nz))
    for r in range(nx):
        first[r] = np.tile(np.repeat(table[r % 8], ny), nx // 8) * (np.arange(nz) // 128 == r // 8)
    across = np.tile(quad[:, None] * quad[None, :], (1, nz // 8))
    return [
        np.concatenate(
            [np.tile(table.T, (1, nz // 8)), np.tile(table, (1, nz // 8)), first, across, 1.0 / mult[1, :8]]
        ).astype(np.float32),
        halves(np.concatenate([along_x(turned), along_y(turned)], axis=1)),
        halves(along_z(turned)),
        halves(along_x(stiff) + along_y(stiff)),
        halves(along_z(stiff)),
        halves(np.concatenate([ghost_rhs[0], ghost_rhs[1]], axis=1)),
        halves(ghost_matrices(stiff).sum(axis=0)),
        halves(np.concatenate([along_x(turned), along_y(turned)], axis=1)[points]),
        halves((along_x(stiff) + along_y(stiff))[points]),
        ghost_weights,
    ]


def corner_row(sx, sy):
    return CORNERS + (0 if sx > 0 else 2) + (0 if sy > 0 else 1)


def strip_row(kind, sx, sy):
    if kind in ("x", "y"):
        return POINTS + 2 * (corner_row(sx, sy) - CORNERS) + (kind == "y")
    if kind == "cx":
        return POINTS + 8 + 2 * (sx < 0) + (sy < 0)
    return POINTS + 12 + 2 * (sy < 0) + (sx < 0)


def ghost_matrices(m):
    along = np.zeros((2, POINTS, STRIPS))
    blocks = np.kron(np.eye(2), m)
    for sign in (1, -1):
        node = 0 if sign > 0 else 7
        top_x, top_y = (X_UP, Y_UP) if sign > 0 else (X_DOWN, Y_DOWN)
        for r in range(16):
            along[0, top_x + r, top_x + r] += m[node, node]
            along[1, top_x + r, top_x:top_x + 16] += blocks[r]
            along[1, top_y + r, top_y + r] += m[node, node]
            along[0, top_y + r, top_y:top_y + 16] += blocks[r]
        for side in (1, -1):
            r = 15 if side > 0 else 0
            along[0, top_x + r, strip_row("x", sign, side)] += 1.0
            along[0, top_y + r, strip_row("y", side, sign)] += 1.0
            along[0, corner_row(sign, side), strip_row("cx", sign, side)] += 1.0
            along[0, corner_row(side, sign), strip_row("cy", side, sign)] += 1.0
            along[0, corner_row(sign, side), corner_row(sign, side)] += m[node, node]
            along[1, corner_row(side, sign), corner_row(side, sign)] += m[node, node]
    return along


def split(value):
    high = value.astype(BF16)
    low = (value - high.astype(F32)).astype(BF16)
    return high, low


def dot(a, b):
    return jnp.dot(a, b, preferred_element_type=F32)


def left(matrix, parts):
    high, low = parts
    return dot(matrix[0], high) + dot(matrix[0], low) + dot(matrix[1], high)


def right(parts, matrix):
    high, low = parts
    return dot(high, matrix[0]) + dot(low, matrix[0]) + dot(high, matrix[1])


def kernel(
    n_stream,
    n_vert,
    base_h, adj_h, reac_h, tab_h, cxy_h, cz_h, bxy_h, bz_h,
    gc_h, gb_h, cf_h, bf_h, gw_h,
    moved, asm, vec, coef,
    base, adj, reac, tab, cxy, cz, bxy, bz, gc, gb, cf, bf, gw, kxy, kz, wts, imult,
    imass, conv, loc, raw, part3,
    own, strips, ghost_reac, extra, mine, mine_reac, outbox, inbox, strip_out, tiles, red_a, red_b,
    in_sem, send_sem, recv_sem, strip_send, strip_recv, red_send, red_recv,
    *halo,
):
    me_s = lax.axis_index("stream")
    me_v = lax.axis_index("vert")
    nx, ny, nz = reac.shape
    rows = nx * ny

    inputs = [
        (tab_h, tab), (adj_h, adj), (base_h, base),
        (cf_h, cf), (cz_h, cz), (gw_h, gw), (cxy_h, cxy), (reac_h, reac), (gc_h, gc),
        (bxy_h, bxy), (bz_h, bz), (bf_h, bf), (gb_h, gb),
    ]
    loads = [pltpu.make_async_copy(a, b, in_sem.at[i]) for i, (a, b) in enumerate(inputs)]
    for load in loads[:3]:
        load.start()

    def near(ds, dv):
        return (lax.rem(me_s + ds + n_stream, n_stream), lax.rem(me_v + dv + n_vert, n_vert))

    strips[...] = jnp.zeros_like(strips)
    ghost_reac[...] = jnp.zeros_like(ghost_reac)
    inbox[...] = jnp.zeros_like(inbox)
    mine[:, CORNERS + 4:, :] = jnp.zeros((3, POINTS - CORNERS - 4, nz), F32)
    mine_reac[CORNERS + 4:, :] = jnp.zeros((POINTS - CORNERS - 4, nz), F32)

    barrier = pltpu.get_barrier_semaphore()
    partners = [near(ds, dv) for ds, dv in SIDES]
    partners += [near(0, k) for k in range(1, n_vert)]
    partners += [near(k, 0) for k in range(1, n_stream)]
    for partner in partners:
        pl.semaphore_signal(barrier, inc=1, device_id=partner, device_id_type=MESH)

    has_xl = me_s > 0
    has_xh = me_s < n_stream - 1
    has_yl = me_v > 0
    has_yh = me_v < n_vert - 1

    def exists(ds, dv):
        conditions = []
        if ds:
            conditions.append(has_xh if ds > 0 else has_xl)
        if dv:
            conditions.append(has_yh if dv > 0 else has_yl)
        return functools.reduce(jnp.logical_and, conditions)

    def flat(ref):
        return ref[...].reshape(rows, nz)

    lane = lax.broadcasted_iota(jnp.int32, (ny, nz), 1) % 8
    sub = lax.broadcasted_iota(jnp.int32, (8, nz), 0)
    row = lax.broadcasted_iota(jnp.int32, (ny, nz), 0)

    def fold_store(value, ref):
        for i in range(nx):
            v = value[i * ny:(i + 1) * ny]
            up = pltpu.roll(v, nz - 1, 1)
            down = pltpu.roll(v, 1, 1)
            ref[i] = v + jnp.where(lane == 7, up, 0.0) + jnp.where(lane == 0, down, 0.0)
        both = ref[7] + ref[8]
        ref[7] = both
        ref[8] = both
        both = ref[:, 7:8, :] + ref[:, 8:9, :]
        ref[:, 7:8, :] = both
        ref[:, 8:9, :] = both

    def copies(e, src):
        xs, ys, cs = halo[3 * e:3 * e + 3]
        made = []
        for n, (ds, dv) in enumerate(SIDES):
            if dv == 0:
                a = src.at[:, nx - 1 if ds > 0 else 0]
                b = xs.at[0 if ds > 0 else 1]
            else:
                at = pl.ds(ny - 1 if dv > 0 else 0, 1)
                if ds == 0:
                    a = src.at[:, :, at, :]
                    b = ys.at[0 if dv > 0 else 1].at[:, :, pl.ds(0 if dv > 0 else 7, 1), :]
                else:
                    a = src.at[:, nx - 1 if ds > 0 else 0, at, :]
                    b = cs.at[0 if ds > 0 else 1].at[:, pl.ds(0 if dv > 0 else ny - 1, 1), :]
            made.append(
                pltpu.make_async_remote_copy(
                    src_ref=a, dst_ref=b,
                    send_sem=send_sem.at[e, n], recv_sem=recv_sem.at[e, n],
                    device_id=near(ds, dv), device_id_type=MESH,
                )
            )
        for copy, (ds, dv) in zip(made, SIDES):
            pl.when(exists(ds, dv))(copy.start)
        return [[copy] for copy in made]

    def strip_copies(pair, field_x, field_y, scale, m, which):
        def slope(node):
            return [0.0 if j == node else float(m[node, j]) for j in range(8)]

        columns = {}
        for node in (0, 7):
            factors = jnp.zeros((8, nz), F32)
            for j, c in enumerate(slope(node)):
                factors = jnp.where(sub == j, c, factors)
            columns[node] = factors

        def part(field, x, ys):
            value = field[x, ys, :]
            return value * imass[x, ys, :] if scale else value

        def sum_x(sx, start, y):
            terms = [c * part(field_x, start + j, slice(y, y + 1)) for j, c in enumerate(slope(0 if sx > 0 else 7)) if c]
            return functools.reduce(jnp.add, terms)

        def sum_y(sy, x, start):
            tile = columns[0 if sy > 0 else 7] * part(field_y, x, slice(start, start + 8))
            return jnp.sum(tile, axis=0, keepdims=True)

        made = []
        for n, (ds, dv) in enumerate(SIDES):
            here_x, here_y = (nx - 1 if ds > 0 else 0), (ny - 1 if dv > 0 else 0)
            start_x, start_y = (nx - 8 if ds > 0 else 0), (ny - 8 if dv > 0 else 0)
            if dv == 0:
                first = strip_row("cx", -ds, 1)
                two = [sum_x(-ds, start_x, ny - 1), sum_x(-ds, start_x, 0)]
            elif ds == 0:
                first = strip_row("cy", 1, -dv)
                two = [sum_y(-dv, nx - 1, start_y), sum_y(-dv, 0, start_y)]
            else:
                first = strip_row("x", -ds, -dv)
                two = [sum_x(-ds, start_x, here_y), sum_y(-dv, here_x, start_y)]
            at = first - POINTS
            for k in (0, 1):
                strip_out[pair, at + k:at + k + 1, :] = two[k]
            made.append([
                pltpu.make_async_remote_copy(
                    src_ref=strip_out.at[pair, pl.ds(at, 2), :], dst_ref=strips.at[which, pl.ds(first, 2), :],
                    send_sem=strip_send.at[pair, n], recv_sem=strip_recv.at[pair, n],
                    device_id=near(ds, dv), device_id_type=MESH,
                )
            ])
        return launch(made)

    def reaction_copies():
        made = []
        for n, (ds, dv) in enumerate(SIDES):
            here_x, here_y = (nx - 1 if ds > 0 else 0), (ny - 1 if dv > 0 else 0)
            if dv == 0:
                src, at, size = reac.at[here_x], (X_UP if ds < 0 else X_DOWN), 16
            elif ds == 0:
                src, at, size = reac.at[:, here_y, :], (Y_UP if dv < 0 else Y_DOWN), 16
            else:
                src, at, size = reac.at[here_x, pl.ds(here_y, 1), :], corner_row(-ds, -dv), 1
            made.append([
                pltpu.make_async_remote_copy(
                    src_ref=src, dst_ref=ghost_reac.at[pl.ds(at, size), :],
                    send_sem=send_sem.at[6, n], recv_sem=recv_sem.at[6, n],
                    device_id=near(ds, dv), device_id_type=MESH,
                )
            ])
        return launch(made)

    def launch(made):
        for group, (ds, dv) in zip(made, SIDES):
            @pl.when(bool(group) and exists(ds, dv))
            def _(group=group):
                for copy in group:
                    copy.start()
        return made

    def arrive(made):
        for group, (ds, dv) in zip(made, SIDES):
            @pl.when(bool(group) and exists(-ds, -dv))
            def _(group=group):
                for copy in group:
                    copy.wait_recv()

    def leave(made):
        for group, (ds, dv) in zip(made, SIDES):
            @pl.when(bool(group) and exists(ds, dv))
            def _(group=group):
                for copy in group:
                    copy.wait_send()

    def with_halo(e, f, src, i, more=False):
        xs, ys, cs = halo[3 * e:3 * e + 3]
        if more:
            low, high = extra[Y_DOWN + i:Y_DOWN + i + 1], extra[Y_UP + i:Y_UP + i + 1]
        else:
            low, high = ys[0, f, i], ys[1, f, i]
        low = src[f, i, 0:8, :] + jnp.where((sub == 0) & has_yl, low, 0.0)
        high = src[f, i, ny - 8:ny, :] + jnp.where((sub == 7) & has_yh, high, 0.0)
        value = jnp.concatenate([low, high], axis=0)
        if i in (0, nx - 1):
            side = 0 if i == 0 else 1
            sx = -1 if i == 0 else 1
            there = has_xl if i == 0 else has_xh
            known = ((row == 0) & has_yl) | ((row == ny - 1) & has_yh)
            if more:
                top = X_UP if sx > 0 else X_DOWN
                below, above = corner_row(sx, -1), corner_row(sx, 1)
                face = extra[top:top + 16]
                corner = jnp.where(row == 0, extra[below:below + 1], extra[above:above + 1])
            else:
                face, corner = xs[side, f], cs[side, f]
            value = value + jnp.where(there, face + jnp.where(known, corner, 0.0), 0.0)
        return value

    def ghost_points(e, f, value, i, which, scale=None):
        xs, ys, cs = halo[3 * e:3 * e + 3]

        def put(at, size, mine, theirs, weight, there):
            rest = mine - theirs
            if scale is not None:
                rest = rest * weight
            strips[which, at:at + size, :] = jnp.where(there, rest, 0.0)

        by = [None] * 3 if scale is None else [scale, scale[0:1], scale[ny - 1:ny]]
        put(Y_DOWN + i, 1, value[0:1], ys[0, f, i, 0:1, :], by[1], has_yl)
        put(Y_UP + i, 1, value[ny - 1:ny], ys[1, f, i, 7:8, :], by[2], has_yh)
        if i in (0, nx - 1):
            side = 0 if i == 0 else 1
            sx = -1 if i == 0 else 1
            there = has_xl if i == 0 else has_xh
            put(X_UP if sx > 0 else X_DOWN, 16, value, xs[side, f], by[0], there)
            put(corner_row(sx, -1), 1, value[0:1], cs[side, f, 0:1, :], by[1], there & has_yl)
            put(corner_row(sx, 1), 1, value[ny - 1:ny], cs[side, f, ny - 1:ny, :], by[2], there & has_yh)

    lane_p = lax.broadcasted_iota(jnp.int32, (POINTS, nz), 1) % 8
    row_p = lax.broadcasted_iota(jnp.int32, (POINTS, nz), 0)

    def fold_points(value, dst):
        up = pltpu.roll(value, nz - 1, 1)
        down = pltpu.roll(value, 1, 1)
        value = value + jnp.where(lane_p == 7, up, 0.0) + jnp.where(lane_p == 0, down, 0.0)
        up = pltpu.roll(value, POINTS - 1, 0)
        down = pltpu.roll(value, 1, 0)
        on_face = row_p < CORNERS
        dst[...] = (
            value
            + jnp.where(on_face & (row_p % 16 == 7), up, 0.0)
            + jnp.where(on_face & (row_p % 16 == 8), down, 0.0)
        )

    def gather(src, dst):
        dst[X_UP:X_UP + 16, :] = src[nx - 1]
        dst[X_DOWN:X_DOWN + 16, :] = src[0]
        for i in range(nx):
            dst[Y_UP + i:Y_UP + i + 1, :] = src[i, ny - 1:ny, :]
            dst[Y_DOWN + i:Y_DOWN + i + 1, :] = src[i, 0:1, :]
        for sx in (1, -1):
            for sy in (1, -1):
                at, y = corner_row(sx, sy), (ny - 1 if sy > 0 else 0)
                dst[at:at + 1, :] = src[nx - 1 if sx > 0 else 0, y:y + 1, :]

    def point_copies(pair, e):
        made = []
        for n, (ds, dv) in enumerate(SIDES):
            if dv == 0:
                a, b, size = (X_UP, X_DOWN, 16) if ds > 0 else (X_DOWN, X_UP, 16)
            elif ds == 0:
                a, b, size = (Y_UP, Y_DOWN, 16) if dv > 0 else (Y_DOWN, Y_UP, 16)
            else:
                a, b, size = corner_row(ds, dv), corner_row(-ds, -dv), 1
            made.append([
                pltpu.make_async_remote_copy(
                    src_ref=outbox.at[pair, pl.ds(a, size), :], dst_ref=inbox.at[pair, pl.ds(b, size), :],
                    send_sem=send_sem.at[e, n], recv_sem=recv_sem.at[e, n],
                    device_id=near(ds, dv), device_id_type=MESH,
                )
            ])
        return launch(made)

    def operate(value, parts):
        return wts[...].reshape(rows, nz) * (
            left(bxy, parts) + right(parts, bz) + flat(reac) * value
        )

    def slopes(parts, k):
        both = left(kxy, parts)
        raw[k, 0] = both[:rows].reshape(nx, ny, nz)
        raw[k, 1] = both[rows:].reshape(nx, ny, nz)
        third = right(parts, kz)
        for i in range(nx):
            v = third[i * ny:(i + 1) * ny]
            other = jnp.where(lane == 7, pltpu.roll(v, nz - 1, 1), pltpu.roll(v, 1, 1))
            asm[k, 2, i] = jnp.where((lane == 7) | (lane == 0), 0.5 * (v + other), v)

    def slope_copies(e, first, count):
        xs, ys = halo[3 * e:3 * e + 2]
        made = []
        for n, (ds, dv) in enumerate(SIDES):
            group = []
            if ds * dv == 0:
                some = pl.ds(first, count)
                if dv == 0:
                    a = raw.at[some, 0, nx - 1 if ds > 0 else 0]
                    b = xs.at[0 if ds > 0 else 1]
                else:
                    a = raw.at[some, 1, :, pl.ds(ny - 1 if dv > 0 else 0, 1), :]
                    b = ys.at[0 if dv > 0 else 1].at[:, :, pl.ds(0 if dv > 0 else 7, 1), :]
                group.append(
                    pltpu.make_async_remote_copy(
                        src_ref=a, dst_ref=b,
                        send_sem=send_sem.at[e, n], recv_sem=recv_sem.at[e, n],
                        device_id=near(ds, dv), device_id_type=MESH,
                    )
                )
            made.append(group)
        return launch(made)

    def average(e, f, k):
        xs, ys = halo[3 * e:3 * e + 2]
        middle = 0.5 * (raw[k, 0, 7] + raw[k, 0, 8])
        for i in range(nx):
            v = raw[k, 0, i]
            if i in (7, 8):
                v = middle
            elif i == 0:
                v = jnp.where(has_xl, 0.5 * (v + xs[0, f]), v)
            elif i == nx - 1:
                v = jnp.where(has_xh, 0.5 * (v + xs[1, f]), v)
            asm[k, 0, i] = v
            v = raw[k, 1, i]
            other = jnp.concatenate([ys[0, f, i], ys[1, f, i]], axis=0)
            other = jnp.where(row == 7, pltpu.roll(v, ny - 1, 0), other)
            other = jnp.where(row == 8, pltpu.roll(v, 1, 0), other)
            shared = (row == 7) | (row == 8) | ((row == 0) & has_yl) | ((row == ny - 1) & has_yh)
            asm[k, 1, i] = jnp.where(shared, 0.5 * (v + other), v)

    def to_row(value, slot):
        s = value.reshape(rows // 8, 8, nz).sum(axis=0)
        s = s[:, :128] + s[:, 128:]
        tiles[slot:slot + 1, :] = jnp.sum(s, axis=0, keepdims=True)

    table, quad = gll_tables()
    turned = table.T * quad[None, :] / quad[:, None]
    stiff = turned @ table
    loads[0].wait()
    column = lax.broadcasted_iota(jnp.int32, (ny, nz), 1)

    def put_block(dst, at, mask, tile):
        high = tile.astype(BF16).astype(F32)
        dst[0, at:at + ny, :] = jnp.where(mask, high, 0.0).astype(BF16)
        dst[1, at:at + ny, :] = jnp.where(mask, tile - high, 0.0).astype(BF16)

    tile_z = jnp.concatenate([tab[0:8], tab[0:8]], axis=0)
    tile_y = jnp.concatenate([tab[8:16], tab[8:16]], axis=0)
    tile_w = jnp.concatenate([tab[32:40], tab[32:40]], axis=0)
    tile_m = jnp.concatenate([tab[40:48], tab[40:48]], axis=0)
    edge = ((row == 0) & (me_v == 0)) | ((row == ny - 1) & (me_v == n_vert - 1))
    tile_m = tile_m * jnp.where(edge, 2.0, 1.0)
    for i in range(nx):
        here = column // 8 == 2 * i + row // 8
        put_block(kz, i * ny, here, tile_z)
        put_block(kxy, rows + i * ny, here, tile_y)
        put_block(kxy, i * ny, column % ny == row, jnp.broadcast_to(tab[16 + i:17 + i], (ny, nz)))
        wts[i] = tile_w * float(quad[i % 8])
        value = tile_m
        if i in (0, nx - 1):
            value = value * jnp.where((me_s == 0) if i == 0 else (me_s == n_stream - 1), 1.0, 0.5)
        elif i % 8 in (0, 7):
            value = value * 0.5
        imult[i] = value
        imass[i] = time_step * value / wts[i]

    loads[1].wait()
    gather(adj.at[2], mine.at[1])
    gather(imass, mine.at[2])
    for c in range(3):
        parts = split(flat(adj.at[c]))
        both = left(kxy, parts)
        third = right(parts, kz)
        if c == 0:
            loads[2].wait()
            for load in loads[3:]:
                load.start()
        conv[c] = (
            flat(base.at[0]) * both[:rows] + flat(base.at[1]) * both[rows:] + flat(base.at[2]) * third
        ).reshape(nx, ny, nz)
    for j in range(3):
        parts = split(flat(base.at[j]))
        a = flat(adj.at[j])
        both = left(kxy, parts)
        conv[0] -= (a * both[:rows]).reshape(nx, ny, nz)
        conv[1] -= (a * both[rows:]).reshape(nx, ny, nz)
        conv[2] -= (a * right(parts, kz)).reshape(nx, ny, nz)
    for c in range(3):
        fold_store(flat(conv.at[c]) * flat(wts), part3.at[c])
    pl.semaphore_wait(barrier, len(partners))
    sends = [copies(0, part3), strip_copies(0, part3.at[0], part3.at[1], True, turned, 0)]

    def right_side(fields):
        pair = jnp.concatenate([fields[0], fields[1]], axis=0)
        return flat(wts) * (left(cxy, split(pair)) + right(split(fields[2]), cz))

    for load in loads[3:6]:
        load.wait()
    gather(part3.at[2], mine.at[0])
    pair = jnp.concatenate([flat(adj.at[c]) + flat(imass) * flat(part3.at[c]) for c in (0, 1)], axis=0)
    third = mine[1] + mine[2] * mine[0]
    fold_points(gw[...] * (left(cf, split(pair)) + right(split(third), cz)), outbox.at[0])
    sends.append(point_copies(0, 1))
    for load in loads[6:]:
        load.wait()
    sends.append(reaction_copies())
    gather(reac, mine_reac)

    arrive(sends[0])
    for c in range(3):
        for i in range(nx):
            value = with_halo(0, c, part3, i)
            moved[c, i] = adj[c, i] + value * imass[i]
            ghost_points(0, c, value, i, c, imass[i])
    fold_store(right_side([flat(moved.at[c]) for c in range(3)]), own.at[0])
    arrive(sends[1])
    ghosts = jnp.concatenate([strips[0], strips[1]], axis=0)
    fold_points(gw[...] * (left(gc, split(ghosts)) + right(split(strips[2, 0:POINTS, :]), cz)), extra)
    arrive(sends[2])
    extra[...] = extra[...] + inbox[0]
    for i in range(nx):
        vec[0, i] = with_halo(1, 0, own, i, True)

    v = flat(vec.at[0])
    parts = split(v)
    image = operate(v, parts)
    fold_store(image, loc.at[1].at[0])
    sends += [copies(2, loc.at[1]), strip_copies(1, loc.at[1].at[0], loc.at[1].at[0], False, stiff, 3)]
    first = flat(loc.at[1].at[0])
    gather(loc.at[1].at[0], mine.at[0])
    points = mine[0]
    fold_points(
        gw[...] * (left(bf, split(first)) + right(split(points), bz) + mine_reac[...] * points), outbox.at[1]
    )
    sends.append(point_copies(1, 3))
    to_row(v * v * flat(imult), 0)
    to_row(v * image, 1)
    slopes(parts, 0)
    sends.append(slope_copies(5, 0, 1))
    arrive(sends[3])
    arrive(sends[4])
    for i in range(nx):
        value = with_halo(2, 0, loc.at[1], i)
        vec[1, i] = value
        ghost_points(2, 0, value, i, 3)

    v = flat(vec.at[1])
    parts = split(v)
    image = operate(v, parts)
    fold_store(image, own.at[0])
    arrive(sends[5])
    points = strips[3, 0:POINTS, :]
    fold_points(
        gw[...] * (left(gb, split(strips[3])) + right(split(points), bz) + ghost_reac[...] * points), extra
    )
    to_row(v * v * flat(imult), 2)
    to_row(v * image, 3)
    arrive(sends[6])
    extra[...] = extra[...] + inbox[1]
    for i in range(nx):
        vec[2, i] = with_halo(3, 0, own, i, True)

    v = flat(vec.at[2])
    parts = split(v)
    image = operate(v, parts)
    to_row(v * v * flat(imult), 4)
    to_row(v * image, 5)

    tiles[6:8, :] = jnp.zeros((2, 128), F32)
    group = lax.broadcasted_iota(jnp.int32, (8, 128), 1) // 16
    packed = tiles[...]
    for shift in (64, 32, 16):
        packed = packed + pltpu.roll(packed, shift, 1)
    packed = jnp.where(group == lax.broadcasted_iota(jnp.int32, (8, 128), 0), packed, 0.0)
    red_a[n_vert - 1:n_vert, :] = jnp.sum(packed, axis=0, keepdims=True)

    def spread(slots, n, which):
        for k in range(1, n):
            pltpu.make_async_remote_copy(
                src_ref=slots.at[pl.ds(n - 1, 1)], dst_ref=slots.at[pl.ds(k - 1, 1)],
                send_sem=red_send.at[which], recv_sem=red_recv.at[which],
                device_id=near(0, k) if which == 0 else near(k, 0), device_id_type=MESH,
            ).start()

    def whole(slots, n, which):
        return pltpu.make_async_remote_copy(
            src_ref=slots.at[pl.ds(0, n - 1)], dst_ref=slots.at[pl.ds(0, n - 1)],
            send_sem=red_send.at[which], recv_sem=red_recv.at[which],
            device_id=near(0, 1), device_id_type=MESH,
        )

    spread(red_a, n_vert, 0)
    slopes(split(flat(vec.at[1])), 1)
    slopes(parts, 2)
    sends.append(slope_copies(4, 1, 2))
    whole(red_a, n_vert, 0).wait_recv()
    red_b[n_stream - 1:n_stream, :] = jnp.sum(red_a[...], axis=0, keepdims=True)
    spread(red_b, n_stream, 1)

    arrive(sends[7])
    average(5, 0, 0)
    arrive(sends[8])
    average(4, 0, 1)
    average(4, 1, 2)

    whole(red_b, n_stream, 1).wait_recv()
    total = jnp.sum(red_b[...], axis=0, keepdims=True)
    m = [jnp.sum(jnp.where(group[0:1] == k, total, 0.0), axis=1, keepdims=True) for k in range(6)]
    a0 = m[0] / m[1]
    r1 = a0 * a0 * m[2] - m[0]
    k1 = 1.0 + r1 / m[0]
    p1 = k1 * k1 * m[1] - 2.0 * k1 * a0 * m[2] + a0 * a0 * m[3]
    a1 = r1 / p1
    e1 = -(a0 + a1 * k1)
    e2 = a1 * a0
    r2 = m[0] + 2.0 * e1 * m[1] + (e1 * e1 + 2.0 * e2) * m[2] + 2.0 * e1 * e2 * m[3] + e2 * e2 * m[4]
    b2 = r2 / r1
    f0 = 1.0 + b2 * k1
    f1 = e1 - b2 * a0
    f2 = e2
    p2 = (
        f0 * f0 * m[1] + 2.0 * f0 * f1 * m[2] + (f1 * f1 + 2.0 * f0 * f2) * m[3]
        + 2.0 * f1 * f2 * m[4] + f2 * f2 * m[5]
    )
    a2 = r2 / p2
    c0 = a0 + a1 * k1 + a2 * f0
    c1 = a2 * f1 - a1 * a0
    c2 = a2 * f2
    for k, c in enumerate((c0, c1, c2)):
        coef[k:k + 1, :] = jnp.broadcast_to(c, (1, nz))
    for made in sends:
        leave(made)
    whole(red_a, n_vert, 0).wait_send()
    whole(red_b, n_stream, 1).wait_send()


def combine(moved, asm, vec, coef, out_h, pres_h, out, pres, sems):
    copies = []
    for i in range(pres.shape[0]):
        pres[i] = coef[0:1] * vec[0, i] + coef[1:2] * vec[1, i] + coef[2:3] * vec[2, i]
    copies.append(pltpu.make_async_copy(pres, pres_h, sems.at[3]))
    copies[-1].start()
    for d in range(3):
        for i in range(pres.shape[0]):
            out[d, i] = moved[d, i] - (
                coef[0:1] * asm[0, d, i] + coef[1:2] * asm[1, d, i] + coef[2:3] * asm[2, d, i]
            )
        copies.append(pltpu.make_async_copy(out.at[d], out_h.at[d], sems.at[d]))
        copies[-1].start()
    for copy in copies:
        copy.wait()


def on_device(n_stream, n_vert, base_flow, adjoint_velocity, reaction):
    nx, ny, nz = reaction.shape
    consts = constants(nx, ny, nz)
    field = (nx, ny, nz)
    operands = [base_flow, adjoint_velocity, reaction, *[jnp.asarray(c) for c in consts]]
    scratch = [
        pltpu.VMEM(base_flow.shape, F32),
        pltpu.VMEM(base_flow.shape, F32),
        pltpu.VMEM(field, F32),
        *[pltpu.VMEM(c.shape, c.dtype) for c in consts],
        pltpu.VMEM((2, 2 * nx * ny, nx * ny), BF16),
        pltpu.VMEM((2, nz, nz), BF16),
        pltpu.VMEM(field, F32),
        pltpu.VMEM(field, F32),
        pltpu.VMEM(field, F32),
        pltpu.VMEM((3, *field), F32),
        pltpu.VMEM((3, 1, *field), F32),
        pltpu.VMEM((3, 2, *field), F32),
        pltpu.VMEM((3, *field), F32),
        pltpu.VMEM((1, *field), F32),
        pltpu.VMEM((4, STRIPS, nz), F32),
        pltpu.VMEM((POINTS, nz), F32),
        pltpu.VMEM((POINTS, nz), F32),
        pltpu.VMEM((3, POINTS, nz), F32),
        pltpu.VMEM((POINTS, nz), F32),
        pltpu.VMEM((2, POINTS, nz), F32),
        pltpu.VMEM((2, POINTS, nz), F32),
        pltpu.VMEM((2, 16, nz), F32),
        pltpu.VMEM((8, 128), F32),
        pltpu.VMEM((n_vert, 128), F32),
        pltpu.VMEM((n_stream, 128), F32),
        pltpu.SemaphoreType.DMA((3 + len(consts),)),
        pltpu.SemaphoreType.DMA((7, 8)),
        pltpu.SemaphoreType.DMA((7, 8)),
        pltpu.SemaphoreType.DMA((2, 8)),
        pltpu.SemaphoreType.DMA((2, 8)),
        pltpu.SemaphoreType.DMA((2,)),
        pltpu.SemaphoreType.DMA((2,)),
    ]
    for count in FIELDS:
        scratch += [
            pltpu.VMEM((2, count, ny, nz), F32),
            pltpu.VMEM((2, count, nx, 8, nz), F32),
            pltpu.VMEM((2, count, ny, nz), F32),
        ]
    pieces = pl.pallas_call(
        functools.partial(kernel, n_stream, n_vert),
        out_shape=(
            pltpu.VMEM((3, *field), F32),
            pltpu.VMEM((3, 3, *field), F32),
            pltpu.VMEM((3, *field), F32),
            pltpu.VMEM((8, nz), F32),
        ),
        in_specs=[pl.BlockSpec(memory_space=pl.ANY)] * len(operands),
        out_specs=tuple([pl.BlockSpec(memory_space=pltpu.VMEM)] * 4),
        scratch_shapes=scratch,
        compiler_params=pltpu.CompilerParams(
            collective_id=0, has_side_effects=True, vmem_limit_bytes=48 * 1024 * 1024
        ),
    )(*[pltpu.with_memory_space_constraint(a, pltpu.HBM) for a in operands])
    return pl.pallas_call(
        combine,
        out_shape=(
            pltpu.HBM(base_flow.shape, F32),
            pltpu.HBM(field, F32),
        ),
        in_specs=[pl.BlockSpec(memory_space=pltpu.VMEM)] * 4,
        out_specs=tuple([pl.BlockSpec(memory_space=pl.ANY)] * 2),
        scratch_shapes=[
            pltpu.VMEM(base_flow.shape, F32),
            pltpu.VMEM(field, F32),
            pltpu.SemaphoreType.DMA((4,)),
        ],
        compiler_params=pltpu.CompilerParams(vmem_limit_bytes=16 * 1024 * 1024),
    )(*[pltpu.with_memory_space_constraint(a, pltpu.VMEM) for a in pieces])


def solution(mesh):
    placed = (
        P(None, "stream", "vert", None),
        P(None, "stream", "vert", None),
        P("stream", "vert", None),
    )
    return jax.shard_map(
        functools.partial(on_device, mesh.shape["stream"], mesh.shape["vert"]),
        mesh=mesh,
        in_specs=placed,
        out_specs=(P(None, "stream", "vert", None), P("stream", "vert", None)),
        check_vma=False,
    )
```

```python
import functools

import jax
import jax.numpy as jnp
import ml_dtypes
import numpy as np
from jax import lax
from jax.experimental import pallas as pl
from jax.experimental.pallas import tpu as pltpu
from jax.sharding import PartitionSpec as P

time_step = 0.05
MESH = pl.DeviceIdType.MESH
F32 = jnp.float32
BF16 = jnp.bfloat16
SIDES = ((1, 0), (-1, 0), (0, 1), (0, -1), (1, 1), (1, -1), (-1, 1), (-1, -1))
FIELDS = (3, 1, 1, 1, 2, 1)
X_UP, X_DOWN, Y_UP, Y_DOWN, CORNERS, POINTS, STRIPS = 0, 16, 32, 48, 64, 80, 128


def gll_tables():
    degree = 7
    inner_nodes = np.array([0.8717401485096066, 0.5917001814331423, 0.2092992179024789])
    points_ref = np.concatenate([[-1.0], -inner_nodes, inner_nodes[::-1], [1.0]])
    previous = np.ones(8)
    current = points_ref.copy()
    for order_now in range(1, degree):
        following = ((2 * order_now + 1) * points_ref * current - order_now * previous) / (
            order_now + 1
        )
        previous = current
        current = following
    quadrature = 2.0 / (degree * (degree + 1) * current**2)
    derivative_table = np.zeros((8, 8))
    for i in range(8):
        for j in range(8):
            if i != j:
                derivative_table[i, j] = current[i] / (current[j] * (points_ref[i] - points_ref[j]))
    derivative_table[0, 0] = -degree * (degree + 1) / 4.0
    derivative_table[7, 7] = degree * (degree + 1) / 4.0
    return (derivative_table, quadrature)


def halves(matrix):
    high = matrix.astype(np.float32).astype(ml_dtypes.bfloat16)
    low = (matrix - high.astype(np.float64)).astype(ml_dtypes.bfloat16)
    return np.stack([high, low])


def constants(nx, ny, nz):
    table, quad = gll_tables()
    table = table.astype(np.float32).astype(np.float64)
    quad = quad.astype(np.float32).astype(np.float64)
    turned = table.T * quad[None, :] / quad[:, None]
    stiff = turned @ table
    eye = np.eye

    def along_x(m):
        return np.kron(np.kron(eye(nx // 8), m), eye(ny))

    def along_y(m):
        return np.kron(eye(nx * ny // 8), m)

    def along_z(m):
        return np.kron(eye(nz // 8), m.T)

    weights = (
        np.tile(quad, nx // 8)[:, None, None]
        * np.tile(quad, ny // 8)[None, :, None]
        * np.tile(quad, nz // 8)[None, None, :]
    ).astype(np.float32)
    twice = np.array([2.0, 1, 1, 1, 1, 1, 1, 2.0])
    mult = (
        np.tile(twice, nx // 8)[:, None, None]
        * np.tile(twice, ny // 8)[None, :, None]
        * np.tile(twice, nz // 8)[None, None, :]
    )
    ghost_rhs = ghost_matrices(turned)
    points = np.zeros(POINTS, np.int64)
    points[X_UP:X_UP + 16] = (nx - 1) * ny + np.arange(ny)
    points[X_DOWN:X_DOWN + 16] = np.arange(ny)
    points[Y_UP:Y_UP + 16] = np.arange(nx) * ny + ny - 1
    points[Y_DOWN:Y_DOWN + 16] = np.arange(nx) * ny
    for sx in (1, -1):
        for sy in (1, -1):
            points[corner_row(sx, sy)] = ((nx - 1) * ny if sx > 0 else 0) + (ny - 1 if sy > 0 else 0)
    ghost_weights = np.zeros((POINTS, nz), np.float32)
    for top, face in ((X_UP, weights[0]), (X_DOWN, weights[-1]), (Y_UP, weights[:, 0]), (Y_DOWN, weights[:, -1])):
        ghost_weights[top:top + 16] = face
    ghost_weights[CORNERS:CORNERS + 4] = weights[0, 0]
    first = np.zeros((nx, nz))
    for r in range(nx):
        first[r] = np.tile(np.repeat(table[r % 8], ny), nx // 8) * (np.arange(nz) // 128 == r // 8)
    across = np.tile(quad[:, None] * quad[None, :], (1, nz // 8))
    return [
        np.concatenate(
            [np.tile(table.T, (1, nz // 8)), np.tile(table, (1, nz // 8)), first, across, 1.0 / mult[1, :8]]
        ).astype(np.float32),
        halves(np.concatenate([along_x(turned), along_y(turned)], axis=1)),
        halves(along_z(turned)),
        halves(along_x(stiff) + along_y(stiff)),
        halves(along_z(stiff)),
        halves(np.concatenate([ghost_rhs[0], ghost_rhs[1]], axis=1)),
        halves(ghost_matrices(stiff).sum(axis=0)),
        halves(np.concatenate([along_x(turned), along_y(turned)], axis=1)[points]),
        halves((along_x(stiff) + along_y(stiff))[points]),
        ghost_weights,
    ]


def corner_row(sx, sy):
    return CORNERS + (0 if sx > 0 else 2) + (0 if sy > 0 else 1)


def strip_row(kind, sx, sy):
    if kind in ("x", "y"):
        return POINTS + 2 * (corner_row(sx, sy) - CORNERS) + (kind == "y")
    if kind == "cx":
        return POINTS + 8 + 2 * (sx < 0) + (sy < 0)
    return POINTS + 12 + 2 * (sy < 0) + (sx < 0)


def ghost_matrices(m):
    along = np.zeros((2, POINTS, STRIPS))
    blocks = np.kron(np.eye(2), m)
    for sign in (1, -1):
        node = 0 if sign > 0 else 7
        top_x, top_y = (X_UP, Y_UP) if sign > 0 else (X_DOWN, Y_DOWN)
        for r in range(16):
            along[0, top_x + r, top_x + r] += m[node, node]
            along[1, top_x + r, top_x:top_x + 16] += blocks[r]
            along[1, top_y + r, top_y + r] += m[node, node]
            along[0, top_y + r, top_y:top_y + 16] += blocks[r]
        for side in (1, -1):
            r = 15 if side > 0 else 0
            along[0, top_x + r, strip_row("x", sign, side)] += 1.0
            along[0, top_y + r, strip_row("y", side, sign)] += 1.0
            along[0, corner_row(sign, side), strip_row("cx", sign, side)] += 1.0
            along[0, corner_row(side, sign), strip_row("cy", side, sign)] += 1.0
            along[0, corner_row(sign, side), corner_row(sign, side)] += m[node, node]
            along[1, corner_row(side, sign), corner_row(side, sign)] += m[node, node]
    return along


def split(value):
    high = value.astype(BF16)
    low = (value - high.astype(F32)).astype(BF16)
    return high, low


def dot(a, b):
    return jnp.dot(a, b, preferred_element_type=F32)


def left(matrix, parts):
    high, low = parts
    return dot(
        jnp.concatenate([matrix[0], matrix[0], matrix[1]], axis=1),
        jnp.concatenate([high, low, high], axis=0),
    )


def right(parts, matrix):
    high, low = parts
    return dot(
        jnp.concatenate([high, low, high], axis=1),
        jnp.concatenate([matrix[0], matrix[0], matrix[1]], axis=0),
    )


def kernel(
    n_stream,
    n_vert,
    base_h, adj_h, reac_h, tab_h, cxy_h, cz_h, bxy_h, bz_h,
    gc_h, gb_h, cf_h, bf_h, gw_h,
    moved, asm, vec, coef,
    base, adj, reac, tab, cxy, cz, bxy, bz, gc, gb, cf, bf, gw, kxy, kz, wts, imult,
    imass, conv, loc, raw, part3,
    own, strips, ghost_reac, extra, mine, mine_reac, outbox, inbox, strip_out, tiles, red_a, red_b,
    in_sem, send_sem, recv_sem, strip_send, strip_recv, red_send, red_recv,
    *halo,
):
    me_s = lax.axis_index("stream")
    me_v = lax.axis_index("vert")
    nx, ny, nz = reac.shape
    rows = nx * ny

    inputs = [
        (tab_h, tab), (adj_h, adj), (base_h, base),
        (cf_h, cf), (cz_h, cz), (gw_h, gw), (cxy_h, cxy), (reac_h, reac), (gc_h, gc),
        (bxy_h, bxy), (bz_h, bz), (bf_h, bf), (gb_h, gb),
    ]
    loads = [pltpu.make_async_copy(a, b, in_sem.at[i]) for i, (a, b) in enumerate(inputs)]
    for load in loads[:3]:
        load.start()

    def near(ds, dv):
        return (lax.rem(me_s + ds + n_stream, n_stream), lax.rem(me_v + dv + n_vert, n_vert))

    strips[...] = jnp.zeros_like(strips)
    ghost_reac[...] = jnp.zeros_like(ghost_reac)
    inbox[...] = jnp.zeros_like(inbox)
    mine[:, CORNERS + 4:, :] = jnp.zeros((3, POINTS - CORNERS - 4, nz), F32)
    mine_reac[CORNERS + 4:, :] = jnp.zeros((POINTS - CORNERS - 4, nz), F32)

    barrier = pltpu.get_barrier_semaphore()
    partners = [near(ds, dv) for ds, dv in SIDES]
    partners += [near(0, k) for k in range(1, n_vert)]
    partners += [near(k, 0) for k in range(1, n_stream)]
    for partner in partners:
        pl.semaphore_signal(barrier, inc=1, device_id=partner, device_id_type=MESH)

    has_xl = me_s > 0
    has_xh = me_s < n_stream - 1
    has_yl = me_v > 0
    has_yh = me_v < n_vert - 1

    def exists(ds, dv):
        conditions = []
        if ds:
            conditions.append(has_xh if ds > 0 else has_xl)
        if dv:
            conditions.append(has_yh if dv > 0 else has_yl)
        return functools.reduce(jnp.logical_and, conditions)

    def flat(ref):
        return ref[...].reshape(rows, nz)

    lane = lax.broadcasted_iota(jnp.int32, (ny, nz), 1) % 8
    sub = lax.broadcasted_iota(jnp.int32, (8, nz), 0)
    row = lax.broadcasted_iota(jnp.int32, (ny, nz), 0)

    def fold_store(value, ref):
        for i in range(nx):
            v = value[i * ny:(i + 1) * ny]
            up = pltpu.roll(v, nz - 1, 1)
            down = pltpu.roll(v, 1, 1)
            ref[i] = v + jnp.where(lane == 7, up, 0.0) + jnp.where(lane == 0, down, 0.0)
        both = ref[7] + ref[8]
        ref[7] = both
        ref[8] = both
        both = ref[:, 7:8, :] + ref[:, 8:9, :]
        ref[:, 7:8, :] = both
        ref[:, 8:9, :] = both

    def copies(e, src):
        xs, ys, cs = halo[3 * e:3 * e + 3]
        made = []
        for n, (ds, dv) in enumerate(SIDES):
            if dv == 0:
                a = src.at[:, nx - 1 if ds > 0 else 0]
                b = xs.at[0 if ds > 0 else 1]
            else:
                at = pl.ds(ny - 1 if dv > 0 else 0, 1)
                if ds == 0:
                    a = src.at[:, :, at, :]
                    b = ys.at[0 if dv > 0 else 1].at[:, :, pl.ds(0 if dv > 0 else 7, 1), :]
                else:
                    a = src.at[:, nx - 1 if ds > 0 else 0, at, :]
                    b = cs.at[0 if ds > 0 else 1].at[:, pl.ds(0 if dv > 0 else ny - 1, 1), :]
            made.append(
                pltpu.make_async_remote_copy(
                    src_ref=a, dst_ref=b,
                    send_sem=send_sem.at[e, n], recv_sem=recv_sem.at[e, n],
                    device_id=near(ds, dv), device_id_type=MESH,
                )
            )
        for copy, (ds, dv) in zip(made, SIDES):
            pl.when(exists(ds, dv))(copy.start)
        return [[copy] for copy in made]

    def strip_copies(pair, field_x, field_y, scale, m, which):
        def slope(node):
            return [0.0 if j == node else float(m[node, j]) for j in range(8)]

        columns = {}
        for node in (0, 7):
            factors = jnp.zeros((8, nz), F32)
            for j, c in enumerate(slope(node)):
                factors = jnp.where(sub == j, c, factors)
            columns[node] = factors

        def part(field, x, ys):
            value = field[x, ys, :]
            return value * imass[x, ys, :] if scale else value

        def sum_x(sx, start, y):
            terms = [c * part(field_x, start + j, slice(y, y + 1)) for j, c in enumerate(slope(0 if sx > 0 else 7)) if c]
            return functools.reduce(jnp.add, terms)

        def sum_y(sy, x, start):
            tile = columns[0 if sy > 0 else 7] * part(field_y, x, slice(start, start + 8))
            return jnp.sum(tile, axis=0, keepdims=True)

        made = []
        for n, (ds, dv) in enumerate(SIDES):
            here_x, here_y = (nx - 1 if ds > 0 else 0), (ny - 1 if dv > 0 else 0)
            start_x, start_y = (nx - 8 if ds > 0 else 0), (ny - 8 if dv > 0 else 0)
            if dv == 0:
                first = strip_row("cx", -ds, 1)
                two = [sum_x(-ds, start_x, ny - 1), sum_x(-ds, start_x, 0)]
            elif ds == 0:
                first = strip_row("cy", 1, -dv)
                two = [sum_y(-dv, nx - 1, start_y), sum_y(-dv, 0, start_y)]
            else:
                first = strip_row("x", -ds, -dv)
                two = [sum_x(-ds, start_x, here_y), sum_y(-dv, here_x, start_y)]
            at = first - POINTS
            for k in (0, 1):
                strip_out[pair, at + k:at + k + 1, :] = two[k]
            made.append([
                pltpu.make_async_remote_copy(
                    src_ref=strip_out.at[pair, pl.ds(at, 2), :], dst_ref=strips.at[which, pl.ds(first, 2), :],
                    send_sem=strip_send.at[pair, n], recv_sem=strip_recv.at[pair, n],
                    device_id=near(ds, dv), device_id_type=MESH,
                )
            ])
        return launch(made)

    def reaction_copies():
        made = []
        for n, (ds, dv) in enumerate(SIDES):
            here_x, here_y = (nx - 1 if ds > 0 else 0), (ny - 1 if dv > 0 else 0)
            if dv == 0:
                src, at, size = reac.at[here_x], (X_UP if ds < 0 else X_DOWN), 16
            elif ds == 0:
                src, at, size = reac.at[:, here_y, :], (Y_UP if dv < 0 else Y_DOWN), 16
            else:
                src, at, size = reac.at[here_x, pl.ds(here_y, 1), :], corner_row(-ds, -dv), 1
            made.append([
                pltpu.make_async_remote_copy(
                    src_ref=src, dst_ref=ghost_reac.at[pl.ds(at, size), :],
                    send_sem=send_sem.at[6, n], recv_sem=recv_sem.at[6, n],
                    device_id=near(ds, dv), device_id_type=MESH,
                )
            ])
        return launch(made)

    def launch(made):
        for group, (ds, dv) in zip(made, SIDES):
            @pl.when(bool(group) and exists(ds, dv))
            def _(group=group):
                for copy in group:
                    copy.start()
        return made

    def arrive(made):
        for group, (ds, dv) in zip(made, SIDES):
            @pl.when(bool(group) and exists(-ds, -dv))
            def _(group=group):
                for copy in group:
                    copy.wait_recv()

    def leave(made):
        for group, (ds, dv) in zip(made, SIDES):
            @pl.when(bool(group) and exists(ds, dv))
            def _(group=group):
                for copy in group:
                    copy.wait_send()

    def with_halo(e, f, src, i, more=False):
        xs, ys, cs = halo[3 * e:3 * e + 3]
        if more:
            low, high = extra[Y_DOWN + i:Y_DOWN + i + 1], extra[Y_UP + i:Y_UP + i + 1]
        else:
            low, high = ys[0, f, i], ys[1, f, i]
        low = src[f, i, 0:8, :] + jnp.where((sub == 0) & has_yl, low, 0.0)
        high = src[f, i, ny - 8:ny, :] + jnp.where((sub == 7) & has_yh, high, 0.0)
        value = jnp.concatenate([low, high], axis=0)
        if i in (0, nx - 1):
            side = 0 if i == 0 else 1
            sx = -1 if i == 0 else 1
            there = has_xl if i == 0 else has_xh
            known = ((row == 0) & has_yl) | ((row == ny - 1) & has_yh)
            if more:
                top = X_UP if sx > 0 else X_DOWN
                below, above = corner_row(sx, -1), corner_row(sx, 1)
                face = extra[top:top + 16]
                corner = jnp.where(row == 0, extra[below:below + 1], extra[above:above + 1])
            else:
                face, corner = xs[side, f], cs[side, f]
            value = value + jnp.where(there, face + jnp.where(known, corner, 0.0), 0.0)
        return value

    def ghost_points(e, f, value, i, which, scale=None):
        xs, ys, cs = halo[3 * e:3 * e + 3]

        def put(at, size, mine, theirs, weight, there):
            rest = mine - theirs
            if scale is not None:
                rest = rest * weight
            strips[which, at:at + size, :] = jnp.where(there, rest, 0.0)

        by = [None] * 3 if scale is None else [scale, scale[0:1], scale[ny - 1:ny]]
        put(Y_DOWN + i, 1, value[0:1], ys[0, f, i, 0:1, :], by[1], has_yl)
        put(Y_UP + i, 1, value[ny - 1:ny], ys[1, f, i, 7:8, :], by[2], has_yh)
        if i in (0, nx - 1):
            side = 0 if i == 0 else 1
            sx = -1 if i == 0 else 1
            there = has_xl if i == 0 else has_xh
            put(X_UP if sx > 0 else X_DOWN, 16, value, xs[side, f], by[0], there)
            put(corner_row(sx, -1), 1, value[0:1], cs[side, f, 0:1, :], by[1], there & has_yl)
            put(corner_row(sx, 1), 1, value[ny - 1:ny], cs[side, f, ny - 1:ny, :], by[2], there & has_yh)

    lane_p = lax.broadcasted_iota(jnp.int32, (POINTS, nz), 1) % 8
    row_p = lax.broadcasted_iota(jnp.int32, (POINTS, nz), 0)

    def fold_points(value, dst):
        up = pltpu.roll(value, nz - 1, 1)
        down = pltpu.roll(value, 1, 1)
        value = value + jnp.where(lane_p == 7, up, 0.0) + jnp.where(lane_p == 0, down, 0.0)
        up = pltpu.roll(value, POINTS - 1, 0)
        down = pltpu.roll(value, 1, 0)
        on_face = row_p < CORNERS
        dst[...] = (
            value
            + jnp.where(on_face & (row_p % 16 == 7), up, 0.0)
            + jnp.where(on_face & (row_p % 16 == 8), down, 0.0)
        )

    def gather(src, dst):
        dst[X_UP:X_UP + 16, :] = src[nx - 1]
        dst[X_DOWN:X_DOWN + 16, :] = src[0]
        for i in range(nx):
            dst[Y_UP + i:Y_UP + i + 1, :] = src[i, ny - 1:ny, :]
            dst[Y_DOWN + i:Y_DOWN + i + 1, :] = src[i, 0:1, :]
        for sx in (1, -1):
            for sy in (1, -1):
                at, y = corner_row(sx, sy), (ny - 1 if sy > 0 else 0)
                dst[at:at + 1, :] = src[nx - 1 if sx > 0 else 0, y:y + 1, :]

    def point_copies(pair, e):
        made = []
        for n, (ds, dv) in enumerate(SIDES):
            if dv == 0:
                a, b, size = (X_UP, X_DOWN, 16) if ds > 0 else (X_DOWN, X_UP, 16)
            elif ds == 0:
                a, b, size = (Y_UP, Y_DOWN, 16) if dv > 0 else (Y_DOWN, Y_UP, 16)
            else:
                a, b, size = corner_row(ds, dv), corner_row(-ds, -dv), 1
            made.append([
                pltpu.make_async_remote_copy(
                    src_ref=outbox.at[pair, pl.ds(a, size), :], dst_ref=inbox.at[pair, pl.ds(b, size), :],
                    send_sem=send_sem.at[e, n], recv_sem=recv_sem.at[e, n],
                    device_id=near(ds, dv), device_id_type=MESH,
                )
            ])
        return launch(made)

    def operate(value, parts):
        return wts[...].reshape(rows, nz) * (
            left(bxy, parts) + right(parts, bz) + flat(reac) * value
        )

    def slopes(parts, k):
        both = left(kxy, parts)
        raw[k, 0] = both[:rows].reshape(nx, ny, nz)
        raw[k, 1] = both[rows:].reshape(nx, ny, nz)
        third = right(parts, kz)
        for i in range(nx):
            v = third[i * ny:(i + 1) * ny]
            other = jnp.where(lane == 7, pltpu.roll(v, nz - 1, 1), pltpu.roll(v, 1, 1))
            asm[k, 2, i] = jnp.where((lane == 7) | (lane == 0), 0.5 * (v + other), v)

    def slope_copies(e, first, count):
        xs, ys = halo[3 * e:3 * e + 2]
        made = []
        for n, (ds, dv) in enumerate(SIDES):
            group = []
            if ds * dv == 0:
                some = pl.ds(first, count)
                if dv == 0:
                    a = raw.at[some, 0, nx - 1 if ds > 0 else 0]
                    b = xs.at[0 if ds > 0 else 1]
                else:
                    a = raw.at[some, 1, :, pl.ds(ny - 1 if dv > 0 else 0, 1), :]
                    b = ys.at[0 if dv > 0 else 1].at[:, :, pl.ds(0 if dv > 0 else 7, 1), :]
                group.append(
                    pltpu.make_async_remote_copy(
                        src_ref=a, dst_ref=b,
                        send_sem=send_sem.at[e, n], recv_sem=recv_sem.at[e, n],
                        device_id=near(ds, dv), device_id_type=MESH,
                    )
                )
            made.append(group)
        return launch(made)

    def average(e, f, k):
        xs, ys = halo[3 * e:3 * e + 2]
        middle = 0.5 * (raw[k, 0, 7] + raw[k, 0, 8])
        for i in range(nx):
            v = raw[k, 0, i]
            if i in (7, 8):
                v = middle
            elif i == 0:
                v = jnp.where(has_xl, 0.5 * (v + xs[0, f]), v)
            elif i == nx - 1:
                v = jnp.where(has_xh, 0.5 * (v + xs[1, f]), v)
            asm[k, 0, i] = v
            v = raw[k, 1, i]
            other = jnp.concatenate([ys[0, f, i], ys[1, f, i]], axis=0)
            other = jnp.where(row == 7, pltpu.roll(v, ny - 1, 0), other)
            other = jnp.where(row == 8, pltpu.roll(v, 1, 0), other)
            shared = (row == 7) | (row == 8) | ((row == 0) & has_yl) | ((row == ny - 1) & has_yh)
            asm[k, 1, i] = jnp.where(shared, 0.5 * (v + other), v)

    def to_row(value, slot):
        s = value.reshape(rows // 8, 8, nz).sum(axis=0)
        s = s[:, :128] + s[:, 128:]
        tiles[slot:slot + 1, :] = jnp.sum(s, axis=0, keepdims=True)

    table, quad = gll_tables()
    turned = table.T * quad[None, :] / quad[:, None]
    stiff = turned @ table
    loads[0].wait()
    column = lax.broadcasted_iota(jnp.int32, (ny, nz), 1)

    def put_block(dst, at, mask, tile):
        high = tile.astype(BF16).astype(F32)
        dst[0, at:at + ny, :] = jnp.where(mask, high, 0.0).astype(BF16)
        dst[1, at:at + ny, :] = jnp.where(mask, tile - high, 0.0).astype(BF16)

    tile_z = jnp.concatenate([tab[0:8], tab[0:8]], axis=0)
    tile_y = jnp.concatenate([tab[8:16], tab[8:16]], axis=0)
    tile_w = jnp.concatenate([tab[32:40], tab[32:40]], axis=0)
    tile_m = jnp.concatenate([tab[40:48], tab[40:48]], axis=0)
    edge = ((row == 0) & (me_v == 0)) | ((row == ny - 1) & (me_v == n_vert - 1))
    tile_m = tile_m * jnp.where(edge, 2.0, 1.0)
    for i in range(nx):
        here = column // 8 == 2 * i + row // 8
        put_block(kz, i * ny, here, tile_z)
        put_block(kxy, rows + i * ny, here, tile_y)
        put_block(kxy, i * ny, column % ny == row, jnp.broadcast_to(tab[16 + i:17 + i], (ny, nz)))
        wts[i] = tile_w * float(quad[i % 8])
        value = tile_m
        if i in (0, nx - 1):
            value = value * jnp.where((me_s == 0) if i == 0 else (me_s == n_stream - 1), 1.0, 0.5)
        elif i % 8 in (0, 7):
            value = value * 0.5
        imult[i] = value
        imass[i] = time_step * value / wts[i]

    loads[1].wait()
    gather(adj.at[2], mine.at[1])
    gather(imass, mine.at[2])
    for c in range(3):
        parts = split(flat(adj.at[c]))
        both = left(kxy, parts)
        third = right(parts, kz)
        if c == 0:
            loads[2].wait()
            for load in loads[3:]:
                load.start()
        conv[c] = (
            flat(base.at[0]) * both[:rows] + flat(base.at[1]) * both[rows:] + flat(base.at[2]) * third
        ).reshape(nx, ny, nz)
    for j in range(3):
        parts = split(flat(base.at[j]))
        a = flat(adj.at[j])
        both = left(kxy, parts)
        conv[0] -= (a * both[:rows]).reshape(nx, ny, nz)
        conv[1] -= (a * both[rows:]).reshape(nx, ny, nz)
        conv[2] -= (a * right(parts, kz)).reshape(nx, ny, nz)
    for c in range(3):
        fold_store(flat(conv.at[c]) * flat(wts), part3.at[c])
    pl.semaphore_wait(barrier, len(partners))
    sends = [copies(0, part3), strip_copies(0, part3.at[0], part3.at[1], True, turned, 0)]

    def right_side(fields):
        pair = jnp.concatenate([fields[0], fields[1]], axis=0)
        return flat(wts) * (left(cxy, split(pair)) + right(split(fields[2]), cz))

    for load in loads[3:6]:
        load.wait()
    gather(part3.at[2], mine.at[0])
    pair = jnp.concatenate([flat(adj.at[c]) + flat(imass) * flat(part3.at[c]) for c in (0, 1)], axis=0)
    third = mine[1] + mine[2] * mine[0]
    fold_points(gw[...] * (left(cf, split(pair)) + right(split(third), cz)), outbox.at[0])
    sends.append(point_copies(0, 1))
    for load in loads[6:]:
        load.wait()
    sends.append(reaction_copies())
    gather(reac, mine_reac)

    arrive(sends[0])
    for c in range(3):
        for i in range(nx):
            value = with_halo(0, c, part3, i)
            moved[c, i] = adj[c, i] + value * imass[i]
            ghost_points(0, c, value, i, c, imass[i])
    fold_store(right_side([flat(moved.at[c]) for c in range(3)]), own.at[0])
    arrive(sends[1])
    ghosts = jnp.concatenate([strips[0], strips[1]], axis=0)
    fold_points(gw[...] * (left(gc, split(ghosts)) + right(split(strips[2, 0:POINTS, :]), cz)), extra)
    arrive(sends[2])
    extra[...] = extra[...] + inbox[0]
    for i in range(nx):
        vec[0, i] = with_halo(1, 0, own, i, True)

    v = flat(vec.at[0])
    parts = split(v)
    image = operate(v, parts)
    fold_store(image, loc.at[1].at[0])
    sends += [copies(2, loc.at[1]), strip_copies(1, loc.at[1].at[0], loc.at[1].at[0], False, stiff, 3)]
    first = flat(loc.at[1].at[0])
    gather(loc.at[1].at[0], mine.at[0])
    points = mine[0]
    fold_points(
        gw[...] * (left(bf, split(first)) + right(split(points), bz) + mine_reac[...] * points), outbox.at[1]
    )
    sends.append(point_copies(1, 3))
    to_row(v * v * flat(imult), 0)
    to_row(v * image, 1)
    slopes(parts, 0)
    sends.append(slope_copies(5, 0, 1))
    arrive(sends[3])
    arrive(sends[4])
    for i in range(nx):
        value = with_halo(2, 0, loc.at[1], i)
        vec[1, i] = value
        ghost_points(2, 0, value, i, 3)

    v = flat(vec.at[1])
    parts = split(v)
    image = operate(v, parts)
    fold_store(image, own.at[0])
    arrive(sends[5])
    points = strips[3, 0:POINTS, :]
    fold_points(
        gw[...] * (left(gb, split(strips[3])) + right(split(points), bz) + ghost_reac[...] * points), extra
    )
    to_row(v * v * flat(imult), 2)
    to_row(v * image, 3)
    arrive(sends[6])
    extra[...] = extra[...] + inbox[1]
    for i in range(nx):
        vec[2, i] = with_halo(3, 0, own, i, True)

    v = flat(vec.at[2])
    parts = split(v)
    image = operate(v, parts)
    to_row(v * v * flat(imult), 4)
    to_row(v * image, 5)

    tiles[6:8, :] = jnp.zeros((2, 128), F32)
    group = lax.broadcasted_iota(jnp.int32, (8, 128), 1) // 16
    packed = tiles[...]
    for shift in (64, 32, 16):
        packed = packed + pltpu.roll(packed, shift, 1)
    packed = jnp.where(group == lax.broadcasted_iota(jnp.int32, (8, 128), 0), packed, 0.0)
    red_a[n_vert - 1:n_vert, :] = jnp.sum(packed, axis=0, keepdims=True)

    def spread(slots, n, which):
        for k in range(1, n):
            pltpu.make_async_remote_copy(
                src_ref=slots.at[pl.ds(n - 1, 1)], dst_ref=slots.at[pl.ds(k - 1, 1)],
                send_sem=red_send.at[which], recv_sem=red_recv.at[which],
                device_id=near(0, k) if which == 0 else near(k, 0), device_id_type=MESH,
            ).start()

    def whole(slots, n, which):
        return pltpu.make_async_remote_copy(
            src_ref=slots.at[pl.ds(0, n - 1)], dst_ref=slots.at[pl.ds(0, n - 1)],
            send_sem=red_send.at[which], recv_sem=red_recv.at[which],
            device_id=near(0, 1), device_id_type=MESH,
        )

    spread(red_a, n_vert, 0)
    slopes(split(flat(vec.at[1])), 1)
    slopes(parts, 2)
    sends.append(slope_copies(4, 1, 2))
    whole(red_a, n_vert, 0).wait_recv()
    red_b[n_stream - 1:n_stream, :] = jnp.sum(red_a[...], axis=0, keepdims=True)
    spread(red_b, n_stream, 1)

    arrive(sends[7])
    average(5, 0, 0)
    arrive(sends[8])
    average(4, 0, 1)
    average(4, 1, 2)

    for made in sends:
        leave(made)
    whole(red_a, n_vert, 0).wait_send()
    whole(red_b, n_stream, 1).wait_recv()
    total = jnp.sum(red_b[...], axis=0, keepdims=True)
    m = [jnp.sum(jnp.where(group[0:1] == k, total, 0.0), axis=1, keepdims=True) for k in range(6)]
    a0 = m[0] / m[1]
    r1 = a0 * a0 * m[2] - m[0]
    k1 = 1.0 + r1 / m[0]
    p1 = k1 * k1 * m[1] - 2.0 * k1 * a0 * m[2] + a0 * a0 * m[3]
    a1 = r1 / p1
    e1 = -(a0 + a1 * k1)
    e2 = a1 * a0
    r2 = m[0] + 2.0 * e1 * m[1] + (e1 * e1 + 2.0 * e2) * m[2] + 2.0 * e1 * e2 * m[3] + e2 * e2 * m[4]
    b2 = r2 / r1
    f0 = 1.0 + b2 * k1
    f1 = e1 - b2 * a0
    f2 = e2
    p2 = (
        f0 * f0 * m[1] + 2.0 * f0 * f1 * m[2] + (f1 * f1 + 2.0 * f0 * f2) * m[3]
        + 2.0 * f1 * f2 * m[4] + f2 * f2 * m[5]
    )
    a2 = r2 / p2
    c0 = a0 + a1 * k1 + a2 * f0
    c1 = a2 * f1 - a1 * a0
    c2 = a2 * f2
    for k, c in enumerate((c0, c1, c2)):
        coef[k:k + 1, :] = jnp.broadcast_to(c, (1, nz))
    whole(red_b, n_stream, 1).wait_send()


def combine(moved, asm, vec, coef, out_h, pres_h, out, pres, sems):
    copies = []
    for i in range(pres.shape[0]):
        pres[i] = coef[0:1] * vec[0, i] + coef[1:2] * vec[1, i] + coef[2:3] * vec[2, i]
    copies.append(pltpu.make_async_copy(pres, pres_h, sems.at[3]))
    copies[-1].start()
    for d in range(3):
        for i in range(pres.shape[0]):
            out[d, i] = moved[d, i] - (
                coef[0:1] * asm[0, d, i] + coef[1:2] * asm[1, d, i] + coef[2:3] * asm[2, d, i]
            )
        copies.append(pltpu.make_async_copy(out.at[d], out_h.at[d], sems.at[d]))
        copies[-1].start()
    for copy in copies:
        copy.wait()


def on_device(n_stream, n_vert, base_flow, adjoint_velocity, reaction):
    nx, ny, nz = reaction.shape
    consts = constants(nx, ny, nz)
    field = (nx, ny, nz)
    operands = [base_flow, adjoint_velocity, reaction, *[jnp.asarray(c) for c in consts]]
    scratch = [
        pltpu.VMEM(base_flow.shape, F32),
        pltpu.VMEM(base_flow.shape, F32),
        pltpu.VMEM(field, F32),
        *[pltpu.VMEM(c.shape, c.dtype) for c in consts],
        pltpu.VMEM((2, 2 * nx * ny, nx * ny), BF16),
        pltpu.VMEM((2, nz, nz), BF16),
        pltpu.VMEM(field, F32),
        pltpu.VMEM(field, F32),
        pltpu.VMEM(field, F32),
        pltpu.VMEM((3, *field), F32),
        pltpu.VMEM((3, 1, *field), F32),
        pltpu.VMEM((3, 2, *field), F32),
        pltpu.VMEM((3, *field), F32),
        pltpu.VMEM((1, *field), F32),
        pltpu.VMEM((4, STRIPS, nz), F32),
        pltpu.VMEM((POINTS, nz), F32),
        pltpu.VMEM((POINTS, nz), F32),
        pltpu.VMEM((3, POINTS, nz), F32),
        pltpu.VMEM((POINTS, nz), F32),
        pltpu.VMEM((2, POINTS, nz), F32),
        pltpu.VMEM((2, POINTS, nz), F32),
        pltpu.VMEM((2, 16, nz), F32),
        pltpu.VMEM((8, 128), F32),
        pltpu.VMEM((n_vert, 128), F32),
        pltpu.VMEM((n_stream, 128), F32),
        pltpu.SemaphoreType.DMA((3 + len(consts),)),
        pltpu.SemaphoreType.DMA((7, 8)),
        pltpu.SemaphoreType.DMA((7, 8)),
        pltpu.SemaphoreType.DMA((2, 8)),
        pltpu.SemaphoreType.DMA((2, 8)),
        pltpu.SemaphoreType.DMA((2,)),
        pltpu.SemaphoreType.DMA((2,)),
    ]
    for count in FIELDS:
        scratch += [
            pltpu.VMEM((2, count, ny, nz), F32),
            pltpu.VMEM((2, count, nx, 8, nz), F32),
            pltpu.VMEM((2, count, ny, nz), F32),
        ]
    pieces = pl.pallas_call(
        functools.partial(kernel, n_stream, n_vert),
        out_shape=(
            pltpu.VMEM((3, *field), F32),
            pltpu.VMEM((3, 3, *field), F32),
            pltpu.VMEM((3, *field), F32),
            pltpu.VMEM((8, nz), F32),
        ),
        in_specs=[pl.BlockSpec(memory_space=pl.ANY)] * len(operands),
        out_specs=tuple([pl.BlockSpec(memory_space=pltpu.VMEM)] * 4),
        scratch_shapes=scratch,
        compiler_params=pltpu.CompilerParams(
            collective_id=0, has_side_effects=True, vmem_limit_bytes=48 * 1024 * 1024
        ),
    )(*[pltpu.with_memory_space_constraint(a, pltpu.HBM) for a in operands])
    return pl.pallas_call(
        combine,
        out_shape=(
            pltpu.HBM(base_flow.shape, F32),
            pltpu.HBM(field, F32),
        ),
        in_specs=[pl.BlockSpec(memory_space=pltpu.VMEM)] * 4,
        out_specs=tuple([pl.BlockSpec(memory_space=pl.ANY)] * 2),
        scratch_shapes=[
            pltpu.VMEM(base_flow.shape, F32),
            pltpu.VMEM(field, F32),
            pltpu.SemaphoreType.DMA((4,)),
        ],
        compiler_params=pltpu.CompilerParams(vmem_limit_bytes=16 * 1024 * 1024),
    )(*[pltpu.with_memory_space_constraint(a, pltpu.VMEM) for a in pieces])


def solution(mesh):
    placed = (
        P(None, "stream", "vert", None),
        P(None, "stream", "vert", None),
        P("stream", "vert", None),
    )
    return jax.shard_map(
        functools.partial(on_device, mesh.shape["stream"], mesh.shape["vert"]),
        mesh=mesh,
        in_specs=placed,
        out_specs=(P(None, "stream", "vert", None), P("stream", "vert", None)),
        check_vma=False,
    )
```

```python
import functools

import jax
import jax.numpy as jnp
import ml_dtypes
import numpy as np
from jax import lax
from jax.experimental import pallas as pl
from jax.experimental.pallas import tpu as pltpu
from jax.sharding import PartitionSpec as P

time_step = 0.05
MESH = pl.DeviceIdType.MESH
F32 = jnp.float32
BF16 = jnp.bfloat16
SIDES = ((1, 0), (-1, 0), (0, 1), (0, -1), (1, 1), (1, -1), (-1, 1), (-1, -1))
FIELDS = (3, 1, 1, 1, 2, 1)
X_UP, X_DOWN, Y_UP, Y_DOWN, CORNERS, POINTS, STRIPS = 0, 16, 32, 48, 64, 80, 128


def gll_tables():
    degree = 7
    inner_nodes = np.array([0.8717401485096066, 0.5917001814331423, 0.2092992179024789])
    points_ref = np.concatenate([[-1.0], -inner_nodes, inner_nodes[::-1], [1.0]])
    previous = np.ones(8)
    current = points_ref.copy()
    for order_now in range(1, degree):
        following = ((2 * order_now + 1) * points_ref * current - order_now * previous) / (
            order_now + 1
        )
        previous = current
        current = following
    quadrature = 2.0 / (degree * (degree + 1) * current**2)
    derivative_table = np.zeros((8, 8))
    for i in range(8):
        for j in range(8):
            if i != j:
                derivative_table[i, j] = current[i] / (current[j] * (points_ref[i] - points_ref[j]))
    derivative_table[0, 0] = -degree * (degree + 1) / 4.0
    derivative_table[7, 7] = degree * (degree + 1) / 4.0
    return (derivative_table, quadrature)


def halves(matrix):
    high = matrix.astype(np.float32).astype(ml_dtypes.bfloat16)
    low = (matrix - high.astype(np.float64)).astype(ml_dtypes.bfloat16)
    return np.stack([high, low])


def constants(nx, ny, nz):
    table, quad = gll_tables()
    table = table.astype(np.float32).astype(np.float64)
    quad = quad.astype(np.float32).astype(np.float64)
    turned = table.T * quad[None, :] / quad[:, None]
    stiff = turned @ table
    eye = np.eye

    def along_x(m):
        return np.kron(np.kron(eye(nx // 8), m), eye(ny))

    def along_y(m):
        return np.kron(eye(nx * ny // 8), m)

    def along_z(m):
        return np.kron(eye(nz // 8), m.T)

    weights = (
        np.tile(quad, nx // 8)[:, None, None]
        * np.tile(quad, ny // 8)[None, :, None]
        * np.tile(quad, nz // 8)[None, None, :]
    ).astype(np.float32)
    twice = np.array([2.0, 1, 1, 1, 1, 1, 1, 2.0])
    mult = (
        np.tile(twice, nx // 8)[:, None, None]
        * np.tile(twice, ny // 8)[None, :, None]
        * np.tile(twice, nz // 8)[None, None, :]
    )
    ghost_rhs = ghost_matrices(turned)
    points = np.zeros(POINTS, np.int64)
    points[X_UP:X_UP + 16] = (nx - 1) * ny + np.arange(ny)
    points[X_DOWN:X_DOWN + 16] = np.arange(ny)
    points[Y_UP:Y_UP + 16] = np.arange(nx) * ny + ny - 1
    points[Y_DOWN:Y_DOWN + 16] = np.arange(nx) * ny
    for sx in (1, -1):
        for sy in (1, -1):
            points[corner_row(sx, sy)] = ((nx - 1) * ny if sx > 0 else 0) + (ny - 1 if sy > 0 else 0)
    ghost_weights = np.zeros((POINTS, nz), np.float32)
    for top, face in ((X_UP, weights[0]), (X_DOWN, weights[-1]), (Y_UP, weights[:, 0]), (Y_DOWN, weights[:, -1])):
        ghost_weights[top:top + 16] = face
    ghost_weights[CORNERS:CORNERS + 4] = weights[0, 0]
    first = np.zeros((nx, nz))
    for r in range(nx):
        first[r] = np.tile(np.repeat(table[r % 8], ny), nx // 8) * (np.arange(nz) // 128 == r // 8)
    across = np.tile(quad[:, None] * quad[None, :], (1, nz // 8))
    return [
        np.concatenate(
            [np.tile(table.T, (1, nz // 8)), np.tile(table, (1, nz // 8)), first, across, 1.0 / mult[1, :8]]
        ).astype(np.float32),
        halves(np.concatenate([along_x(turned), along_y(turned)], axis=1)),
        halves(along_z(turned)),
        halves(along_x(stiff) + along_y(stiff)),
        halves(along_z(stiff)),
        halves(np.concatenate([ghost_rhs[0], ghost_rhs[1]], axis=1)),
        halves(ghost_matrices(stiff).sum(axis=0)),
        halves(np.concatenate([along_x(turned), along_y(turned)], axis=1)[points]),
        halves((along_x(stiff) + along_y(stiff))[points]),
        ghost_weights,
    ]


def corner_row(sx, sy):
    return CORNERS + (0 if sx > 0 else 2) + (0 if sy > 0 else 1)


def strip_row(kind, sx, sy):
    if kind in ("x", "y"):
        return POINTS + 2 * (corner_row(sx, sy) - CORNERS) + (kind == "y")
    if kind == "cx":
        return POINTS + 8 + 2 * (sx < 0) + (sy < 0)
    return POINTS + 12 + 2 * (sy < 0) + (sx < 0)


def ghost_matrices(m):
    along = np.zeros((2, POINTS, STRIPS))
    blocks = np.kron(np.eye(2), m)
    for sign in (1, -1):
        node = 0 if sign > 0 else 7
        top_x, top_y = (X_UP, Y_UP) if sign > 0 else (X_DOWN, Y_DOWN)
        for r in range(16):
            along[0, top_x + r, top_x + r] += m[node, node]
            along[1, top_x + r, top_x:top_x + 16] += blocks[r]
            along[1, top_y + r, top_y + r] += m[node, node]
            along[0, top_y + r, top_y:top_y + 16] += blocks[r]
        for side in (1, -1):
            r = 15 if side > 0 else 0
            along[0, top_x + r, strip_row("x", sign, side)] += 1.0
            along[0, top_y + r, strip_row("y", side, sign)] += 1.0
            along[0, corner_row(sign, side), strip_row("cx", sign, side)] += 1.0
            along[0, corner_row(side, sign), strip_row("cy", side, sign)] += 1.0
            along[0, corner_row(sign, side), corner_row(sign, side)] += m[node, node]
            along[1, corner_row(side, sign), corner_row(side, sign)] += m[node, node]
    return along


def split(value):
    high = value.astype(BF16)
    low = (value - high.astype(F32)).astype(BF16)
    return high, low


def dot(a, b):
    return jnp.dot(a, b, preferred_element_type=F32)


def left(matrix, parts):
    high, low = parts
    return dot(
        jnp.concatenate([matrix[0], matrix[0], matrix[1]], axis=1),
        jnp.concatenate([high, low, high], axis=0),
    )


def right(parts, matrix):
    high, low = parts
    return dot(
        jnp.concatenate([high, low, high], axis=1),
        jnp.concatenate([matrix[0], matrix[0], matrix[1]], axis=0),
    )


def kernel(
    n_stream,
    n_vert,
    base_h, adj_h, reac_h, tab_h, cxy_h, cz_h, bxy_h, bz_h,
    gc_h, gb_h, cf_h, bf_h, gw_h,
    moved, asm, vec, coef,
    base, adj, reac, tab, cxy, cz, bxy, bz, gc, gb, cf, bf, gw, kxy, kz, wts, imult,
    imass, conv, loc, raw, part3,
    own, strips, ghost_reac, extra, mine, mine_reac, outbox, inbox, strip_out, tiles, red_a, red_b,
    in_sem, send_sem, recv_sem, strip_send, strip_recv, red_send, red_recv,
    *halo,
):
    me_s = lax.axis_index("stream")
    me_v = lax.axis_index("vert")
    nx, ny, nz = reac.shape
    rows = nx * ny

    inputs = [
        (tab_h, tab), (adj_h, adj), (base_h, base),
        (cf_h, cf), (cz_h, cz), (gw_h, gw), (cxy_h, cxy), (reac_h, reac), (gc_h, gc),
        (bxy_h, bxy), (bz_h, bz), (bf_h, bf), (gb_h, gb),
    ]
    loads = [pltpu.make_async_copy(a, b, in_sem.at[i]) for i, (a, b) in enumerate(inputs)]
    for load in loads[:3]:
        load.start()

    def near(ds, dv):
        return (lax.rem(me_s + ds + n_stream, n_stream), lax.rem(me_v + dv + n_vert, n_vert))

    strips[...] = jnp.zeros_like(strips)
    ghost_reac[...] = jnp.zeros_like(ghost_reac)
    inbox[...] = jnp.zeros_like(inbox)
    mine[:, CORNERS + 4:, :] = jnp.zeros((3, POINTS - CORNERS - 4, nz), F32)
    mine_reac[CORNERS + 4:, :] = jnp.zeros((POINTS - CORNERS - 4, nz), F32)

    barrier = pltpu.get_barrier_semaphore()
    partners = [near(ds, dv) for ds, dv in SIDES]
    partners += [near(0, k) for k in range(1, n_vert)]
    partners += [near(k, 0) for k in range(1, n_stream)]
    for partner in partners:
        pl.semaphore_signal(barrier, inc=1, device_id=partner, device_id_type=MESH)

    has_xl = me_s > 0
    has_xh = me_s < n_stream - 1
    has_yl = me_v > 0
    has_yh = me_v < n_vert - 1

    def exists(ds, dv):
        conditions = []
        if ds:
            conditions.append(has_xh if ds > 0 else has_xl)
        if dv:
            conditions.append(has_yh if dv > 0 else has_yl)
        return functools.reduce(jnp.logical_and, conditions)

    def flat(ref):
        return ref[...].reshape(rows, nz)

    lane = lax.broadcasted_iota(jnp.int32, (ny, nz), 1) % 8
    sub = lax.broadcasted_iota(jnp.int32, (8, nz), 0)
    row = lax.broadcasted_iota(jnp.int32, (ny, nz), 0)

    def fold_store(value, ref):
        for i in range(nx):
            v = value[i * ny:(i + 1) * ny]
            up = pltpu.roll(v, nz - 1, 1)
            down = pltpu.roll(v, 1, 1)
            ref[i] = v + jnp.where(lane == 7, up, 0.0) + jnp.where(lane == 0, down, 0.0)
        both = ref[7] + ref[8]
        ref[7] = both
        ref[8] = both
        both = ref[:, 7:8, :] + ref[:, 8:9, :]
        ref[:, 7:8, :] = both
        ref[:, 8:9, :] = both

    def copies(e, src):
        xs, ys, cs = halo[3 * e:3 * e + 3]
        made = []
        for n, (ds, dv) in enumerate(SIDES):
            if dv == 0:
                a = src.at[:, nx - 1 if ds > 0 else 0]
                b = xs.at[0 if ds > 0 else 1]
            else:
                at = pl.ds(ny - 1 if dv > 0 else 0, 1)
                if ds == 0:
                    a = src.at[:, :, at, :]
                    b = ys.at[0 if dv > 0 else 1].at[:, :, pl.ds(0 if dv > 0 else 7, 1), :]
                else:
                    a = src.at[:, nx - 1 if ds > 0 else 0, at, :]
                    b = cs.at[0 if ds > 0 else 1].at[:, pl.ds(0 if dv > 0 else ny - 1, 1), :]
            made.append(
                pltpu.make_async_remote_copy(
                    src_ref=a, dst_ref=b,
                    send_sem=send_sem.at[e, n], recv_sem=recv_sem.at[e, n],
                    device_id=near(ds, dv), device_id_type=MESH,
                )
            )
        for copy, (ds, dv) in zip(made, SIDES):
            pl.when(exists(ds, dv))(copy.start)
        return [[copy] for copy in made]

    def strip_copies(pair, field_x, field_y, scale, m, which):
        def slope(node):
            return [0.0 if j == node else float(m[node, j]) for j in range(8)]

        columns = {}
        for node in (0, 7):
            factors = jnp.zeros((8, nz), F32)
            for j, c in enumerate(slope(node)):
                factors = jnp.where(sub == j, c, factors)
            columns[node] = factors

        def part(field, x, ys):
            value = field[x, ys, :]
            return value * imass[x, ys, :] if scale else value

        def sum_x(sx, start, y):
            terms = [c * part(field_x, start + j, slice(y, y + 1)) for j, c in enumerate(slope(0 if sx > 0 else 7)) if c]
            return functools.reduce(jnp.add, terms)

        def sum_y(sy, x, start):
            tile = columns[0 if sy > 0 else 7] * part(field_y, x, slice(start, start + 8))
            return jnp.sum(tile, axis=0, keepdims=True)

        made = []
        for n, (ds, dv) in enumerate(SIDES):
            here_x, here_y = (nx - 1 if ds > 0 else 0), (ny - 1 if dv > 0 else 0)
            start_x, start_y = (nx - 8 if ds > 0 else 0), (ny - 8 if dv > 0 else 0)
            if dv == 0:
                first = strip_row("cx", -ds, 1)
                two = [sum_x(-ds, start_x, ny - 1), sum_x(-ds, start_x, 0)]
            elif ds == 0:
                first = strip_row("cy", 1, -dv)
                two = [sum_y(-dv, nx - 1, start_y), sum_y(-dv, 0, start_y)]
            else:
                first = strip_row("x", -ds, -dv)
                two = [sum_x(-ds, start_x, here_y), sum_y(-dv, here_x, start_y)]
            at = first - POINTS
            for k in (0, 1):
                strip_out[pair, at + k:at + k + 1, :] = two[k]
            made.append([
                pltpu.make_async_remote_copy(
                    src_ref=strip_out.at[pair, pl.ds(at, 2), :], dst_ref=strips.at[which, pl.ds(first, 2), :],
                    send_sem=strip_send.at[pair, n], recv_sem=strip_recv.at[pair, n],
                    device_id=near(ds, dv), device_id_type=MESH,
                )
            ])
        return launch(made)

    def reaction_copies():
        made = []
        for n, (ds, dv) in enumerate(SIDES):
            here_x, here_y = (nx - 1 if ds > 0 else 0), (ny - 1 if dv > 0 else 0)
            if dv == 0:
                src, at, size = reac.at[here_x], (X_UP if ds < 0 else X_DOWN), 16
            elif ds == 0:
                src, at, size = reac.at[:, here_y, :], (Y_UP if dv < 0 else Y_DOWN), 16
            else:
                src, at, size = reac.at[here_x, pl.ds(here_y, 1), :], corner_row(-ds, -dv), 1
            made.append([
                pltpu.make_async_remote_copy(
                    src_ref=src, dst_ref=ghost_reac.at[pl.ds(at, size), :],
                    send_sem=send_sem.at[6, n], recv_sem=recv_sem.at[6, n],
                    device_id=near(ds, dv), device_id_type=MESH,
                )
            ])
        return launch(made)

    def launch(made):
        for group, (ds, dv) in zip(made, SIDES):
            @pl.when(bool(group) and exists(ds, dv))
            def _(group=group):
                for copy in group:
                    copy.start()
        return made

    def arrive(made):
        for group, (ds, dv) in zip(made, SIDES):
            @pl.when(bool(group) and exists(-ds, -dv))
            def _(group=group):
                for copy in group:
                    copy.wait_recv()

    def leave(made):
        for group, (ds, dv) in zip(made, SIDES):
            @pl.when(bool(group) and exists(ds, dv))
            def _(group=group):
                for copy in group:
                    copy.wait_send()

    def with_halo(e, f, src, i, more=False):
        xs, ys, cs = halo[3 * e:3 * e + 3]
        if more:
            low, high = extra[Y_DOWN + i:Y_DOWN + i + 1], extra[Y_UP + i:Y_UP + i + 1]
        else:
            low, high = ys[0, f, i], ys[1, f, i]
        low = src[f, i, 0:8, :] + jnp.where((sub == 0) & has_yl, low, 0.0)
        high = src[f, i, ny - 8:ny, :] + jnp.where((sub == 7) & has_yh, high, 0.0)
        value = jnp.concatenate([low, high], axis=0)
        if i in (0, nx - 1):
            side = 0 if i == 0 else 1
            sx = -1 if i == 0 else 1
            there = has_xl if i == 0 else has_xh
            known = ((row == 0) & has_yl) | ((row == ny - 1) & has_yh)
            if more:
                top = X_UP if sx > 0 else X_DOWN
                below, above = corner_row(sx, -1), corner_row(sx, 1)
                face = extra[top:top + 16]
                corner = jnp.where(row == 0, extra[below:below + 1], extra[above:above + 1])
            else:
                face, corner = xs[side, f], cs[side, f]
            value = value + jnp.where(there, face + jnp.where(known, corner, 0.0), 0.0)
        return value

    def ghost_points(e, f, value, i, which, scale=None):
        xs, ys, cs = halo[3 * e:3 * e + 3]

        def put(at, size, mine, theirs, weight, there):
            rest = mine - theirs
            if scale is not None:
                rest = rest * weight
            strips[which, at:at + size, :] = jnp.where(there, rest, 0.0)

        by = [None] * 3 if scale is None else [scale, scale[0:1], scale[ny - 1:ny]]
        put(Y_DOWN + i, 1, value[0:1], ys[0, f, i, 0:1, :], by[1], has_yl)
        put(Y_UP + i, 1, value[ny - 1:ny], ys[1, f, i, 7:8, :], by[2], has_yh)
        if i in (0, nx - 1):
            side = 0 if i == 0 else 1
            sx = -1 if i == 0 else 1
            there = has_xl if i == 0 else has_xh
            put(X_UP if sx > 0 else X_DOWN, 16, value, xs[side, f], by[0], there)
            put(corner_row(sx, -1), 1, value[0:1], cs[side, f, 0:1, :], by[1], there & has_yl)
            put(corner_row(sx, 1), 1, value[ny - 1:ny], cs[side, f, ny - 1:ny, :], by[2], there & has_yh)

    lane_p = lax.broadcasted_iota(jnp.int32, (POINTS, nz), 1) % 8
    row_p = lax.broadcasted_iota(jnp.int32, (POINTS, nz), 0)

    def fold_points(value, dst):
        up = pltpu.roll(value, nz - 1, 1)
        down = pltpu.roll(value, 1, 1)
        value = value + jnp.where(lane_p == 7, up, 0.0) + jnp.where(lane_p == 0, down, 0.0)
        up = pltpu.roll(value, POINTS - 1, 0)
        down = pltpu.roll(value, 1, 0)
        on_face = row_p < CORNERS
        dst[...] = (
            value
            + jnp.where(on_face & (row_p % 16 == 7), up, 0.0)
            + jnp.where(on_face & (row_p % 16 == 8), down, 0.0)
        )

    def gather(src, dst):
        dst[X_UP:X_UP + 16, :] = src[nx - 1]
        dst[X_DOWN:X_DOWN + 16, :] = src[0]
        for i in range(nx):
            dst[Y_UP + i:Y_UP + i + 1, :] = src[i, ny - 1:ny, :]
            dst[Y_DOWN + i:Y_DOWN + i + 1, :] = src[i, 0:1, :]
        for sx in (1, -1):
            for sy in (1, -1):
                at, y = corner_row(sx, sy), (ny - 1 if sy > 0 else 0)
                dst[at:at + 1, :] = src[nx - 1 if sx > 0 else 0, y:y + 1, :]

    def point_copies(pair, e):
        made = []
        for n, (ds, dv) in enumerate(SIDES):
            if dv == 0:
                a, b, size = (X_UP, X_DOWN, 16) if ds > 0 else (X_DOWN, X_UP, 16)
            elif ds == 0:
                a, b, size = (Y_UP, Y_DOWN, 16) if dv > 0 else (Y_DOWN, Y_UP, 16)
            else:
                a, b, size = corner_row(ds, dv), corner_row(-ds, -dv), 1
            made.append([
                pltpu.make_async_remote_copy(
                    src_ref=outbox.at[pair, pl.ds(a, size), :], dst_ref=inbox.at[pair, pl.ds(b, size), :],
                    send_sem=send_sem.at[e, n], recv_sem=recv_sem.at[e, n],
                    device_id=near(ds, dv), device_id_type=MESH,
                )
            ])
        return launch(made)

    def operate(value, parts):
        return wts[...].reshape(rows, nz) * (
            left(bxy, parts) + right(parts, bz) + flat(reac) * value
        )

    def slopes(parts, k):
        both = left(kxy, parts)
        raw[k, 0] = both[:rows].reshape(nx, ny, nz)
        raw[k, 1] = both[rows:].reshape(nx, ny, nz)
        third = right(parts, kz)
        for i in range(nx):
            v = third[i * ny:(i + 1) * ny]
            other = jnp.where(lane == 7, pltpu.roll(v, nz - 1, 1), pltpu.roll(v, 1, 1))
            asm[k, 2, i] = jnp.where((lane == 7) | (lane == 0), 0.5 * (v + other), v)

    def slope_copies(e, first, count):
        xs, ys = halo[3 * e:3 * e + 2]
        made = []
        for n, (ds, dv) in enumerate(SIDES):
            group = []
            if ds * dv == 0:
                some = pl.ds(first, count)
                if dv == 0:
                    a = raw.at[some, 0, nx - 1 if ds > 0 else 0]
                    b = xs.at[0 if ds > 0 else 1]
                else:
                    a = raw.at[some, 1, :, pl.ds(ny - 1 if dv > 0 else 0, 1), :]
                    b = ys.at[0 if dv > 0 else 1].at[:, :, pl.ds(0 if dv > 0 else 7, 1), :]
                group.append(
                    pltpu.make_async_remote_copy(
                        src_ref=a, dst_ref=b,
                        send_sem=send_sem.at[e, n], recv_sem=recv_sem.at[e, n],
                        device_id=near(ds, dv), device_id_type=MESH,
                    )
                )
            made.append(group)
        return launch(made)

    def average(e, f, k):
        xs, ys = halo[3 * e:3 * e + 2]
        middle = 0.5 * (raw[k, 0, 7] + raw[k, 0, 8])
        for i in range(nx):
            v = raw[k, 0, i]
            if i in (7, 8):
                v = middle
            elif i == 0:
                v = jnp.where(has_xl, 0.5 * (v + xs[0, f]), v)
            elif i == nx - 1:
                v = jnp.where(has_xh, 0.5 * (v + xs[1, f]), v)
            asm[k, 0, i] = v
            v = raw[k, 1, i]
            other = jnp.concatenate([ys[0, f, i], ys[1, f, i]], axis=0)
            other = jnp.where(row == 7, pltpu.roll(v, ny - 1, 0), other)
            other = jnp.where(row == 8, pltpu.roll(v, 1, 0), other)
            shared = (row == 7) | (row == 8) | ((row == 0) & has_yl) | ((row == ny - 1) & has_yh)
            asm[k, 1, i] = jnp.where(shared, 0.5 * (v + other), v)

    def to_row(value, slot):
        s = value.reshape(rows // 8, 8, nz).sum(axis=0)
        s = s[:, :128] + s[:, 128:]
        tiles[slot:slot + 1, :] = jnp.sum(s, axis=0, keepdims=True)

    table, quad = gll_tables()
    turned = table.T * quad[None, :] / quad[:, None]
    stiff = turned @ table
    loads[0].wait()
    column = lax.broadcasted_iota(jnp.int32, (ny, nz), 1)

    def put_block(dst, at, mask, tile):
        high = tile.astype(BF16).astype(F32)
        dst[0, at:at + ny, :] = jnp.where(mask, high, 0.0).astype(BF16)
        dst[1, at:at + ny, :] = jnp.where(mask, tile - high, 0.0).astype(BF16)

    tile_z = jnp.concatenate([tab[0:8], tab[0:8]], axis=0)
    tile_y = jnp.concatenate([tab[8:16], tab[8:16]], axis=0)
    tile_w = jnp.concatenate([tab[32:40], tab[32:40]], axis=0)
    tile_m = jnp.concatenate([tab[40:48], tab[40:48]], axis=0)
    edge = ((row == 0) & (me_v == 0)) | ((row == ny - 1) & (me_v == n_vert - 1))
    tile_m = tile_m * jnp.where(edge, 2.0, 1.0)
    for i in range(nx):
        here = column // 8 == 2 * i + row // 8
        put_block(kz, i * ny, here, tile_z)
        put_block(kxy, rows + i * ny, here, tile_y)
        put_block(kxy, i * ny, column % ny == row, jnp.broadcast_to(tab[16 + i:17 + i], (ny, nz)))
        wts[i] = tile_w * float(quad[i % 8])
        value = tile_m
        if i in (0, nx - 1):
            value = value * jnp.where((me_s == 0) if i == 0 else (me_s == n_stream - 1), 1.0, 0.5)
        elif i % 8 in (0, 7):
            value = value * 0.5
        imult[i] = value
        imass[i] = time_step * value / wts[i]

    loads[1].wait()
    gather(adj.at[2], mine.at[1])
    gather(imass, mine.at[2])
    for c in range(3):
        parts = split(flat(adj.at[c]))
        both = left(kxy, parts)
        third = right(parts, kz)
        if c == 0:
            loads[2].wait()
            for load in loads[3:]:
                load.start()
        conv[c] = (
            flat(base.at[0]) * both[:rows] + flat(base.at[1]) * both[rows:] + flat(base.at[2]) * third
        ).reshape(nx, ny, nz)
    for j in range(3):
        parts = split(flat(base.at[j]))
        a = flat(adj.at[j])
        both = left(kxy, parts)
        conv[0] -= (a * both[:rows]).reshape(nx, ny, nz)
        conv[1] -= (a * both[rows:]).reshape(nx, ny, nz)
        conv[2] -= (a * right(parts, kz)).reshape(nx, ny, nz)
    for c in range(3):
        fold_store(flat(conv.at[c]) * flat(wts), part3.at[c])
    pl.semaphore_wait(barrier, len(partners))
    sends = [copies(0, part3)]

    def right_side(fields):
        pair = jnp.concatenate([fields[0], fields[1]], axis=0)
        return flat(wts) * (left(cxy, split(pair)) + right(split(fields[2]), cz))

    for load in loads[3:6]:
        load.wait()
    gather(part3.at[2], mine.at[0])
    pair = jnp.concatenate([flat(adj.at[c]) + flat(imass) * flat(part3.at[c]) for c in (0, 1)], axis=0)
    third = mine[1] + mine[2] * mine[0]
    fold_points(gw[...] * (left(cf, split(pair)) + right(split(third), cz)), outbox.at[0])
    ahead = point_copies(0, 1)
    sends += [strip_copies(0, part3.at[0], part3.at[1], True, turned, 0), ahead]
    for load in loads[6:]:
        load.wait()
    sends.append(reaction_copies())
    gather(reac, mine_reac)

    arrive(sends[0])
    for c in range(3):
        for i in range(nx):
            value = with_halo(0, c, part3, i)
            moved[c, i] = adj[c, i] + value * imass[i]
            ghost_points(0, c, value, i, c, imass[i])
    fold_store(right_side([flat(moved.at[c]) for c in range(3)]), own.at[0])
    arrive(sends[1])
    ghosts = jnp.concatenate([strips[0], strips[1]], axis=0)
    fold_points(gw[...] * (left(gc, split(ghosts)) + right(split(strips[2, 0:POINTS, :]), cz)), extra)
    arrive(sends[2])
    extra[...] = extra[...] + inbox[0]
    for i in range(nx):
        vec[0, i] = with_halo(1, 0, own, i, True)

    v = flat(vec.at[0])
    parts = split(v)
    image = operate(v, parts)
    fold_store(image, loc.at[1].at[0])
    sends.append(copies(2, loc.at[1]))
    first = flat(loc.at[1].at[0])
    gather(loc.at[1].at[0], mine.at[0])
    points = mine[0]
    fold_points(
        gw[...] * (left(bf, split(first)) + right(split(points), bz) + mine_reac[...] * points), outbox.at[1]
    )
    ahead = point_copies(1, 3)
    sends += [strip_copies(1, loc.at[1].at[0], loc.at[1].at[0], False, stiff, 3), ahead]
    to_row(v * v * flat(imult), 0)
    to_row(v * image, 1)
    slopes(parts, 0)
    sends.append(slope_copies(5, 0, 1))
    arrive(sends[3])
    arrive(sends[4])
    for i in range(nx):
        value = with_halo(2, 0, loc.at[1], i)
        vec[1, i] = value
        ghost_points(2, 0, value, i, 3)

    v = flat(vec.at[1])
    parts = split(v)
    image = operate(v, parts)
    fold_store(image, own.at[0])
    arrive(sends[5])
    points = strips[3, 0:POINTS, :]
    fold_points(
        gw[...] * (left(gb, split(strips[3])) + right(split(points), bz) + ghost_reac[...] * points), extra
    )
    to_row(v * v * flat(imult), 2)
    to_row(v * image, 3)
    arrive(sends[6])
    extra[...] = extra[...] + inbox[1]
    for i in range(nx):
        vec[2, i] = with_halo(3, 0, own, i, True)

    v = flat(vec.at[2])
    parts = split(v)
    image = operate(v, parts)
    to_row(v * v * flat(imult), 4)
    to_row(v * image, 5)

    tiles[6:8, :] = jnp.zeros((2, 128), F32)
    group = lax.broadcasted_iota(jnp.int32, (8, 128), 1) // 16
    packed = tiles[...]
    for shift in (64, 32, 16):
        packed = packed + pltpu.roll(packed, shift, 1)
    packed = jnp.where(group == lax.broadcasted_iota(jnp.int32, (8, 128), 0), packed, 0.0)
    red_a[n_vert - 1:n_vert, :] = jnp.sum(packed, axis=0, keepdims=True)

    def spread(slots, n, which):
        for k in range(1, n):
            pltpu.make_async_remote_copy(
                src_ref=slots.at[pl.ds(n - 1, 1)], dst_ref=slots.at[pl.ds(k - 1, 1)],
                send_sem=red_send.at[which], recv_sem=red_recv.at[which],
                device_id=near(0, k) if which == 0 else near(k, 0), device_id_type=MESH,
            ).start()

    def whole(slots, n, which):
        return pltpu.make_async_remote_copy(
            src_ref=slots.at[pl.ds(0, n - 1)], dst_ref=slots.at[pl.ds(0, n - 1)],
            send_sem=red_send.at[which], recv_sem=red_recv.at[which],
            device_id=near(0, 1), device_id_type=MESH,
        )

    spread(red_a, n_vert, 0)
    slopes(split(flat(vec.at[1])), 1)
    slopes(parts, 2)
    sends.append(slope_copies(4, 1, 2))
    whole(red_a, n_vert, 0).wait_recv()
    red_b[n_stream - 1:n_stream, :] = jnp.sum(red_a[...], axis=0, keepdims=True)
    spread(red_b, n_stream, 1)

    arrive(sends[7])
    average(5, 0, 0)
    arrive(sends[8])
    average(4, 0, 1)
    average(4, 1, 2)

    for made in sends:
        leave(made)
    whole(red_a, n_vert, 0).wait_send()
    whole(red_b, n_stream, 1).wait_recv()
    total = jnp.sum(red_b[...], axis=0, keepdims=True)
    m = [jnp.sum(jnp.where(group[0:1] == k, total, 0.0), axis=1, keepdims=True) for k in range(6)]
    a0 = m[0] / m[1]
    r1 = a0 * a0 * m[2] - m[0]
    k1 = 1.0 + r1 / m[0]
    p1 = k1 * k1 * m[1] - 2.0 * k1 * a0 * m[2] + a0 * a0 * m[3]
    a1 = r1 / p1
    e1 = -(a0 + a1 * k1)
    e2 = a1 * a0
    r2 = m[0] + 2.0 * e1 * m[1] + (e1 * e1 + 2.0 * e2) * m[2] + 2.0 * e1 * e2 * m[3] + e2 * e2 * m[4]
    b2 = r2 / r1
    f0 = 1.0 + b2 * k1
    f1 = e1 - b2 * a0
    f2 = e2
    p2 = (
        f0 * f0 * m[1] + 2.0 * f0 * f1 * m[2] + (f1 * f1 + 2.0 * f0 * f2) * m[3]
        + 2.0 * f1 * f2 * m[4] + f2 * f2 * m[5]
    )
    a2 = r2 / p2
    c0 = a0 + a1 * k1 + a2 * f0
    c1 = a2 * f1 - a1 * a0
    c2 = a2 * f2
    for k, c in enumerate((c0, c1, c2)):
        coef[k:k + 1, :] = jnp.broadcast_to(c, (1, nz))
    whole(red_b, n_stream, 1).wait_send()


def combine(moved, asm, vec, coef, out_h, pres_h, out, pres, sems):
    copies = []
    for i in range(pres.shape[0]):
        pres[i] = coef[0:1] * vec[0, i] + coef[1:2] * vec[1, i] + coef[2:3] * vec[2, i]
    copies.append(pltpu.make_async_copy(pres, pres_h, sems.at[3]))
    copies[-1].start()
    for d in range(3):
        for i in range(pres.shape[0]):
            out[d, i] = moved[d, i] - (
                coef[0:1] * asm[0, d, i] + coef[1:2] * asm[1, d, i] + coef[2:3] * asm[2, d, i]
            )
        copies.append(pltpu.make_async_copy(out.at[d], out_h.at[d], sems.at[d]))
        copies[-1].start()
    for copy in copies:
        copy.wait()


def on_device(n_stream, n_vert, base_flow, adjoint_velocity, reaction):
    nx, ny, nz = reaction.shape
    consts = constants(nx, ny, nz)
    field = (nx, ny, nz)
    operands = [base_flow, adjoint_velocity, reaction, *[jnp.asarray(c) for c in consts]]
    scratch = [
        pltpu.VMEM(base_flow.shape, F32),
        pltpu.VMEM(base_flow.shape, F32),
        pltpu.VMEM(field, F32),
        *[pltpu.VMEM(c.shape, c.dtype) for c in consts],
        pltpu.VMEM((2, 2 * nx * ny, nx * ny), BF16),
        pltpu.VMEM((2, nz, nz), BF16),
        pltpu.VMEM(field, F32),
        pltpu.VMEM(field, F32),
        pltpu.VMEM(field, F32),
        pltpu.VMEM((3, *field), F32),
        pltpu.VMEM((3, 1, *field), F32),
        pltpu.VMEM((3, 2, *field), F32),
        pltpu.VMEM((3, *field), F32),
        pltpu.VMEM((1, *field), F32),
        pltpu.VMEM((4, STRIPS, nz), F32),
        pltpu.VMEM((POINTS, nz), F32),
        pltpu.VMEM((POINTS, nz), F32),
        pltpu.VMEM((3, POINTS, nz), F32),
        pltpu.VMEM((POINTS, nz), F32),
        pltpu.VMEM((2, POINTS, nz), F32),
        pltpu.VMEM((2, POINTS, nz), F32),
        pltpu.VMEM((2, 16, nz), F32),
        pltpu.VMEM((8, 128), F32),
        pltpu.VMEM((n_vert, 128), F32),
        pltpu.VMEM((n_stream, 128), F32),
        pltpu.SemaphoreType.DMA((3 + len(consts),)),
        pltpu.SemaphoreType.DMA((7, 8)),
        pltpu.SemaphoreType.DMA((7, 8)),
        pltpu.SemaphoreType.DMA((2, 8)),
        pltpu.SemaphoreType.DMA((2, 8)),
        pltpu.SemaphoreType.DMA((2,)),
        pltpu.SemaphoreType.DMA((2,)),
    ]
    for count in FIELDS:
        scratch += [
            pltpu.VMEM((2, count, ny, nz), F32),
            pltpu.VMEM((2, count, nx, 8, nz), F32),
            pltpu.VMEM((2, count, ny, nz), F32),
        ]
    pieces = pl.pallas_call(
        functools.partial(kernel, n_stream, n_vert),
        out_shape=(
            pltpu.VMEM((3, *field), F32),
            pltpu.VMEM((3, 3, *field), F32),
            pltpu.VMEM((3, *field), F32),
            pltpu.VMEM((8, nz), F32),
        ),
        in_specs=[pl.BlockSpec(memory_space=pl.ANY)] * len(operands),
        out_specs=tuple([pl.BlockSpec(memory_space=pltpu.VMEM)] * 4),
        scratch_shapes=scratch,
        compiler_params=pltpu.CompilerParams(
            collective_id=0, has_side_effects=True, vmem_limit_bytes=48 * 1024 * 1024
        ),
    )(*[pltpu.with_memory_space_constraint(a, pltpu.HBM) for a in operands])
    return pl.pallas_call(
        combine,
        out_shape=(
            pltpu.HBM(base_flow.shape, F32),
            pltpu.HBM(field, F32),
        ),
        in_specs=[pl.BlockSpec(memory_space=pltpu.VMEM)] * 4,
        out_specs=tuple([pl.BlockSpec(memory_space=pl.ANY)] * 2),
        scratch_shapes=[
            pltpu.VMEM(base_flow.shape, F32),
            pltpu.VMEM(field, F32),
            pltpu.SemaphoreType.DMA((4,)),
        ],
        compiler_params=pltpu.CompilerParams(vmem_limit_bytes=16 * 1024 * 1024),
    )(*[pltpu.with_memory_space_constraint(a, pltpu.VMEM) for a in pieces])


def solution(mesh):
    placed = (
        P(None, "stream", "vert", None),
        P(None, "stream", "vert", None),
        P("stream", "vert", None),
    )
    return jax.shard_map(
        functools.partial(on_device, mesh.shape["stream"], mesh.shape["vert"]),
        mesh=mesh,
        in_specs=placed,
        out_specs=(P(None, "stream", "vert", None), P("stream", "vert", None)),
        check_vma=False,
    )
```
